32 devices in a mesh: dp: 4 (over z), row: 4 (over y, x), col: 2 (over core).
Axes of the slice: x: 2, y: 2, z: 4, core: 2. Of those that a mesh axis runs over, the one named last changes fastest.
Arguments:
- tokens_in: bfloat16 [2048, 4, 384], P('dp', 'row'), may hold values from -6 to 6
- lengths: int32 [16], P(('dp', 'row')), may hold values from 32 to 256, as said below
- joint_weight: float32 [768, 12, 192], P('row', 'col', 'dp'), may hold values from -0.21875 to 0.21875
- joint_first: float32 [768, 12, 192], P('row', 'col', 'dp'), may hold values from -14.08 to 14.08
- joint_second: float32 [768, 12, 192], P('row', 'col', 'dp'), may hold values from 1.024 to 4.096
- output_weight: float32 [768, 4, 192], P('col', 'row', 'dp'), may hold values from -1.75 to 1.75
- output_first: float32 [768, 4, 192], P('col', 'row', 'dp'), may hold values from -2.816 to 2.816
- output_second: float32 [768, 4, 192], P('col', 'row', 'dp'), may hold values from 0.04096 to 0.16384
- up_weight: float32 [768, 2, 1536], P('row', 'col', 'dp'), may hold values from -0.21875 to 0.21875
- up_first: float32 [768, 2, 1536], P('row', 'col', 'dp'), may hold values from -8.448 to 8.448
- up_second: float32 [768, 2, 1536], P('row', 'col', 'dp'), may hold values from 0.36864 to 1.47456
- down_weight: float32 [3072, 4, 192], P('col', 'row', 'dp'), may hold values from -0.109375 to 0.109375
- down_first: float32 [3072, 4, 192], P('col', 'row', 'dp'), may hold values from -14.08 to 14.08
- down_second: float32 [3072, 4, 192], P('col', 'row', 'dp'), may hold values from 1.024 to 4.096
- vectors: float32 [9216], replicated, may hold values from -2.5 to 2.5, as said below
- vector_first: float32 [9216], replicated, may hold values from -19.712 to 19.712
- vector_second: float32 [9216], replicated, may hold values from 2.00704 to 8.02816
- out_grad: bfloat16 [2048, 4, 384], P('dp', 'row'), may hold values from -6 to 6
Outputs:
- layer_out: float32 [2048, 4, 384], P('dp', 'row')
- tokens_grad: float32 [2048, 4, 384], P('dp', 'row')
- joint_first_new: float32 [768, 12, 192], P('row', 'col', 'dp')
- joint_second_new: float32 [768, 12, 192], P('row', 'col', 'dp')
- joint_weight_new: float32 [768, 12, 192], P('row', 'col', 'dp')
- output_first_new: float32 [768, 4, 192], P('col', 'row', 'dp')
- output_second_new: float32 [768, 4, 192], P('col', 'row', 'dp')
- output_weight_new: float32 [768, 4, 192], P('col', 'row', 'dp')
- up_first_new: float32 [768, 2, 1536], P('row', 'col', 'dp')
- up_second_new: float32 [768, 2, 1536], P('row', 'col', 'dp')
- up_weight_new: float32 [768, 2, 1536], P('row', 'col', 'dp')
- down_first_new: float32 [3072, 4, 192], P('col', 'row', 'dp')
- down_second_new: float32 [3072, 4, 192], P('col', 'row', 'dp')
- down_weight_new: float32 [3072, 4, 192], P('col', 'row', 'dp')
- vector_first_new: float32 [9216], replicated
- vector_second_new: float32 [9216], replicated
- vectors_new: float32 [9216], replicated
The draws below stay inside these ranges and needn't reach their ends.
Inputs may be any that keep to these rules, and one draw needn't show every extreme that they name: `lengths`: at least one sequence has 256 real tokens. `vectors`: the gains g1 and g2 lie in 0.5 to 1.5.
All inputs are finite; a program needn't handle non-finite values.
Results may differ from the reference program's by a relative error of at most 0.01.
Values may be sent and summed in bfloat16 or wider, within the bound.
No kernel may reach another device: no remote copies, remote signals or barrier semaphores. Data moves between devices by JAX's collectives and lax.ppermute only.
A program may use at most 128 MiB of HBM per device.

```python
import math
import jax
import jax.numpy as jnp
from jax import lax

D = 768
H = 12
HD = 64
FF = 3072
LEN = 256
STEP = 10
SEQS = 16
TOKENS = 4096
N_ROW = 4
N_COL = 2


def first_moment(key, shape, scale):
    return 0.11 * scale * jnp.clip(jax.random.normal(key, shape, jnp.float32), -4.0, 4.0)


def second_moment(key, shape, scale):
    spread = jax.random.uniform(key, shape, jnp.float32, 0.0, 2.0)
    return 0.001 * scale * scale * jnp.exp2(spread)


def draw_lengths(key, part):
    key = jax.random.fold_in(key, 1)
    first, second = jax.random.split(key)
    drawn = jax.random.randint(first, (SEQS,), LEN // 8, LEN + 1)
    place = jax.random.randint(second, (), 0, SEQS)
    return jnp.where(jnp.arange(SEQS) == place, LEN, drawn).astype(jnp.int32)


def draw_joint_first(key, part):
    key = jax.random.fold_in(key, 2)
    return first_moment(key, (D, H, 3 * HD), 0.5 * TOKENS ** 0.5)


def draw_joint_second(key, part):
    key = jax.random.fold_in(key, 3)
    return second_moment(key, (D, H, 3 * HD), 0.5 * TOKENS ** 0.5)


def draw_output_first(key, part):
    key = jax.random.fold_in(key, 4)
    return first_moment(key, (D, N_ROW, D // N_ROW), 0.1 * TOKENS ** 0.5)


def draw_output_second(key, part):
    key = jax.random.fold_in(key, 5)
    return second_moment(key, (D, N_ROW, D // N_ROW), 0.1 * TOKENS ** 0.5)


def draw_up_first(key, part):
    key = jax.random.fold_in(key, 6)
    return first_moment(key, (D, N_COL, FF // N_COL), 0.3 * TOKENS ** 0.5)


def draw_up_second(key, part):
    key = jax.random.fold_in(key, 7)
    return second_moment(key, (D, N_COL, FF // N_COL), 0.3 * TOKENS ** 0.5)


def draw_down_first(key, part):
    key = jax.random.fold_in(key, 8)
    return first_moment(key, (FF, N_ROW, D // N_ROW), 0.5 * TOKENS ** 0.5)


def draw_down_second(key, part):
    key = jax.random.fold_in(key, 9)
    return second_moment(key, (FF, N_ROW, D // N_ROW), 0.5 * TOKENS ** 0.5)


def draw_vectors(key, part):
    key = jax.random.fold_in(key, 10)
    first, second = jax.random.split(key)
    width = 8 * D + FF
    biases = 0.5 * jnp.clip(jax.random.normal(first, (width,), jnp.float32), -5.0, 5.0)
    gains = 1.0 + 0.1 * jnp.clip(jax.random.normal(second, (width,), jnp.float32), -5.0, 5.0)
    index = jnp.arange(width)
    is_gain = (index >= 3 * D) & (index < 4 * D) | (index >= 6 * D) & (index < 7 * D)
    return jnp.where(is_gain, gains, biases)


def draw_vector_first(key, part):
    key = jax.random.fold_in(key, 11)
    return first_moment(key, (8 * D + FF,), 0.7 * TOKENS ** 0.5)


def draw_vector_second(key, part):
    key = jax.random.fold_in(key, 12)
    return second_moment(key, (8 * D + FF,), 0.7 * TOKENS ** 0.5)


def level_of(key, dims, cuts, smallest, high):
    level = 1.0
    for axis_at, blocks in cuts:
        heights = jax.random.uniform(jax.random.fold_in(jax.random.fold_in(key, 6), axis_at), (blocks,), jnp.float32, smallest / len(cuts), high / len(cuts))
        level = level * jnp.repeat(jnp.exp(heights), dims[axis_at] // blocks).reshape((-1,) + (1,) * (len(dims) - 1 - axis_at))
    return level


def scatter_about(stream_key, shape, scale, limit, cuts=(), kind=jnp.bfloat16):
    entries = jax.random.normal(stream_key, shape, jnp.float32) * scale
    if len(cuts) > 0:
        entries = level_of(stream_key, shape, cuts, -0.22, 0.18) * entries
    return jnp.clip(entries, min=-limit, max=limit).astype(kind)


def setup_inputs(seed: int = 0) -> dict:
    key_list = jax.random.split(jax.random.key(seed), 19)
    return {
        "tokens_in": scatter_about(key_list[0], (TOKENS // 2, N_ROW, 2 * D // N_ROW), 1.0, 6.0, ((0, 4), (1, 4))),
        "lengths": draw_lengths(jax.random.fold_in(key_list[18], 71), 0),
        "joint_weight": scatter_about(key_list[2], (D, H, 3 * HD), D ** -0.5, 0.21875, ((0, 4), (1, 2), (2, 4)), jnp.float32),
        "joint_first": draw_joint_first(jax.random.fold_in(key_list[18], 71), 0),
        "joint_second": draw_joint_second(jax.random.fold_in(key_list[18], 71), 0),
        "output_weight": scatter_about(key_list[5], (D, N_ROW, D // N_ROW), (4 * D // LEN) ** -0.5, 1.75, ((0, 2), (1, 4), (2, 4)), jnp.float32),
        "output_first": draw_output_first(jax.random.fold_in(key_list[18], 71), 0),
        "output_second": draw_output_second(jax.random.fold_in(key_list[18], 71), 0),
        "up_weight": scatter_about(key_list[8], (D, N_COL, FF // N_COL), D ** -0.5, 0.21875, ((0, 4), (1, 2), (2, 4)), jnp.float32),
        "up_first": draw_up_first(jax.random.fold_in(key_list[18], 71), 0),
        "up_second": draw_up_second(jax.random.fold_in(key_list[18], 71), 0),
        "down_weight": scatter_about(key_list[11], (FF, N_ROW, D // N_ROW), FF ** -0.5, 0.109375, ((0, 2), (1, 4), (2, 4)), jnp.float32),
        "down_first": draw_down_first(jax.random.fold_in(key_list[18], 71), 0),
        "down_second": draw_down_second(jax.random.fold_in(key_list[18], 71), 0),
        "vectors": draw_vectors(jax.random.fold_in(key_list[18], 71), 0),
        "vector_first": draw_vector_first(jax.random.fold_in(key_list[18], 71), 0),
        "vector_second": draw_vector_second(jax.random.fold_in(key_list[18], 71), 0),
        "out_grad": scatter_about(key_list[17], (TOKENS // 2, N_ROW, 2 * D // N_ROW), 1.0, 6.0, ((0, 4), (1, 4))),
    }


@jax.custom_vjp
def low(v):
    return lax.optimization_barrier(v.astype(jnp.bfloat16)).astype(jnp.float32)

@jax.custom_vjp
def low_back(v):
    return v

def low_keep(v):
    return (low(v), None)

def low_pass(kept, grad):
    return (grad,)

def back_keep(v):
    return (v, None)

def back_low(kept, grad):
    return (low(grad),)
low.defvjp(low_keep, low_pass)
low_back.defvjp(back_keep, back_low)
NORM_EPS = 1e-12
BETA_ONE = 0.9
BETA_TWO = 0.999
ADAM_EPS = 1e-08
DECAY = 0.01
VECTOR_RATE = 0.2
HIGHEST_PRECISION = lax.Precision.HIGHEST

def to_matrix(packed):
    return packed.reshape(TOKENS // 2, N_ROW, 2, D // N_ROW).transpose(0, 2, 1, 3).reshape(TOKENS, D)

def to_packed(matrix):
    return matrix.reshape(TOKENS // 2, 2, N_ROW, D // N_ROW).transpose(0, 2, 1, 3).reshape(TOKENS // 2, N_ROW, 2 * D // N_ROW)

def layer_norm(resid, gain, shift):
    mean = lax.optimization_barrier(jnp.mean(resid, axis=-1, keepdims=True))
    var = lax.optimization_barrier(jnp.mean(resid * resid, axis=-1, keepdims=True)) - mean * mean
    return (resid - mean) * lax.rsqrt(var + NORM_EPS) * gain + shift

def attend(block):
    query, keyed, valued, valid = block
    scores = jnp.einsum('gqhe,gkhe->ghqk', query, keyed, precision=HIGHEST_PRECISION) * 0.125
    scores = low_back(scores)
    scores = jnp.where(valid[:, None, None, :], scores, -1e+30)
    top = lax.optimization_barrier(jnp.max(scores, axis=-1, keepdims=True))
    expo = jnp.exp(scores - top)
    probs = expo / lax.optimization_barrier(jnp.sum(expo, axis=-1, keepdims=True))
    return jnp.einsum('ghqk,gkhe->gqhe', low(probs), valued, precision=HIGHEST_PRECISION)

def matmul(left, right):
    return jnp.dot(left, right, preferred_element_type=jnp.float32, precision=HIGHEST_PRECISION)

def forward(tokens, joint, output, upward, downward, vectors, valid):
    bias_query = vectors[0:D].reshape(H, HD)
    bias_value = vectors[D:2 * D].reshape(H, HD)
    bias_out = vectors[2 * D:3 * D]
    gain_one = vectors[3 * D:4 * D]
    shift_one = vectors[4 * D:5 * D]
    bias_down = vectors[5 * D:6 * D]
    gain_two = vectors[6 * D:7 * D]
    shift_two = vectors[7 * D:8 * D]
    bias_up = vectors[8 * D:8 * D + FF]
    mixed = jnp.einsum('td,dhe->the', tokens, low(joint), precision=HIGHEST_PRECISION)
    query = low(low_back(mixed[:, :, 0:HD] + bias_query))
    keyed = low(low_back(mixed[:, :, HD:2 * HD]))
    valued = low(low_back(mixed[:, :, 2 * HD:3 * HD] + bias_value))
    group = math.gcd(SEQS, max(1, 4096 // LEN))
    shape = (SEQS // group, group, LEN, H, HD)
    attended = lax.map(jax.checkpoint(attend), (query.reshape(shape), keyed.reshape(shape), valued.reshape(shape), valid.reshape(SEQS // group, group, LEN)))
    attended = low(low_back(attended.reshape(TOKENS, D)))
    branch = low_back(matmul(attended, low(output).reshape(D, D)) + bias_out)
    hidden = layer_norm(tokens + branch, gain_one, shift_one)
    pre = low_back(matmul(low(hidden), low(upward).reshape(D, FF)) + bias_up)
    act = jax.nn.gelu(pre, approximate=False)
    down = low_back(matmul(low(act), low(downward).reshape(FF, D)) + bias_down)
    return layer_norm(hidden + down, gain_two, shift_two)

def adamw(weight, first, second, grad, rate, decay):
    first_new = BETA_ONE * first + (1.0 - BETA_ONE) * grad
    second_new = BETA_TWO * second + (1.0 - BETA_TWO) * grad * grad
    fix_one = 1.0 - BETA_ONE ** STEP
    fix_two = 1.0 - BETA_TWO ** STEP
    update = first_new / fix_one / (jnp.sqrt(second_new / fix_two) + ADAM_EPS) + decay * weight
    return (first_new, second_new, weight - rate * update)

def reference(tokens_in, lengths, joint_weight, joint_first, joint_second, output_weight, output_first, output_second, up_weight, up_first, up_second, down_weight, down_first, down_second, vectors, vector_first, vector_second, out_grad):
    valid = jnp.arange(LEN, dtype=jnp.int32)[None, :] < lengths[:, None]
    start = to_matrix(tokens_in.astype(jnp.float32))

    def run(tokens, joint, output, upward, downward, vecs):
        return forward(tokens, joint, output, upward, downward, vecs, valid)
    result, pull = jax.vjp(run, start, joint_weight, output_weight, up_weight, down_weight, vectors)
    grads = pull(to_matrix(out_grad.astype(jnp.float32)))
    joint_new = adamw(joint_weight, joint_first, joint_second, grads[1], D ** (-0.5), DECAY)
    output_new = adamw(output_weight, output_first, output_second, grads[2], (4 * D // LEN) ** (-0.5), DECAY)
    up_new = adamw(up_weight, up_first, up_second, grads[3], D ** (-0.5), DECAY)
    down_new = adamw(down_weight, down_first, down_second, grads[4], FF ** (-0.5), DECAY)
    vector_new = adamw(vectors, vector_first, vector_second, grads[5], VECTOR_RATE, 0.0)
    return (to_packed(result), to_packed(grads[0]), joint_new[0], joint_new[1], joint_new[2], output_new[0], output_new[1], output_new[2], up_new[0], up_new[1], up_new[2], down_new[0], down_new[1], down_new[2], vector_new[0], vector_new[1], vector_new[2])
```

```python
from functools import partial

import jax
import jax.numpy as jnp
from jax import lax
from jax.experimental import pallas as pl
from jax.experimental.pallas import tpu as pltpu
from jax.sharding import PartitionSpec as P

D = 768
H = 12
HD = 64
FF = 3072
LEN = 256
STEP = 10

NORM_EPS = 1e-12
BETA_ONE = 0.9
BETA_TWO = 0.999
ADAM_EPS = 1e-08
DECAY = 0.01
VECTOR_RATE = 0.2

F32 = jnp.float32
BF16 = jnp.bfloat16

ROWS = 4
QUADS = 4
W = D // ROWS
S = W // QUADS
COLS = D // 2
HEADS = COLS // HD
FFC = FF // 2
MIX = HEADS * 3 * HD
PAIRS = LEN // 2
CHUNK = (W, COLS)
MIB = 1024 * 1024


def swap(value, axis, mask):
    n = lax.axis_size(axis)
    return lax.ppermute(value, axis, [(i, i ^ mask) for i in range(n)])


def shape(*dims, dtype=BF16):
    return jax.ShapeDtypeStruct(dims, dtype)


def run(kernel, where, args, outs, scratch=(), limit=8, after=(), fetch=False):
    vmem = pl.BlockSpec(memory_space=pltpu.VMEM)
    first, late = 1 + len(args), len(after)

    def body(*refs):
        kernel(*refs[:first], *refs[first + late :])

    out = pl.pallas_call(
        body,
        out_shape=outs,
        in_specs=[pl.BlockSpec(memory_space=pltpu.SMEM)]
        + [pl.BlockSpec(memory_space=pl.ANY) if fetch else vmem] * len(args)
        + [pl.BlockSpec(memory_space=pl.ANY)] * late,
        out_specs=[vmem] * len(outs),
        scratch_shapes=list(scratch),
        compiler_params=pltpu.CompilerParams(vmem_limit_bytes=limit * MIB),
    )(where, *args, *after)
    return list(out)


def dot(left, right, dims):
    return lax.dot_general(left, right, (dims, ((), ())), preferred_element_type=F32)


NN = ((1,), (0,))
NT = ((1,), (1,))
TN = ((0,), (0,))


def each(count, body):
    def step(i, carry):
        body(i)
        return carry

    lax.fori_loop(0, count, step, 0)


def row_of(vecs, start, count):
    return jnp.concatenate([vecs[start + i : start + i + 1, :] for i in range(count)], axis=1)


def vector_row(vecs, k):
    return row_of(vecs, 6 * k, 6)


def pick_col(where, left, right):
    return jnp.where(where[2] == 0, left, right)


def split_parts(value):
    high = value.astype(BF16)
    return high, (value - high.astype(F32)).astype(BF16)


def opening_kernel(where, tokens, grads, joint, output, *refs):
    outs, first = refs[:ROWS], refs[ROWS]
    tokens_in, grads_in, joint_in, output_in, done = refs[ROWS + 1 :]
    copies = [
        pltpu.make_async_copy(source, target, done.at[i])
        for i, (source, target) in enumerate(
            [(joint, joint_in), (output, output_in), (tokens, tokens_in), (grads, grads_in)]
        )
    ]
    for copy in copies:
        copy.start()
    copies[0].wait()
    copies[1].wait()
    for h in range(HEADS // 2):
        pair = [joint_in[h].astype(BF16), joint_in[h + HEADS // 2].astype(BF16)]
        first[h * S : (h + 1) * S, :] = jnp.concatenate(pair, axis=1)
    first[HEADS // 2 * S :, :] = output_in[...].astype(BF16)
    copies[2].wait()
    copies[3].wait()
    for m, out in enumerate(outs):
        out[0] = tokens_in[where[0] ^ m]
        out[1] = grads_in[where[0] ^ m]


def second_shard_kernel(where, up, second):
    for q in range(3):
        second[:, q * 128 : (q + 1) * 128] = up[pl.ds(q, W, stride=3), :].astype(BF16)


def third_shard_kernel(where, down, third):
    for q in range(4):
        third[q * S : (q + 1) * S, :] = down[:, q * COLS : (q + 1) * COLS].astype(BF16)


def pair_kernel(where, b0, b1, pair):
    pair[0] = b0[...]
    pair[1] = b1[...]


def whole_kernel(where, *refs):
    *pieces, line = refs
    for k in range(QUADS):
        line[k] = pieces[k][...] if len(pieces) == QUADS else pieces[k // 2][k % 2]


def halves_kernel(where, from_x, from_y, near_y, far_x):
    near_y[...] = from_y[0:2]
    far_x[...] = from_x[2:4]


def token_kernel(where, tokens, grads, *outs):
    for m, out in enumerate(outs):
        out[0] = tokens[where[0] ^ m]
        out[1] = grads[where[0] ^ m]


ORDER = (0, 2, 1, 3)


def blocks(where, pieces):
    found = [(piece, i) for piece in pieces for i in range(piece.shape[0])]
    for at, (piece, i) in enumerate(found):
        yield where[0] ^ (at // QUADS), where[1] ^ ORDER[at % QUADS], piece[i]


def unpack_tokens(x):
    parts = [jnp.concatenate([x[r][:, :W], x[r][:, W:]], axis=0) for r in range(ROWS)]
    return jnp.concatenate(parts, axis=1)


def pack_tokens(value, room, k):
    for r in range(ROWS):
        both = value[:, r * W : (r + 1) * W]
        room[r, k] = jnp.concatenate([both[:PAIRS], both[PAIRS:]], axis=1).astype(BF16)


def attend_kernel(where, t0, t1, t2, t3, vecs, *refs):
    pieces, refs = refs[:5], refs[5:]
    tokens, grads, wj, wo, mixed, probs, attended, part, room, mixing, scores, parts = refs
    for m, piece in enumerate([t0, t1, t2, t3]):
        room[where[0] ^ m] = piece[...]
    tokens[...] = unpack_tokens([room[r, 0] for r in range(ROWS)])
    grads[...] = unpack_tokens([room[r, 1] for r in range(ROWS)])
    half = HEADS // 2
    for row, quad, value in blocks(where, pieces):
        for h in range(half):
            rows = value[h * S : (h + 1) * S, :]
            for k, cut in enumerate([rows[:, :W], rows[:, W:]]):
                start = pl.multiple_of((h + k * half) * 3 * HD + quad * S, 16)
                wj[row, pl.ds(start, S), :] = cut
        start = pl.multiple_of(row * W + quad * S, 16)
        wo[pl.ds(start, S), :] = value[half * S :, :]
    total = dot(wj[0], tokens[:, :W], NT)
    for r in range(1, ROWS):
        total = total + dot(wj[r], tokens[:, r * W : (r + 1) * W], NT)
    mixing[...] = total
    query_bias, value_bias = [
        pick_col(where, row_of(vecs, start, 3), row_of(vecs, start + 3, 3)) for start in (0, 6)
    ]
    zero = jnp.zeros((1, HD), F32)
    row = []
    for h in range(HEADS):
        at = slice(h * HD, (h + 1) * HD)
        row += [query_bias[:, at], zero, value_bias[:, at]]
    row = jnp.concatenate(row, axis=1)
    high, low = split_parts(row)
    rest = (row - high.astype(F32) - low.astype(F32)).astype(BF16)
    parts[...] = jnp.zeros_like(parts)
    parts[0:1, :] = high.astype(F32)
    parts[1:2, :] = low.astype(F32)
    parts[2:3, :] = rest.astype(F32)
    bias = dot(parts[...].astype(BF16), jnp.ones((8, LEN), BF16), TN)
    mixed[...] = (mixing[...] + bias).astype(BF16)
    slot = lax.broadcasted_iota(jnp.int32, (LEN, 1), 0)
    slot = jnp.where(slot < PAIRS, 2 * slot, 2 * (slot - PAIRS) + 1)
    valid = slot < where[3]
    for h in range(HEADS):
        base = h * 3 * HD
        query, keyed, valued = [mixed[base + k * HD : base + (k + 1) * HD, :] for k in range(3)]
        scores[...] = dot(keyed, query, TN)
        for q in range(2):
            at = slice(q * 128, (q + 1) * 128)
            score = jnp.where(valid, scores[:, at] * 0.125, -1e30)
            expo = jnp.exp(score - jnp.max(score, axis=0, keepdims=True))
            prob = expo * (1.0 / jnp.sum(expo, axis=0, keepdims=True))
            probs[h, :, at] = prob.astype(BF16)
        attended[h * HD : (h + 1) * HD, :] = dot(valued, probs[h], NN).astype(BF16)
    part[...] = dot(attended[...], wo[...], ((0,), (1,))).astype(BF16)


def norm_rows(resid, gain, shift_by):
    mean = jnp.sum(resid, axis=1, keepdims=True) * (1.0 / D)
    var = jnp.sum(resid * resid, axis=1, keepdims=True) * (1.0 / D) - mean * mean
    inverse = lax.rsqrt(var + NORM_EPS)
    normed = (resid - mean) * inverse
    return normed * gain + shift_by, normed, inverse


def norm_back_rows(grad, normed, inverse, gain):
    scaled = grad * gain
    total = jnp.sum(scaled, axis=1, keepdims=True) * (1.0 / D)
    cross = jnp.sum(scaled * normed, axis=1, keepdims=True) * (1.0 / D)
    return (scaled - total - normed * cross) * inverse


STRIP = 32


def strip(i):
    return pl.ds(pl.multiple_of(i * STRIP, STRIP), STRIP)


def up_kernel(where, tokens, p0, p1, vecs, *refs):
    pieces, refs = refs[:5], refs[5:]
    hidden, low, normed, inverse, act, slope, wu, pre = refs
    for row, quad, value in blocks(where, pieces):
        rows = pl.ds(pl.multiple_of(row * W, W), W)
        wu[rows, pl.ds(pl.multiple_of(quad * COLS, COLS), COLS)] = value

    bias_out, gain, shift_by = [vector_row(vecs, k) for k in (2, 3, 4)]

    def first(i):
        at = strip(i)
        resid = tokens[at, :].astype(F32) + (p0[at, :].astype(F32) + p1[at, :].astype(F32))
        out, unit, scale = norm_rows(resid + bias_out, gain, shift_by)
        hidden[at, :] = out
        low[at, :] = out.astype(BF16)
        normed[at, :] = unit
        inverse[at, :] = scale

    each(LEN // STRIP, first)
    pre[...] = dot(low[...], wu[...], NN)
    bias = pick_col(where, row_of(vecs, 48, 12), row_of(vecs, 60, 12))
    for q in range(4):
        cols = slice(q * COLS, (q + 1) * COLS)
        shift_up = bias[:, cols]

        def second(i, cols=cols, shift_up=shift_up):
            at = (strip(i), cols)
            value = pre[at] + shift_up
            phi = 0.5 * (1.0 + lax.erf(value * (0.5**0.5)))
            density = jnp.exp(-0.5 * value * value) * 0.3989422804014327
            act[at] = (value * phi).astype(BF16)
            slope[at] = phi + value * density

        each(LEN // STRIP, second)


def down_kernel(where, act, *refs):
    pieces, wd, part = refs[:5], refs[5], refs[6]
    for row, quad, value in blocks(where, pieces):
        rows = pl.ds(pl.multiple_of(row * W + quad * S, 16), S)
        for q in range(4):
            wd[rows, q * COLS : (q + 1) * COLS] = value[q * S : (q + 1) * S, :]
    part[...] = dot(act[...], wd[...], NT).astype(BF16)


def hand_out(where, room, outs):
    r = where[0]
    last_x, last_y, own = outs[-3:]
    if len(outs) == 5:
        far_x, far_y = [out.at[0:2] for out in outs[:2]]
        near_x, near_y = [out.at[2:4] for out in outs[:2]]
    else:
        far_x, far_y, near_x, near_y = outs[:4]
    far_x[...] = room[r ^ 3, 0:2]
    far_y[...] = room[r ^ 3, 2:4]
    near_x[...] = room[r ^ 1, 0:2]
    near_y[...] = room[r ^ 2, 2:4]
    last_x[...] = room[r ^ 1, 2:4]
    last_y[...] = room[r ^ 2, 0:2]
    own[...] = room[r]


PAIR = shape(2, *CHUNK)
LINE = shape(4, *CHUNK)
HANDED = [LINE] * 2 + [PAIR] * 2 + [LINE]
SPLIT = [PAIR] * 6 + [LINE]

VROWS = 32
VECTOR = (VROWS, COLS)
CARRIED = (2 * W + 2 * VROWS, COLS)
FIRST = (4 * W + 2 * VROWS, COLS)


def put_vector(out, start, value):
    high, low = split_parts(value)
    out[start : start + VROWS, :] = high
    out[start + VROWS : start + 2 * VROWS, :] = low


def get_vector(value, start):
    high = value[start : start + VROWS, :].astype(F32)
    return high + value[start + VROWS : start + 2 * VROWS, :].astype(F32)


def second_norm_kernel(where, hidden, p0, p1, vecs, grads, act, *refs):
    (result, low, grad_two, sums), handed, room = refs[:4], refs[4:11], refs[11]
    sums[...] = jnp.zeros_like(sums)
    bias_down, gain, shift_by = [vector_row(vecs, k) for k in (5, 6, 7)]

    def body(i):
        at = strip(i)
        resid = hidden[at, :] + (p0[at, :].astype(F32) + p1[at, :].astype(F32)) + bias_down
        out, unit, scale = norm_rows(resid, gain, shift_by)
        result[at, :] = out
        grad = grads[at, :].astype(F32)
        back = norm_back_rows(grad, unit, scale, gain)
        grad_two[at, :] = back
        rounded = back.astype(BF16)
        low[at, :] = rounded
        sums[0:1, :] += jnp.sum(rounded.astype(F32), axis=0, keepdims=True)
        sums[1:2, :] += jnp.sum(grad * unit, axis=0, keepdims=True)
        sums[2:3, :] += jnp.sum(grad, axis=0, keepdims=True)

    each(LEN // STRIP, body)
    for q in range(4):
        cols = slice(q * COLS, (q + 1) * COLS)
        grad = dot(low[...], act[:, cols], TN).astype(BF16)
        for r in range(ROWS):
            for z in range(QUADS):
                start = r * W + z * S
                room[r, z, q * S : (q + 1) * S, :] = grad[start : start + S, :]
    hand_out(where, room, handed)


def hidden_back_kernel(where, low, slope, wd, wu, grad_pre, part, sums, back):
    back[...] = dot(low[...], wd[...], NN)
    sums[...] = jnp.zeros_like(sums)
    for q in range(4):
        cols = slice(q * COLS, (q + 1) * COLS)

        def body(i, cols=cols):
            at = (strip(i), cols)
            value = (back[at] * slope[at]).astype(BF16)
            grad_pre[at] = value
            sums[0:1, cols] += jnp.sum(value.astype(F32), axis=0, keepdims=True)

        each(LEN // STRIP, body)
    part[...] = dot(grad_pre[...], wu[...], NT).astype(BF16)


def up_grad_kernel(where, low, grad_pre, *refs):
    handed, room = refs[:5], refs[5]
    for z in range(QUADS):
        grad = dot(low[...], grad_pre[:, z * COLS : (z + 1) * COLS], TN).astype(BF16)
        for r in range(ROWS):
            room[r, z] = grad[r * W : (r + 1) * W, :]
    hand_out(where, room, handed)


def first_norm_kernel(where, grad_two, p0, p1, normed, inverse, vecs, wo, mixed, probs, attended, tokens, sums_two, sums_up, *refs):
    grad_one, grad_mixed, vector, room, low, back, inner, scores, sums = refs
    sums[...] = jnp.zeros_like(sums)
    gain = vector_row(vecs, 3)

    def body(i):
        at = strip(i)
        grad = grad_two[at, :] + (p0[at, :].astype(F32) + p1[at, :].astype(F32))
        unit = normed[at, :]
        out = norm_back_rows(grad, unit, inverse[at, :], gain)
        grad_one[at, :] = out
        rounded = out.astype(BF16)
        low[at, :] = rounded
        sums[0:1, :] += jnp.sum(rounded.astype(F32), axis=0, keepdims=True)
        sums[1:2, :] += jnp.sum(grad * unit, axis=0, keepdims=True)
        sums[2:3, :] += jnp.sum(grad, axis=0, keepdims=True)

    each(LEN // STRIP, body)
    back[...] = dot(wo[...], low[...], ((0,), (1,))).astype(BF16)
    for h in range(HEADS):
        base = h * 3 * HD
        query, keyed, valued = [mixed[base + k * HD : base + (k + 1) * HD, :] for k in range(3)]
        grad_out = back[h * HD : (h + 1) * HD, :]
        inner[...] = dot(valued, grad_out, TN)
        for q in range(2):
            at = slice(q * 128, (q + 1) * 128)
            prob = probs[h, :, at].astype(F32)
            grad = inner[:, at]
            mean = jnp.sum(grad * prob, axis=0, keepdims=True)
            scores[:, at] = (prob * (grad - mean)).astype(BF16)
        grads = [
            dot(keyed, scores[...], NN) * 0.125,
            dot(query, scores[...], NT) * 0.125,
            dot(grad_out, probs[h], NT),
        ]
        for k, grad in enumerate(grads):
            grad_mixed[base + k * HD : base + (k + 1) * HD, :] = grad.astype(BF16)
    half = HEADS // 2
    for r in range(ROWS):
        cut = tokens[:, r * W : (r + 1) * W]
        grad = dot(grad_mixed[...], cut, NN).astype(BF16)
        for z in range(QUADS):
            for h in range(half):
                starts = [(h + k * half) * 3 * HD + z * S for k in range(2)]
                pair = [grad[start : start + S, :] for start in starts]
                room[r, z, h * S : (h + 1) * S, :] = jnp.concatenate(pair, axis=1)
        grad = dot(low[:, r * W : (r + 1) * W], attended[...], ((0,), (1,))).astype(BF16)
        for z in range(QUADS):
            room[r, z, half * S :, :] = grad[z * S : (z + 1) * S, :]
    left = jnp.where(where[2] == 0, 1.0, 0.0)
    right = 1.0 - left
    total = dot(jnp.ones((8, LEN), BF16), grad_mixed[...], NT)[0:1, :]
    vector[...] = jnp.zeros_like(vector)
    for k, start in enumerate([0, 2 * HD]):
        at = [h * 3 * HD + start for h in range(HEADS)]
        row = jnp.concatenate([total[:, i : i + HD] for i in at], axis=1)
        vector[2 * k : 2 * k + 1, :] = row * left
        vector[2 * k + 1 : 2 * k + 2, :] = row * right
    for k, found in enumerate([sums, sums_two]):
        for i in range(3):
            for j in range(2):
                row = 4 + 6 * k + 2 * i + j
                vector[row : row + 1, :] = found[i : i + 1, j * COLS : (j + 1) * COLS] * left
    for j in range(4):
        row = sums_up[0:1, j * COLS : (j + 1) * COLS]
        vector[16 + j : 17 + j, :] = row * left
        vector[20 + j : 21 + j, :] = row * right


def first_hand_kernel(where, room, vector, carried, *refs):
    handed, first = refs[:-1], refs[-1]
    hand_out(where, room, [first, *handed])
    for k in range(4):
        carried[k * W : (k + 1) * W, :] = first[k]
    put_vector(carried, 4 * W, vector[...])


def token_back_kernel(where, grad_mixed, wj, part):
    for r in range(ROWS):
        part[:, r * W : (r + 1) * W] = dot(grad_mixed[...], wj[r], TN).astype(BF16)


def token_sum_kernel(where, result, grad_one, p0, p1, *refs):
    outs, total, room = refs[:4], refs[4], refs[5]

    def body(i):
        at = strip(i)
        total[at, :] = grad_one[at, :] + (p0[at, :].astype(F32) + p1[at, :].astype(F32))

    each(LEN // STRIP, body)
    pack_tokens(result, room, 0)
    pack_tokens(total, room, 1)
    for m, out in enumerate(outs):
        out[...] = room[where[0] ^ m]


def token_out_kernel(where, t0, t1, t2, t3, result, total):
    for m, piece in enumerate([t0, t1, t2, t3]):
        for k, out in enumerate([result, total]):
            for q in range(3):
                value = piece[k, :, q * 128 : (q + 1) * 128].astype(F32)
                out[where[0] ^ m, pl.ds(q, PAIRS, stride=3), :] = value


def pass_kernel(where, last_x, last_y, from_x, from_y, to_x, to_y):
    to_x[...] = (last_x[...].astype(F32) + from_y[0:2].astype(F32)).astype(BF16)
    to_y[...] = (last_y[...].astype(F32) + from_x[0:2].astype(F32)).astype(BF16)


def carry_pass_kernel(where, last_x, last_y, carried, from_x, from_y, to_x, to_y):
    to_x[...] = (last_x[...].astype(F32) + from_y[0:2].astype(F32)).astype(BF16)
    for k in range(2):
        rows = slice(k * W, (k + 1) * W)
        to_y[rows, :] = (last_y[k].astype(F32) + from_x[rows, :].astype(F32)).astype(BF16)
    put_vector(to_y, 2 * W, get_vector(carried, 4 * W) + get_vector(from_x, 4 * W))


def add_plane(own, from_x, from_y, last_x, last_y, room):
    for k in range(2):
        room[k] = (own[k].astype(F32) + from_x(k)) + last_y(k)
        room[2 + k] = (own[2 + k].astype(F32) + from_y(k)) + last_x(k)


def kept_blocks(ref):
    skip = ref.shape[0] - 2
    return lambda k: ref[skip + k].astype(F32)


def kept_rows(ref, start):
    return lambda k: ref[start + k * W : start + (k + 1) * W, :].astype(F32)


def line_kernel(where, own, from_x, from_y, last_x, last_y, kept, *refs):
    *sends, room = refs
    add_plane(own, *[kept_blocks(v) for v in (from_x, from_y, last_x, last_y)], room)
    if sends:
        kept[...] = room[where[1]]
        for mask, send in zip(ORDER[1:], sends):
            send[...] = room[where[1] ^ mask].astype(BF16)
    else:
        kept[...] = room[...]


def near_line_kernel(where, own, from_x, from_y, last_x, last_y, kept, *refs):
    *sends, room = refs
    add_plane(own, *[kept_blocks(v) for v in (from_x, from_y, last_x, last_y)], room)
    if sends:
        for k, mask in enumerate([0, 2]):
            kept[k] = room[where[1] ^ mask]
            sends[0][k] = room[where[1] ^ mask ^ 1].astype(BF16)
    else:
        kept[...] = room[...]


def far_line_kernel(where, kept, got, total, send):
    total[...] = kept[0] + got[0].astype(F32)
    send[...] = (kept[1] + got[1].astype(F32)).astype(BF16)


def carry_near_kernel(where, own, from_x, near_y, last_x, from_y, passed, kept, *refs):
    *sends, room = refs
    near_x = kept_rows(from_x, 2 * W)
    add_plane(own, near_x, kept_blocks(near_y), kept_blocks(last_x), kept_rows(from_y, 0), room)
    vector = get_vector(passed, 2 * W) + get_vector(from_y, 2 * W)
    if kept.ndim == 2:
        for k, mask in enumerate([0, 2]):
            rows = slice(k * W, (k + 1) * W)
            kept[rows, :] = room[where[1] ^ mask]
            sends[0][rows, :] = room[where[1] ^ mask ^ 1].astype(BF16)
        kept[2 * W :, :] = vector
        put_vector(sends[0], 2 * W, vector)
    else:
        kept[...] = room[...]
        sends[0][...] = vector


def add_vector(own, got, start):
    high, low = split_parts(own)
    return (high.astype(F32) + low.astype(F32)) + get_vector(got, start)


def carry_far_kernel(where, kept, got, total, send):
    total[0:W, :] = kept[0:W, :] + got[0:W, :].astype(F32)
    send[0:W, :] = (kept[W : 2 * W, :] + got[W : 2 * W, :].astype(F32)).astype(BF16)
    vector = add_vector(kept[2 * W :, :], got, 2 * W)
    total[W:, :] = vector
    put_vector(send, W, vector)


def adamw(weight, first, second, grad, rate, decay):
    first_new = BETA_ONE * first + (1.0 - BETA_ONE) * grad
    second_new = BETA_TWO * second + (1.0 - BETA_TWO) * grad * grad
    fix_one = 1.0 - BETA_ONE**STEP
    fix_two = 1.0 - BETA_TWO**STEP
    update = first_new / fix_one / (jnp.sqrt(second_new / fix_two) + ADAM_EPS) + decay * weight
    return (first_new, second_new, weight - rate * update)


JOINT_RATE = D ** (-0.5)
OUTPUT_RATE = (4 * D // LEN) ** (-0.5)
DOWN_RATE = FF ** (-0.5)


def first_adam_kernel(where, kept, got, jw, jf, js, ow, of, os, *refs):
    outs, vector = refs[:6], refs[6]
    grad = kept[0:W, :] + got[0:W, :].astype(F32)
    half = HEADS // 2
    for h in range(HEADS):
        rows = grad[h % half * S : (h % half + 1) * S, :]
        cut = rows[:, :W] if h < half else rows[:, W:]
        new = adamw(jw[h], jf[h], js[h], cut, JOINT_RATE, DECAY)
        for out, value in zip(outs[:3], new):
            out[h] = value
    new = adamw(ow[...], of[...], os[...], grad[half * S :, :], OUTPUT_RATE, DECAY)
    for out, value in zip(outs[3:], new):
        out[...] = value
    vector[...] = add_vector(kept[W:, :], got, W)


def vector_adam_kernel(where, mine, other, weight, first, second, *refs):
    outs, grad = refs[:3], refs[3]
    total = mine[...] + other[...]
    for q in range(3):
        grad[pl.ds(q, 24, stride=3), :] = total[0:24, q * 128 : (q + 1) * 128]
    new = adamw(weight[...], first[...], second[...], grad[...], VECTOR_RATE, 0.0)
    for out, value in zip(outs, new):
        out[...] = value


def up_adam_kernel(where, kept, r2, r1, r3, w, f, s, *outs):
    grad = (kept[...] + r1[...].astype(F32)) + (r2[...].astype(F32) + r3[...].astype(F32))
    for q in range(3):
        at = (pl.ds(q, W, stride=3), slice(None))
        cut = grad[:, q * 128 : (q + 1) * 128]
        for out, value in zip(outs, adamw(w[at], f[at], s[at], cut, JOINT_RATE, DECAY)):
            out[at] = value


def down_adam_kernel(where, kept, got, w, f, s, *outs):
    grad = kept[...] + got[...].astype(F32)
    for q in range(4):
        at = (slice(None), slice(q * COLS, (q + 1) * COLS))
        cut = grad[q * S : (q + 1) * S, :]
        for out, value in zip(outs, adamw(w[at], f[at], s[at], cut, DOWN_RATE, DECAY)):
            out[at] = value


def gather_line(where, shard, steps):
    if steps == 1:
        return [shard] + [swap(shard, "dp", mask) for mask in ORDER[1:]]
    pair = run(pair_kernel, where, [shard, swap(shard, "dp", 2)], [PAIR])[0]
    return [pair, swap(pair, "dp", 1)]


def gather_plane(where, line, after=()):
    line = run(whole_kernel, where, line, [LINE], after=after)[0]
    from_x = swap(line, "row", 1)
    from_y = swap(line, "row", 2)
    near_y, far_x = run(halves_kernel, where, [from_x, from_y], [PAIR] * 2)
    return [line, from_x, from_y, swap(near_y, "row", 1), swap(far_x, "row", 2)]


def scatter_first(handed):
    return [swap(value, "row", 1 + i % 2) for i, value in enumerate(handed[:-3])]


def scatter_pass(where, handed, got, after=()):
    return run(pass_kernel, where, handed[-3:-1] + got[:2], [PAIR] * 2, after=after)


def scatter_second(passed):
    return [swap(passed[0], "row", 1), swap(passed[1], "row", 2)]


def exchange(pieces):
    return [pieces[0]] + [swap(pieces[m], "row", m) for m in range(1, ROWS)]


def wide_lines(joint, output, up, down):
    order = jnp.array(ORDER)
    n = lax.axis_size("dp") // QUADS

    def collect(shard, axis):
        whole = lax.all_gather(shard.astype(BF16), "dp", axis=axis, tiled=True)
        return jnp.stack(jnp.split(whole, QUADS, axis=axis))

    joint = collect(joint, 1)
    half = HEADS // 2
    pair = joint.reshape(QUADS, 2, half, S, W)
    pair = jnp.transpose(pair, (0, 2, 3, 1, 4)).reshape(QUADS, half * S, 2 * W)
    first = jnp.concatenate([pair, collect(output, 0)], axis=1)
    second = collect(up, 1)
    third = collect(down, 0).reshape(QUADS, S, 4, COLS)
    third = jnp.transpose(third, (0, 2, 1, 3)).reshape(QUADS, W, COLS)
    return [jnp.take(value, order, axis=0) for value in (first, second, third)]


def wide_sums(first, second, third):
    def give(value, axis):
        whole = jnp.concatenate(list(value), axis=axis)
        return lax.psum_scatter(whole, "dp", scatter_dimension=axis, tiled=True)

    half = HEADS // 2
    pair = first[:, : half * S].reshape(QUADS, half, S, 2, W)
    joint = jnp.transpose(pair, (0, 3, 1, 2, 4)).reshape(QUADS, HEADS, S, W)
    third = jnp.transpose(third.reshape(QUADS, 4, S, COLS), (0, 2, 1, 3))
    third = third.reshape(QUADS, S, FFC)
    return give(joint, 1), give(first[:, half * S :], 0), give(second, 1), give(third, 0)


def per_device(
    tokens_in,
    lengths,
    joint_weight,
    joint_first,
    joint_second,
    output_weight,
    output_first,
    output_second,
    up_weight,
    up_first,
    up_second,
    down_weight,
    down_first,
    down_second,
    vectors,
    vector_first,
    vector_second,
    out_grad,
):
    r = lax.axis_index("row")
    col = lax.axis_index("col")
    direct = lax.axis_size("dp") == QUADS
    z = lax.axis_index("dp") if direct else jnp.int32(0)
    where = jnp.stack([r, z, col, lengths[0]]).astype(jnp.int32)

    joint = [jnp.transpose(v, (1, 2, 0)) for v in (joint_weight, joint_first, joint_second)]
    output = [v[:, 0].T for v in (output_weight, output_first, output_second)]
    down = [v[:, 0].T for v in (down_weight, down_first, down_second)]
    up = [up_weight, up_first, up_second]
    flat = up_weight.size // 128

    sent = [tokens_in.reshape(ROWS, PAIRS, 2 * W), out_grad.reshape(ROWS, PAIRS, 2 * W)]
    blocks_out = [shape(2, PAIRS, 2 * W)] * ROWS
    if direct:
        up = [v.reshape(flat, 128) for v in up]
        one = [shape(*CHUNK)]
        *pieces, first = run(
            opening_kernel,
            where,
            sent + [joint[0], output[0]],
            blocks_out + one,
            [
                pltpu.VMEM(sent[0].shape, BF16),
                pltpu.VMEM(sent[1].shape, BF16),
                pltpu.VMEM(joint[0].shape, F32),
                pltpu.VMEM(output[0].shape, F32),
                pltpu.SemaphoreType.DMA((4,)),
            ],
            limit=56,
            fetch=True,
        )
        tokens_pieces = exchange(pieces)
        first = gather_line(where, first, 1)
        first_pieces = gather_plane(where, first, tokens_pieces[1:])
        shard = run(second_shard_kernel, where, [up[0]], one, after=first[1:])[0]
        second = gather_line(where, shard, 2)
        second_pieces = gather_plane(where, second)
        shard = run(third_shard_kernel, where, [down[0]], one, after=second[1:])[0]
        third = gather_line(where, shard, 2)
        third_pieces = gather_plane(where, third, first_pieces[3:])
    else:
        tokens_pieces = exchange(run(token_kernel, where, sent, blocks_out))
        lines = wide_lines(joint[0], output[0], up_weight[:, 0], down[0])
        first_pieces, second_pieces, third_pieces = [
            gather_plane(where, list(line)) for line in lines
        ]

    vecs = vectors.reshape(72, 128)
    tokens, grads, wj, wo, mixed, probs, attended, part = run(
        attend_kernel,
        where,
        tokens_pieces + [vecs] + first_pieces,
        [
            shape(LEN, D),
            shape(LEN, D),
            shape(ROWS, MIX, W),
            shape(D, COLS),
            shape(MIX, LEN),
            shape(HEADS, LEN, LEN),
            shape(COLS, LEN),
            shape(LEN, D),
        ],
        [
            pltpu.VMEM((ROWS, 2, PAIRS, 2 * W), BF16),
            pltpu.VMEM((MIX, LEN), F32),
            pltpu.VMEM((LEN, LEN), F32),
            pltpu.VMEM((8, MIX), F32),
        ],
    )
    hidden, hidden_low, normed, inverse, act, slope, wu = run(
        up_kernel,
        where,
        [tokens, part, swap(part, "col", 1), vecs] + second_pieces,
        [
            shape(LEN, D, dtype=F32),
            shape(LEN, D),
            shape(LEN, D, dtype=F32),
            shape(LEN, 1, dtype=F32),
            shape(LEN, FFC),
            shape(LEN, FFC, dtype=F32),
            shape(D, FFC),
        ],
        [pltpu.VMEM((LEN, FFC), F32)],
    )
    wd, part = run(
        down_kernel, where, [act] + third_pieces, [shape(D, FFC), shape(LEN, D)]
    )
    out = run(
        second_norm_kernel,
        where,
        [hidden, part, swap(part, "col", 1), vecs, grads, act],
        [shape(LEN, D, dtype=F32), shape(LEN, D), shape(LEN, D, dtype=F32)]
        + [shape(8, D, dtype=F32)]
        + SPLIT,
        [pltpu.VMEM((ROWS, QUADS) + CHUNK, BF16)],
    )
    (result, grad_low, grad_two, sums_two), third_handed = out[:4], out[4:]
    third_got = scatter_first(third_handed)
    grad_pre, part, sums_up = run(
        hidden_back_kernel,
        where,
        [grad_low, slope, wd, wu],
        [shape(LEN, FFC), shape(LEN, D), shape(8, FFC, dtype=F32)],
        [pltpu.VMEM((LEN, FFC), F32)],
    )
    third_passed = scatter_pass(where, third_handed, third_got, [part])
    third_last = scatter_second(third_passed)
    second_handed = run(
        up_grad_kernel,
        where,
        [hidden_low, grad_pre],
        HANDED,
        [pltpu.VMEM((ROWS, QUADS) + CHUNK, BF16)],
        after=third_last,
    )
    grad_one, grad_mixed, vector, room = run(
        first_norm_kernel,
        where,
        [
            grad_two,
            part,
            swap(part, "col", 1),
            normed,
            inverse,
            vecs,
            wo,
            mixed,
            probs,
            attended,
            tokens,
            sums_two,
            sums_up,
        ],
        [shape(LEN, D, dtype=F32), shape(MIX, LEN), shape(*VECTOR, dtype=F32)]
        + [shape(ROWS, QUADS, *CHUNK)],
        [
            pltpu.VMEM((LEN, D), BF16),
            pltpu.VMEM((COLS, LEN), BF16),
            pltpu.VMEM((LEN, LEN), F32),
            pltpu.VMEM((LEN, LEN), BF16),
            pltpu.VMEM((8, D), F32),
        ],
    )
    first_handed = run(
        first_hand_kernel,
        where,
        [room, vector],
        [shape(*FIRST)] + HANDED[1:],
        [pltpu.VMEM((4,) + CHUNK, BF16)],
        after=third_passed + third_got[2:],
    )
    first_got = scatter_first(first_handed)
    first_passed = run(
        carry_pass_kernel,
        where,
        first_handed[2:4] + first_handed[:1] + first_got,
        [PAIR, shape(*CARRIED)],
    )
    first_last = scatter_second(first_passed)

    def like(values):
        return [shape(*v.shape, dtype=F32) for v in values]

    def sums(dims, split):
        return [shape(*dims, dtype=F32), shape(*split)]

    lines = [pltpu.VMEM((4,) + CHUNK, F32)]
    wide = [shape(4, *CHUNK, dtype=F32)]
    third_sum = run(
        near_line_kernel,
        where,
        third_handed[-1:] + third_got[2:] + third_last,
        sums(PAIR.shape, PAIR.shape) if direct else wide,
        lines,
    )
    if direct:
        got = swap(third_sum[1], "dp", 1)
        third_sum = run(far_line_kernel, where, [third_sum[0], got], sums(CHUNK, CHUNK))
    second_got = scatter_first(second_handed)
    second_passed = scatter_pass(where, second_handed, second_got, third_sum[1:])
    second_last = scatter_second(second_passed)
    first_sum = run(
        carry_near_kernel,
        where,
        first_handed[-1:] + first_got + first_last + first_passed[1:],
        sums((2 * W + VROWS, COLS), CARRIED) if direct else wide + [shape(*VECTOR, dtype=F32)],
        lines,
        after=second_passed,
    )
    second_sum = run(
        line_kernel,
        where,
        second_handed[-1:] + second_got + second_last,
        sums(CHUNK, CHUNK) + [shape(*CHUNK)] * 2 if direct else wide,
        lines,
    )
    ready = []
    if direct:
        got = swap(third_sum[1], "dp", 2)
        down_new = run(down_adam_kernel, where, [third_sum[0], got] + down, like(down))
        ready = down_new[:1]
        got = swap(first_sum[1], "dp", 1)
        first_sum = run(
            carry_far_kernel,
            where,
            [first_sum[0], got],
            sums((W + VROWS, COLS), (W + 2 * VROWS, COLS)),
        )
        got = swap(first_sum[1], "dp", 2)
        state = joint + output
        new = run(
            first_adam_kernel,
            where,
            [first_sum[0], got] + state,
            like(state) + [shape(*VECTOR, dtype=F32)],
        )
        joint_new, output_new, vector = new[:3], new[3:6], new[6]

    (part,) = run(token_back_kernel, where, [grad_mixed, wj], [shape(LEN, D)], after=second_passed)
    pieces = run(
        token_sum_kernel,
        where,
        [result, grad_one, part, swap(part, "col", 1)],
        [shape(2, PAIRS, 2 * W)] * ROWS,
        [pltpu.VMEM((LEN, D), F32), pltpu.VMEM((ROWS, 2, PAIRS, 2 * W), BF16)],
        after=ready,
    )
    flat_out = [shape(ROWS, 3 * PAIRS, 128, dtype=F32)] * 2
    out = run(token_out_kernel, where, exchange(pieces), flat_out)
    layer_out, tokens_grad = [v.reshape(tokens_in.shape) for v in out]

    if direct:
        got = [swap(v, "dp", mask) for v, mask in zip(second_sum[1:], ORDER[1:])]
        up_new = run(up_adam_kernel, where, second_sum[:1] + got + up, like(up), after=out[:1])
        up_new = [v.reshape(up_weight.shape) for v in up_new]
    else:
        grads = wide_sums(first_sum[0], second_sum[0], third_sum[0])
        joint_new = adamw(*joint, grads[0], JOINT_RATE, DECAY)
        output_new = adamw(*output, grads[1], OUTPUT_RATE, DECAY)
        up_new = adamw(*up, grads[2][:, None], JOINT_RATE, DECAY)
        down_new = adamw(*down, grads[3], DOWN_RATE, DECAY)
        vector = lax.psum(first_sum[1], "dp")

    state = [v.reshape(72, 128) for v in (vectors, vector_first, vector_second)]
    vector_new = run(
        vector_adam_kernel,
        where,
        [vector, swap(vector, "col", 1)] + state,
        like(state),
        [pltpu.VMEM((72, 128), F32)],
    )
    vector_new = [v.reshape(vectors.shape) for v in vector_new]

    return (
        layer_out,
        tokens_grad,
        *[jnp.transpose(v, (2, 0, 1)) for v in joint_new],
        *[v.T[:, None] for v in output_new],
        *up_new,
        *[v.T[:, None] for v in down_new],
        *vector_new,
    )


def solution(mesh):
    first = P("row", "col", "dp")
    second = P("col", "row", "dp")
    tokens = P("dp", "row", None)
    weights = (first,) * 3 + (second,) * 3 + (first,) * 3 + (second,) * 3 + (P(),) * 3
    in_specs = (tokens, P(("dp", "row"))) + weights + (tokens,)
    out_specs = (tokens, tokens) + weights
    return jax.shard_map(
        per_device, mesh=mesh, in_specs=in_specs, out_specs=out_specs, check_vma=False
    )
```

```python
from functools import partial

import jax
import jax.numpy as jnp
from jax import lax
from jax.experimental import pallas as pl
from jax.experimental.pallas import tpu as pltpu
from jax.sharding import PartitionSpec as P

D = 768
H = 12
HD = 64
FF = 3072
LEN = 256
STEP = 10

NORM_EPS = 1e-12
BETA_ONE = 0.9
BETA_TWO = 0.999
ADAM_EPS = 1e-08
DECAY = 0.01
VECTOR_RATE = 0.2

F32 = jnp.float32
BF16 = jnp.bfloat16

ROWS = 4
QUADS = 4
W = D // ROWS
S = W // QUADS
COLS = D // 2
HEADS = COLS // HD
FFC = FF // 2
MIX = HEADS * 3 * HD
PAIRS = LEN // 2
CHUNK = (W, COLS)
MIB = 1024 * 1024


def swap(value, axis, mask):
    n = lax.axis_size(axis)
    return lax.ppermute(value, axis, [(i, i ^ mask) for i in range(n)])


def shape(*dims, dtype=BF16):
    return jax.ShapeDtypeStruct(dims, dtype)


def run(kernel, where, args, outs, scratch=(), limit=8, after=(), fetch=False):
    vmem = pl.BlockSpec(memory_space=pltpu.VMEM)
    first, late = 1 + len(args), len(after)

    def body(*refs):
        kernel(*refs[:first], *refs[first + late :])

    out = pl.pallas_call(
        body,
        out_shape=outs,
        in_specs=[pl.BlockSpec(memory_space=pltpu.SMEM)]
        + [pl.BlockSpec(memory_space=pl.ANY) if fetch else vmem] * len(args)
        + [pl.BlockSpec(memory_space=pl.ANY)] * late,
        out_specs=[vmem] * len(outs),
        scratch_shapes=list(scratch),
        compiler_params=pltpu.CompilerParams(vmem_limit_bytes=limit * MIB),
    )(where, *args, *after)
    return list(out)


def dot(left, right, dims):
    return lax.dot_general(left, right, (dims, ((), ())), preferred_element_type=F32)


NN = ((1,), (0,))
NT = ((1,), (1,))
TN = ((0,), (0,))


def each(count, body):
    def step(i, carry):
        body(i)
        return carry

    lax.fori_loop(0, count, step, 0)


def row_of(vecs, start, count):
    return jnp.concatenate([vecs[start + i : start + i + 1, :] for i in range(count)], axis=1)


def vector_row(vecs, k):
    return row_of(vecs, 6 * k, 6)


def pick_col(where, left, right):
    return jnp.where(where[2] == 0, left, right)


def split_parts(value):
    high = value.astype(BF16)
    return high, (value - high.astype(F32)).astype(BF16)


def opening_kernel(where, tokens, grads, joint, output, *refs):
    outs, first = refs[:ROWS], refs[ROWS]
    tokens_in, grads_in, joint_in, output_in, done = refs[ROWS + 1 :]
    copies = [
        pltpu.make_async_copy(source, target, done.at[i])
        for i, (source, target) in enumerate(
            [(joint, joint_in), (output, output_in), (tokens, tokens_in), (grads, grads_in)]
        )
    ]
    for copy in copies:
        copy.start()
    copies[0].wait()
    copies[1].wait()
    for h in range(HEADS // 2):
        pair = [joint_in[h].astype(BF16), joint_in[h + HEADS // 2].astype(BF16)]
        first[h * S : (h + 1) * S, :] = jnp.concatenate(pair, axis=1)
    first[HEADS // 2 * S :, :] = output_in[...].astype(BF16)
    copies[2].wait()
    copies[3].wait()
    for m, out in enumerate(outs):
        out[0] = tokens_in[where[0] ^ m]
        out[1] = grads_in[where[0] ^ m]


def second_shard_kernel(where, up, second):
    for q in range(3):
        second[:, q * 128 : (q + 1) * 128] = up[pl.ds(q, W, stride=3), :].astype(BF16)


def third_shard_kernel(where, down, third):
    for q in range(4):
        third[q * S : (q + 1) * S, :] = down[:, q * COLS : (q + 1) * COLS].astype(BF16)


def pair_kernel(where, b0, b1, pair):
    pair[0] = b0[...]
    pair[1] = b1[...]


def whole_kernel(where, *refs):
    *pieces, line = refs
    for k in range(QUADS):
        line[k] = pieces[k][...] if len(pieces) == QUADS else pieces[k // 2][k % 2]


def halves_kernel(where, from_x, from_y, near_y, far_x):
    near_y[...] = from_y[0:2]
    far_x[...] = from_x[2:4]


def token_kernel(where, tokens, grads, *outs):
    for m, out in enumerate(outs):
        out[0] = tokens[where[0] ^ m]
        out[1] = grads[where[0] ^ m]


ORDER = (0, 2, 1, 3)


def blocks(where, pieces):
    found = [(piece, i) for piece in pieces for i in range(piece.shape[0])]
    for at, (piece, i) in enumerate(found):
        yield where[0] ^ (at // QUADS), where[1] ^ ORDER[at % QUADS], piece[i]


def unpack_tokens(x):
    parts = [jnp.concatenate([x[r][:, :W], x[r][:, W:]], axis=0) for r in range(ROWS)]
    return jnp.concatenate(parts, axis=1)


def pack_tokens(value, room, k):
    for r in range(ROWS):
        both = value[:, r * W : (r + 1) * W]
        room[r, k] = jnp.concatenate([both[:PAIRS], both[PAIRS:]], axis=1).astype(BF16)


def attend_kernel(where, t0, t1, t2, t3, vecs, *refs):
    pieces, refs = refs[:5], refs[5:]
    tokens, grads, wj, wo, mixed, probs, attended, part, room, mixing, scores, parts = refs
    for m, piece in enumerate([t0, t1, t2, t3]):
        room[where[0] ^ m] = piece[...]
    tokens[...] = unpack_tokens([room[r, 0] for r in range(ROWS)])
    grads[...] = unpack_tokens([room[r, 1] for r in range(ROWS)])
    half = HEADS // 2
    for row, quad, value in blocks(where, pieces):
        for h in range(half):
            rows = value[h * S : (h + 1) * S, :]
            for k, cut in enumerate([rows[:, :W], rows[:, W:]]):
                start = pl.multiple_of((h + k * half) * 3 * HD + quad * S, 16)
                wj[row, pl.ds(start, S), :] = cut
        start = pl.multiple_of(row * W + quad * S, 16)
        wo[pl.ds(start, S), :] = value[half * S :, :]
    total = dot(wj[0], tokens[:, :W], NT)
    for r in range(1, ROWS):
        total = total + dot(wj[r], tokens[:, r * W : (r + 1) * W], NT)
    mixing[...] = total
    query_bias, value_bias = [
        pick_col(where, row_of(vecs, start, 3), row_of(vecs, start + 3, 3)) for start in (0, 6)
    ]
    zero = jnp.zeros((1, HD), F32)
    row = []
    for h in range(HEADS):
        at = slice(h * HD, (h + 1) * HD)
        row += [query_bias[:, at], zero, value_bias[:, at]]
    row = jnp.concatenate(row, axis=1)
    high, low = split_parts(row)
    rest = (row - high.astype(F32) - low.astype(F32)).astype(BF16)
    parts[...] = jnp.zeros_like(parts)
    parts[0:1, :] = high.astype(F32)
    parts[1:2, :] = low.astype(F32)
    parts[2:3, :] = rest.astype(F32)
    bias = dot(parts[...].astype(BF16), jnp.ones((8, LEN), BF16), TN)
    mixed[...] = (mixing[...] + bias).astype(BF16)
    slot = lax.broadcasted_iota(jnp.int32, (LEN, 1), 0)
    slot = jnp.where(slot < PAIRS, 2 * slot, 2 * (slot - PAIRS) + 1)
    valid = slot < where[3]
    for h in range(HEADS):
        base = h * 3 * HD
        query, keyed, valued = [mixed[base + k * HD : base + (k + 1) * HD, :] for k in range(3)]
        scores[...] = dot(keyed, query, TN)
        for q in range(2):
            at = slice(q * 128, (q + 1) * 128)
            score = jnp.where(valid, scores[:, at] * 0.125, -1e30)
            expo = jnp.exp(score - jnp.max(score, axis=0, keepdims=True))
            prob = expo * (1.0 / jnp.sum(expo, axis=0, keepdims=True))
            probs[h, :, at] = prob.astype(BF16)
        attended[h * HD : (h + 1) * HD, :] = dot(valued, probs[h], NN).astype(BF16)
    part[...] = dot(attended[...], wo[...], ((0,), (1,))).astype(BF16)


def norm_rows(resid, gain, shift_by):
    mean = jnp.sum(resid, axis=1, keepdims=True) * (1.0 / D)
    var = jnp.sum(resid * resid, axis=1, keepdims=True) * (1.0 / D) - mean * mean
    inverse = lax.rsqrt(var + NORM_EPS)
    normed = (resid - mean) * inverse
    return normed * gain + shift_by, normed, inverse


def norm_back_rows(grad, normed, inverse, gain):
    scaled = grad * gain
    total = jnp.sum(scaled, axis=1, keepdims=True) * (1.0 / D)
    cross = jnp.sum(scaled * normed, axis=1, keepdims=True) * (1.0 / D)
    return (scaled - total - normed * cross) * inverse


STRIP = 32


def strip(i):
    return pl.ds(pl.multiple_of(i * STRIP, STRIP), STRIP)


def up_kernel(where, tokens, p0, p1, vecs, *refs):
    pieces, refs = refs[:5], refs[5:]
    hidden, low, normed, inverse, act, slope, wu, pre = refs
    for row, quad, value in blocks(where, pieces):
        rows = pl.ds(pl.multiple_of(row * W, W), W)
        wu[rows, pl.ds(pl.multiple_of(quad * COLS, COLS), COLS)] = value

    bias_out, gain, shift_by = [vector_row(vecs, k) for k in (2, 3, 4)]

    def first(i):
        at = strip(i)
        resid = tokens[at, :].astype(F32) + (p0[at, :].astype(F32) + p1[at, :].astype(F32))
        out, unit, scale = norm_rows(resid + bias_out, gain, shift_by)
        hidden[at, :] = out
        low[at, :] = out.astype(BF16)
        normed[at, :] = unit
        inverse[at, :] = scale

    each(LEN // STRIP, first)
    pre[...] = dot(low[...], wu[...], NN)
    bias = pick_col(where, row_of(vecs, 48, 12), row_of(vecs, 60, 12))
    for q in range(4):
        cols = slice(q * COLS, (q + 1) * COLS)
        shift_up = bias[:, cols]

        def second(i, cols=cols, shift_up=shift_up):
            at = (strip(i), cols)
            value = pre[at] + shift_up
            phi = 0.5 * (1.0 + lax.erf(value * (0.5**0.5)))
            density = jnp.exp(-0.5 * value * value) * 0.3989422804014327
            act[at] = (value * phi).astype(BF16)
            slope[at] = phi + value * density

        each(LEN // STRIP, second)


def down_kernel(where, act, *refs):
    pieces, wd, part = refs[:5], refs[5], refs[6]
    for row, quad, value in blocks(where, pieces):
        rows = pl.ds(pl.multiple_of(row * W + quad * S, 16), S)
        for q in range(4):
            wd[rows, q * COLS : (q + 1) * COLS] = value[q * S : (q + 1) * S, :]
    part[...] = dot(act[...], wd[...], NT).astype(BF16)


def hand_out(where, room, outs):
    r = where[0]
    last_x, last_y, own = outs[-3:]
    if len(outs) == 5:
        far_x, far_y = [out.at[0:2] for out in outs[:2]]
        near_x, near_y = [out.at[2:4] for out in outs[:2]]
    else:
        far_x, far_y, near_x, near_y = outs[:4]
    far_x[...] = room[r ^ 3, 0:2]
    far_y[...] = room[r ^ 3, 2:4]
    near_x[...] = room[r ^ 1, 0:2]
    near_y[...] = room[r ^ 2, 2:4]
    last_x[...] = room[r ^ 1, 2:4]
    last_y[...] = room[r ^ 2, 0:2]
    own[...] = room[r]


PAIR = shape(2, *CHUNK)
LINE = shape(4, *CHUNK)
HANDED = [LINE] * 2 + [PAIR] * 2 + [LINE]
SPLIT = [PAIR] * 6 + [LINE]

VROWS = 32
VECTOR = (VROWS, COLS)
CARRIED = (2 * W + 2 * VROWS, COLS)
FIRST = (4 * W + 2 * VROWS, COLS)


def put_vector(out, start, value):
    high, low = split_parts(value)
    out[start : start + VROWS, :] = high
    out[start + VROWS : start + 2 * VROWS, :] = low


def get_vector(value, start):
    high = value[start : start + VROWS, :].astype(F32)
    return high + value[start + VROWS : start + 2 * VROWS, :].astype(F32)


def second_norm_kernel(where, hidden, p0, p1, vecs, grads, act, *refs):
    (result, low, grad_two, sums), handed, room = refs[:4], refs[4:11], refs[11]
    sums[...] = jnp.zeros_like(sums)
    bias_down, gain, shift_by = [vector_row(vecs, k) for k in (5, 6, 7)]

    def body(i):
        at = strip(i)
        resid = hidden[at, :] + (p0[at, :].astype(F32) + p1[at, :].astype(F32)) + bias_down
        out, unit, scale = norm_rows(resid, gain, shift_by)
        result[at, :] = out
        grad = grads[at, :].astype(F32)
        back = norm_back_rows(grad, unit, scale, gain)
        grad_two[at, :] = back
        rounded = back.astype(BF16)
        low[at, :] = rounded
        sums[0:1, :] += jnp.sum(rounded.astype(F32), axis=0, keepdims=True)
        sums[1:2, :] += jnp.sum(grad * unit, axis=0, keepdims=True)
        sums[2:3, :] += jnp.sum(grad, axis=0, keepdims=True)

    each(LEN // STRIP, body)
    for q in range(4):
        cols = slice(q * COLS, (q + 1) * COLS)
        grad = dot(low[...], act[:, cols], TN).astype(BF16)
        for r in range(ROWS):
            for z in range(QUADS):
                start = r * W + z * S
                room[r, z, q * S : (q + 1) * S, :] = grad[start : start + S, :]
    hand_out(where, room, handed)


def hidden_back_kernel(where, low, slope, wd, wu, grad_pre, part, sums, back):
    back[...] = dot(low[...], wd[...], NN)
    sums[...] = jnp.zeros_like(sums)
    for q in range(4):
        cols = slice(q * COLS, (q + 1) * COLS)

        def body(i, cols=cols):
            at = (strip(i), cols)
            value = (back[at] * slope[at]).astype(BF16)
            grad_pre[at] = value
            sums[0:1, cols] += jnp.sum(value.astype(F32), axis=0, keepdims=True)

        each(LEN // STRIP, body)
    part[...] = dot(grad_pre[...], wu[...], NT).astype(BF16)


def up_grad_kernel(where, low, grad_pre, *refs):
    handed, room = refs[:5], refs[5]
    for z in range(QUADS):
        grad = dot(low[...], grad_pre[:, z * COLS : (z + 1) * COLS], TN).astype(BF16)
        for r in range(ROWS):
            room[r, z] = grad[r * W : (r + 1) * W, :]
    hand_out(where, room, handed)


def first_norm_kernel(where, grad_two, p0, p1, normed, inverse, vecs, wo, mixed, probs, attended, tokens, sums_two, sums_up, *refs):
    grad_one, grad_mixed, vector, room, low, back, inner, scores, sums = refs
    sums[...] = jnp.zeros_like(sums)
    gain = vector_row(vecs, 3)

    def body(i):
        at = strip(i)
        grad = grad_two[at, :] + (p0[at, :].astype(F32) + p1[at, :].astype(F32))
        unit = normed[at, :]
        out = norm_back_rows(grad, unit, inverse[at, :], gain)
        grad_one[at, :] = out
        rounded = out.astype(BF16)
        low[at, :] = rounded
        sums[0:1, :] += jnp.sum(rounded.astype(F32), axis=0, keepdims=True)
        sums[1:2, :] += jnp.sum(grad * unit, axis=0, keepdims=True)
        sums[2:3, :] += jnp.sum(grad, axis=0, keepdims=True)

    each(LEN // STRIP, body)
    back[...] = dot(wo[...], low[...], ((0,), (1,))).astype(BF16)
    for h in range(HEADS):
        base = h * 3 * HD
        query, keyed, valued = [mixed[base + k * HD : base + (k + 1) * HD, :] for k in range(3)]
        grad_out = back[h * HD : (h + 1) * HD, :]
        inner[...] = dot(valued, grad_out, TN)
        for q in range(2):
            at = slice(q * 128, (q + 1) * 128)
            prob = probs[h, :, at].astype(F32)
            grad = inner[:, at]
            mean = jnp.sum(grad * prob, axis=0, keepdims=True)
            scores[:, at] = (prob * (grad - mean)).astype(BF16)
        grads = [
            dot(keyed, scores[...], NN) * 0.125,
            dot(query, scores[...], NT) * 0.125,
            dot(grad_out, probs[h], NT),
        ]
        for k, grad in enumerate(grads):
            grad_mixed[base + k * HD : base + (k + 1) * HD, :] = grad.astype(BF16)
    half = HEADS // 2
    for r in range(ROWS):
        cut = tokens[:, r * W : (r + 1) * W]
        grad = dot(grad_mixed[...], cut, NN).astype(BF16)
        for z in range(QUADS):
            for h in range(half):
                starts = [(h + k * half) * 3 * HD + z * S for k in range(2)]
                pair = [grad[start : start + S, :] for start in starts]
                room[r, z, h * S : (h + 1) * S, :] = jnp.concatenate(pair, axis=1)
        grad = dot(low[:, r * W : (r + 1) * W], attended[...], ((0,), (1,))).astype(BF16)
        for z in range(QUADS):
            room[r, z, half * S :, :] = grad[z * S : (z + 1) * S, :]
    left = jnp.where(where[2] == 0, 1.0, 0.0)
    right = 1.0 - left
    total = dot(jnp.ones((8, LEN), BF16), grad_mixed[...], NT)[0:1, :]
    vector[...] = jnp.zeros_like(vector)
    for k, start in enumerate([0, 2 * HD]):
        at = [h * 3 * HD + start for h in range(HEADS)]
        row = jnp.concatenate([total[:, i : i + HD] for i in at], axis=1)
        vector[2 * k : 2 * k + 1, :] = row * left
        vector[2 * k + 1 : 2 * k + 2, :] = row * right
    for k, found in enumerate([sums, sums_two]):
        for i in range(3):
            for j in range(2):
                row = 4 + 6 * k + 2 * i + j
                vector[row : row + 1, :] = found[i : i + 1, j * COLS : (j + 1) * COLS] * left
    for j in range(4):
        row = sums_up[0:1, j * COLS : (j + 1) * COLS]
        vector[16 + j : 17 + j, :] = row * left
        vector[20 + j : 21 + j, :] = row * right


def first_hand_kernel(where, room, vector, carried, *refs):
    handed, first = refs[:-1], refs[-1]
    hand_out(where, room, [first, *handed])
    for k in range(4):
        carried[k * W : (k + 1) * W, :] = first[k]
    put_vector(carried, 4 * W, vector[...])


def token_back_kernel(where, grad_mixed, wj, part):
    for r in range(ROWS):
        part[:, r * W : (r + 1) * W] = dot(grad_mixed[...], wj[r], TN).astype(BF16)


def token_sum_kernel(where, result, grad_one, p0, p1, *refs):
    outs, total, room = refs[:4], refs[4], refs[5]

    def body(i):
        at = strip(i)
        total[at, :] = grad_one[at, :] + (p0[at, :].astype(F32) + p1[at, :].astype(F32))

    each(LEN // STRIP, body)
    pack_tokens(result, room, 0)
    pack_tokens(total, room, 1)
    for m, out in enumerate(outs):
        out[...] = room[where[0] ^ m]


def token_out_kernel(where, t0, t1, t2, t3, result, total):
    for m, piece in enumerate([t0, t1, t2, t3]):
        for k, out in enumerate([result, total]):
            for q in range(3):
                value = piece[k, :, q * 128 : (q + 1) * 128].astype(F32)
                out[where[0] ^ m, pl.ds(q, PAIRS, stride=3), :] = value


def pass_kernel(where, last_x, last_y, from_x, from_y, to_x, to_y):
    to_x[...] = (last_x[...].astype(F32) + from_y[0:2].astype(F32)).astype(BF16)
    to_y[...] = (last_y[...].astype(F32) + from_x[0:2].astype(F32)).astype(BF16)


def carry_pass_kernel(where, last_x, last_y, carried, from_x, from_y, to_x, to_y):
    to_x[...] = (last_x[...].astype(F32) + from_y[0:2].astype(F32)).astype(BF16)
    for k in range(2):
        rows = slice(k * W, (k + 1) * W)
        to_y[rows, :] = (last_y[k].astype(F32) + from_x[rows, :].astype(F32)).astype(BF16)
    put_vector(to_y, 2 * W, get_vector(carried, 4 * W) + get_vector(from_x, 4 * W))


def add_plane(own, from_x, from_y, last_x, last_y, room):
    for k in range(2):
        room[k] = (own[k].astype(F32) + from_x(k)) + last_y(k)
        room[2 + k] = (own[2 + k].astype(F32) + from_y(k)) + last_x(k)


def kept_blocks(ref):
    skip = ref.shape[0] - 2
    return lambda k: ref[skip + k].astype(F32)


def kept_rows(ref, start):
    return lambda k: ref[start + k * W : start + (k + 1) * W, :].astype(F32)


def line_kernel(where, own, from_x, from_y, last_x, last_y, kept, *refs):
    *sends, room = refs
    add_plane(own, *[kept_blocks(v) for v in (from_x, from_y, last_x, last_y)], room)
    if sends:
        kept[...] = room[where[1]]
        for mask, send in zip(ORDER[1:], sends):
            send[...] = room[where[1] ^ mask].astype(BF16)
    else:
        kept[...] = room[...]


def near_line_kernel(where, own, from_x, from_y, last_x, last_y, kept, *refs):
    *sends, room = refs
    add_plane(own, *[kept_blocks(v) for v in (from_x, from_y, last_x, last_y)], room)
    if sends:
        for k, mask in enumerate([0, 2]):
            kept[k] = room[where[1] ^ mask]
            sends[0][k] = room[where[1] ^ mask ^ 1].astype(BF16)
    else:
        kept[...] = room[...]


def far_line_kernel(where, kept, got, total, send):
    total[...] = kept[0] + got[0].astype(F32)
    send[...] = (kept[1] + got[1].astype(F32)).astype(BF16)


def carry_near_kernel(where, own, from_x, near_y, last_x, from_y, passed, kept, *refs):
    *sends, room = refs
    near_x = kept_rows(from_x, 2 * W)
    add_plane(own, near_x, kept_blocks(near_y), kept_blocks(last_x), kept_rows(from_y, 0), room)
    vector = get_vector(passed, 2 * W) + get_vector(from_y, 2 * W)
    if kept.ndim == 2:
        for k, mask in enumerate([0, 2]):
            rows = slice(k * W, (k + 1) * W)
            kept[rows, :] = room[where[1] ^ mask]
            sends[0][rows, :] = room[where[1] ^ mask ^ 1].astype(BF16)
        kept[2 * W :, :] = vector
        put_vector(sends[0], 2 * W, vector)
    else:
        kept[...] = room[...]
        sends[0][...] = vector


def add_vector(own, got, start):
    high, low = split_parts(own)
    return (high.astype(F32) + low.astype(F32)) + get_vector(got, start)


def carry_far_kernel(where, kept, got, total, send):
    total[0:W, :] = kept[0:W, :] + got[0:W, :].astype(F32)
    send[0:W, :] = (kept[W : 2 * W, :] + got[W : 2 * W, :].astype(F32)).astype(BF16)
    vector = add_vector(kept[2 * W :, :], got, 2 * W)
    total[W:, :] = vector
    put_vector(send, W, vector)


def adamw(weight, first, second, grad, rate, decay):
    first_new = BETA_ONE * first + (1.0 - BETA_ONE) * grad
    second_new = BETA_TWO * second + (1.0 - BETA_TWO) * grad * grad
    fix_one = 1.0 - BETA_ONE**STEP
    fix_two = 1.0 - BETA_TWO**STEP
    update = first_new / fix_one / (jnp.sqrt(second_new / fix_two) + ADAM_EPS) + decay * weight
    return (first_new, second_new, weight - rate * update)


JOINT_RATE = D ** (-0.5)
OUTPUT_RATE = (4 * D // LEN) ** (-0.5)
DOWN_RATE = FF ** (-0.5)


def first_adam_kernel(where, kept, got, jw, jf, js, ow, of, os, *refs):
    outs, vector = refs[:6], refs[6]
    grad = kept[0:W, :] + got[0:W, :].astype(F32)
    half = HEADS // 2
    for h in range(HEADS):
        rows = grad[h % half * S : (h % half + 1) * S, :]
        cut = rows[:, :W] if h < half else rows[:, W:]
        new = adamw(jw[h], jf[h], js[h], cut, JOINT_RATE, DECAY)
        for out, value in zip(outs[:3], new):
            out[h] = value
    new = adamw(ow[...], of[...], os[...], grad[half * S :, :], OUTPUT_RATE, DECAY)
    for out, value in zip(outs[3:], new):
        out[...] = value
    vector[...] = add_vector(kept[W:, :], got, W)


def vector_adam_kernel(where, mine, other, weight, first, second, *refs):
    outs, grad = refs[:3], refs[3]
    total = mine[...] + other[...]
    for q in range(3):
        grad[pl.ds(q, 24, stride=3), :] = total[0:24, q * 128 : (q + 1) * 128]
    new = adamw(weight[...], first[...], second[...], grad[...], VECTOR_RATE, 0.0)
    for out, value in zip(outs, new):
        out[...] = value


def up_adam_kernel(where, kept, r2, r1, r3, w, f, s, *outs):
    grad = (kept[...] + r1[...].astype(F32)) + (r2[...].astype(F32) + r3[...].astype(F32))
    for q in range(3):
        at = (pl.ds(q, W, stride=3), slice(None))
        cut = grad[:, q * 128 : (q + 1) * 128]
        for out, value in zip(outs, adamw(w[at], f[at], s[at], cut, JOINT_RATE, DECAY)):
            out[at] = value


def down_adam_kernel(where, kept, got, w, f, s, *outs):
    grad = kept[...] + got[...].astype(F32)
    for q in range(4):
        at = (slice(None), slice(q * COLS, (q + 1) * COLS))
        cut = grad[q * S : (q + 1) * S, :]
        for out, value in zip(outs, adamw(w[at], f[at], s[at], cut, DOWN_RATE, DECAY)):
            out[at] = value


def gather_line(where, shard, steps):
    if steps == 1:
        return [shard] + [swap(shard, "dp", mask) for mask in ORDER[1:]]
    pair = run(pair_kernel, where, [shard, swap(shard, "dp", 2)], [PAIR])[0]
    return [pair, swap(pair, "dp", 1)]


def gather_plane(where, line, after=()):
    line = run(whole_kernel, where, line, [LINE], after=after)[0]
    from_x = swap(line, "row", 1)
    from_y = swap(line, "row", 2)
    near_y, far_x = run(halves_kernel, where, [from_x, from_y], [PAIR] * 2)
    return [line, from_x, from_y, swap(near_y, "row", 1), swap(far_x, "row", 2)]


def scatter_first(handed):
    return [swap(value, "row", 1 + i % 2) for i, value in enumerate(handed[:-3])]


def scatter_pass(where, handed, got, after=()):
    return run(pass_kernel, where, handed[-3:-1] + got[:2], [PAIR] * 2, after=after)


def scatter_second(passed):
    return [swap(passed[0], "row", 1), swap(passed[1], "row", 2)]


def exchange(pieces):
    return [pieces[0]] + [swap(pieces[m], "row", m) for m in range(1, ROWS)]


def wide_lines(joint, output, up, down):
    order = jnp.array(ORDER)
    n = lax.axis_size("dp") // QUADS

    def collect(shard, axis):
        whole = lax.all_gather(shard.astype(BF16), "dp", axis=axis, tiled=True)
        return jnp.stack(jnp.split(whole, QUADS, axis=axis))

    joint = collect(joint, 1)
    half = HEADS // 2
    pair = joint.reshape(QUADS, 2, half, S, W)
    pair = jnp.transpose(pair, (0, 2, 3, 1, 4)).reshape(QUADS, half * S, 2 * W)
    first = jnp.concatenate([pair, collect(output, 0)], axis=1)
    second = collect(up, 1)
    third = collect(down, 0).reshape(QUADS, S, 4, COLS)
    third = jnp.transpose(third, (0, 2, 1, 3)).reshape(QUADS, W, COLS)
    return [jnp.take(value, order, axis=0) for value in (first, second, third)]


def wide_sums(first, second, third):
    def give(value, axis):
        whole = jnp.concatenate(list(value), axis=axis)
        return lax.psum_scatter(whole, "dp", scatter_dimension=axis, tiled=True)

    half = HEADS // 2
    pair = first[:, : half * S].reshape(QUADS, half, S, 2, W)
    joint = jnp.transpose(pair, (0, 3, 1, 2, 4)).reshape(QUADS, HEADS, S, W)
    third = jnp.transpose(third.reshape(QUADS, 4, S, COLS), (0, 2, 1, 3))
    third = third.reshape(QUADS, S, FFC)
    return give(joint, 1), give(first[:, half * S :], 0), give(second, 1), give(third, 0)


def per_device(
    tokens_in,
    lengths,
    joint_weight,
    joint_first,
    joint_second,
    output_weight,
    output_first,
    output_second,
    up_weight,
    up_first,
    up_second,
    down_weight,
    down_first,
    down_second,
    vectors,
    vector_first,
    vector_second,
    out_grad,
):
    r = lax.axis_index("row")
    col = lax.axis_index("col")
    direct = lax.axis_size("dp") == QUADS
    z = lax.axis_index("dp") if direct else jnp.int32(0)
    where = jnp.stack([r, z, col, lengths[0]]).astype(jnp.int32)

    joint = [jnp.transpose(v, (1, 2, 0)) for v in (joint_weight, joint_first, joint_second)]
    output = [v[:, 0].T for v in (output_weight, output_first, output_second)]
    down = [v[:, 0].T for v in (down_weight, down_first, down_second)]
    up = [up_weight, up_first, up_second]
    flat = up_weight.size // 128

    sent = [tokens_in.reshape(ROWS, PAIRS, 2 * W), out_grad.reshape(ROWS, PAIRS, 2 * W)]
    blocks_out = [shape(2, PAIRS, 2 * W)] * ROWS
    if direct:
        up = [v.reshape(flat, 128) for v in up]
        one = [shape(*CHUNK)]
        *pieces, first = run(
            opening_kernel,
            where,
            sent + [joint[0], output[0]],
            blocks_out + one,
            [
                pltpu.VMEM(sent[0].shape, BF16),
                pltpu.VMEM(sent[1].shape, BF16),
                pltpu.VMEM(joint[0].shape, F32),
                pltpu.VMEM(output[0].shape, F32),
                pltpu.SemaphoreType.DMA((4,)),
            ],
            limit=56,
            fetch=True,
        )
        tokens_pieces = exchange(pieces)
        first = gather_line(where, first, 1)
        first_pieces = gather_plane(where, first, tokens_pieces[1:])
        shard = run(second_shard_kernel, where, [up[0]], one, after=first[1:])[0]
        second = gather_line(where, shard, 2)
        second_pieces = gather_plane(where, second)
        after = second_pieces[:1] + first_pieces[1:3]
        shard = run(third_shard_kernel, where, [down[0]], one, after=after)[0]
        third = gather_line(where, shard, 2)
        third_pieces = gather_plane(where, third, first_pieces[3:])
    else:
        tokens_pieces = exchange(run(token_kernel, where, sent, blocks_out))
        lines = wide_lines(joint[0], output[0], up_weight[:, 0], down[0])
        first_pieces, second_pieces, third_pieces = [
            gather_plane(where, list(line)) for line in lines
        ]

    vecs = vectors.reshape(72, 128)
    tokens, grads, wj, wo, mixed, probs, attended, part = run(
        attend_kernel,
        where,
        tokens_pieces + [vecs] + first_pieces,
        [
            shape(LEN, D),
            shape(LEN, D),
            shape(ROWS, MIX, W),
            shape(D, COLS),
            shape(MIX, LEN),
            shape(HEADS, LEN, LEN),
            shape(COLS, LEN),
            shape(LEN, D),
        ],
        [
            pltpu.VMEM((ROWS, 2, PAIRS, 2 * W), BF16),
            pltpu.VMEM((MIX, LEN), F32),
            pltpu.VMEM((LEN, LEN), F32),
            pltpu.VMEM((8, MIX), F32),
        ],
    )
    hidden, hidden_low, normed, inverse, act, slope, wu = run(
        up_kernel,
        where,
        [tokens, part, swap(part, "col", 1), vecs] + second_pieces,
        [
            shape(LEN, D, dtype=F32),
            shape(LEN, D),
            shape(LEN, D, dtype=F32),
            shape(LEN, 1, dtype=F32),
            shape(LEN, FFC),
            shape(LEN, FFC, dtype=F32),
            shape(D, FFC),
        ],
        [pltpu.VMEM((LEN, FFC), F32)],
    )
    wd, part = run(
        down_kernel, where, [act] + third_pieces, [shape(D, FFC), shape(LEN, D)]
    )
    out = run(
        second_norm_kernel,
        where,
        [hidden, part, swap(part, "col", 1), vecs, grads, act],
        [shape(LEN, D, dtype=F32), shape(LEN, D), shape(LEN, D, dtype=F32)]
        + [shape(8, D, dtype=F32)]
        + SPLIT,
        [pltpu.VMEM((ROWS, QUADS) + CHUNK, BF16)],
    )
    (result, grad_low, grad_two, sums_two), third_handed = out[:4], out[4:]
    third_got = scatter_first(third_handed)
    grad_pre, part, sums_up = run(
        hidden_back_kernel,
        where,
        [grad_low, slope, wd, wu],
        [shape(LEN, FFC), shape(LEN, D), shape(8, FFC, dtype=F32)],
        [pltpu.VMEM((LEN, FFC), F32)],
    )
    third_passed = scatter_pass(where, third_handed, third_got)
    third_last = scatter_second(third_passed)
    second_handed = run(
        up_grad_kernel,
        where,
        [hidden_low, grad_pre],
        HANDED,
        [pltpu.VMEM((ROWS, QUADS) + CHUNK, BF16)],
        after=third_last,
    )
    grad_one, grad_mixed, vector, room = run(
        first_norm_kernel,
        where,
        [
            grad_two,
            part,
            swap(part, "col", 1),
            normed,
            inverse,
            vecs,
            wo,
            mixed,
            probs,
            attended,
            tokens,
            sums_two,
            sums_up,
        ],
        [shape(LEN, D, dtype=F32), shape(MIX, LEN), shape(*VECTOR, dtype=F32)]
        + [shape(ROWS, QUADS, *CHUNK)],
        [
            pltpu.VMEM((LEN, D), BF16),
            pltpu.VMEM((COLS, LEN), BF16),
            pltpu.VMEM((LEN, LEN), F32),
            pltpu.VMEM((LEN, LEN), BF16),
            pltpu.VMEM((8, D), F32),
        ],
    )
    first_handed = run(
        first_hand_kernel,
        where,
        [room, vector],
        [shape(*FIRST)] + HANDED[1:],
        [pltpu.VMEM((4,) + CHUNK, BF16)],
        after=third_passed + third_got[2:],
    )
    first_got = scatter_first(first_handed)
    (part,) = run(token_back_kernel, where, [grad_mixed, wj], [shape(LEN, D)], after=first_handed[:1])
    pieces = run(
        token_sum_kernel,
        where,
        [result, grad_one, part, swap(part, "col", 1)],
        [shape(2, PAIRS, 2 * W)] * ROWS,
        [pltpu.VMEM((LEN, D), F32), pltpu.VMEM((ROWS, 2, PAIRS, 2 * W), BF16)],
    )
    first_passed = run(
        carry_pass_kernel,
        where,
        first_handed[2:4] + first_handed[:1] + first_got,
        [PAIR, shape(*CARRIED)],
        after=pieces[:1],
    )
    first_last = scatter_second(first_passed)

    def like(values):
        return [shape(*v.shape, dtype=F32) for v in values]

    def sums(dims, split):
        return [shape(*dims, dtype=F32), shape(*split)]

    lines = [pltpu.VMEM((4,) + CHUNK, F32)]
    wide = [shape(4, *CHUNK, dtype=F32)]
    third_sum = run(
        near_line_kernel,
        where,
        third_handed[-1:] + third_got[2:] + third_last,
        sums(PAIR.shape, PAIR.shape) if direct else wide,
        lines,
    )
    if direct:
        got = swap(third_sum[1], "dp", 1)
        third_sum = run(far_line_kernel, where, [third_sum[0], got], sums(CHUNK, CHUNK))
        got = swap(third_sum[1], "dp", 2)
        down_new = run(down_adam_kernel, where, [third_sum[0], got] + down, like(down))
        ready = down_new[:1]
    else:
        ready = []
    second_got = scatter_first(second_handed)
    second_passed = scatter_pass(where, second_handed, second_got, ready)
    second_last = scatter_second(second_passed)
    first_sum = run(
        carry_near_kernel,
        where,
        first_handed[-1:] + first_got + first_last + first_passed[1:],
        sums((2 * W + VROWS, COLS), CARRIED) if direct else wide + [shape(*VECTOR, dtype=F32)],
        lines,
        after=second_passed,
    )
    second_sum = run(
        line_kernel,
        where,
        second_handed[-1:] + second_got + second_last,
        sums(CHUNK, CHUNK) + [shape(*CHUNK)] * 2 if direct else wide,
        lines,
    )
    if direct:
        got = swap(first_sum[1], "dp", 1)
        first_sum = run(
            carry_far_kernel,
            where,
            [first_sum[0], got],
            sums((W + VROWS, COLS), (W + 2 * VROWS, COLS)),
        )
        got = swap(first_sum[1], "dp", 2)
        state = joint + output
        new = run(
            first_adam_kernel,
            where,
            [first_sum[0], got] + state,
            like(state) + [shape(*VECTOR, dtype=F32)],
        )
        joint_new, output_new, vector = new[:3], new[3:6], new[6]

    flat_out = [shape(ROWS, 3 * PAIRS, 128, dtype=F32)] * 2
    out = run(token_out_kernel, where, exchange(pieces), flat_out)
    layer_out, tokens_grad = [v.reshape(tokens_in.shape) for v in out]

    if direct:
        got = [swap(v, "dp", mask) for v, mask in zip(second_sum[1:], ORDER[1:])]
        up_new = run(up_adam_kernel, where, second_sum[:1] + got + up, like(up), after=out[:1])
        up_new = [v.reshape(up_weight.shape) for v in up_new]
    else:
        grads = wide_sums(first_sum[0], second_sum[0], third_sum[0])
        joint_new = adamw(*joint, grads[0], JOINT_RATE, DECAY)
        output_new = adamw(*output, grads[1], OUTPUT_RATE, DECAY)
        up_new = adamw(*up, grads[2][:, None], JOINT_RATE, DECAY)
        down_new = adamw(*down, grads[3], DOWN_RATE, DECAY)
        vector = lax.psum(first_sum[1], "dp")

    state = [v.reshape(72, 128) for v in (vectors, vector_first, vector_second)]
    vector_new = run(
        vector_adam_kernel,
        where,
        [vector, swap(vector, "col", 1)] + state,
        like(state),
        [pltpu.VMEM((72, 128), F32)],
    )
    vector_new = [v.reshape(vectors.shape) for v in vector_new]

    return (
        layer_out,
        tokens_grad,
        *[jnp.transpose(v, (2, 0, 1)) for v in joint_new],
        *[v.T[:, None] for v in output_new],
        *up_new,
        *[v.T[:, None] for v in down_new],
        *vector_new,
    )


def solution(mesh):
    first = P("row", "col", "dp")
    second = P("col", "row", "dp")
    tokens = P("dp", "row", None)
    weights = (first,) * 3 + (second,) * 3 + (first,) * 3 + (second,) * 3 + (P(),) * 3
    in_specs = (tokens, P(("dp", "row"))) + weights + (tokens,)
    out_specs = (tokens, tokens) + weights
    return jax.shard_map(
        per_device, mesh=mesh, in_specs=in_specs, out_specs=out_specs, check_vma=False
    )
```

```python
from functools import partial

import jax
import jax.numpy as jnp
from jax import lax
from jax.experimental import pallas as pl
from jax.experimental.pallas import tpu as pltpu
from jax.sharding import PartitionSpec as P

D = 768
H = 12
HD = 64
FF = 3072
LEN = 256
STEP = 10

NORM_EPS = 1e-12
BETA_ONE = 0.9
BETA_TWO = 0.999
ADAM_EPS = 1e-08
DECAY = 0.01
VECTOR_RATE = 0.2

F32 = jnp.float32
BF16 = jnp.bfloat16

ROWS = 4
QUADS = 4
W = D // ROWS
S = W // QUADS
COLS = D // 2
HEADS = COLS // HD
FFC = FF // 2
MIX = HEADS * 3 * HD
PAIRS = LEN // 2
CHUNK = (W, COLS)
PART = (3 * S, COLS)
CROSS = (S, COLS)
MIB = 1024 * 1024


def swap(value, axis, mask):
    n = lax.axis_size(axis)
    return lax.ppermute(value, axis, [(i, i ^ mask) for i in range(n)])


def shape(*dims, dtype=BF16):
    return jax.ShapeDtypeStruct(dims, dtype)


def run(kernel, where, args, outs, scratch=(), limit=8, after=(), fetch=False):
    vmem = pl.BlockSpec(memory_space=pltpu.VMEM)
    first, late = 1 + len(args), len(after)

    def body(*refs):
        kernel(*refs[:first], *refs[first + late :])

    out = pl.pallas_call(
        body,
        out_shape=outs,
        in_specs=[pl.BlockSpec(memory_space=pltpu.SMEM)]
        + [pl.BlockSpec(memory_space=pl.ANY) if fetch else vmem] * len(args)
        + [pl.BlockSpec(memory_space=pl.ANY)] * late,
        out_specs=[vmem] * len(outs),
        scratch_shapes=list(scratch),
        compiler_params=pltpu.CompilerParams(vmem_limit_bytes=limit * MIB),
    )(where, *args, *after)
    return list(out)


def dot(left, right, dims):
    return lax.dot_general(left, right, (dims, ((), ())), preferred_element_type=F32)


NN = ((1,), (0,))
NT = ((1,), (1,))
TN = ((0,), (0,))


def each(count, body):
    def step(i, carry):
        body(i)
        return carry

    lax.fori_loop(0, count, step, 0)


def row_of(vecs, start, count):
    return jnp.concatenate([vecs[start + i : start + i + 1, :] for i in range(count)], axis=1)


def vector_row(vecs, k):
    return row_of(vecs, 6 * k, 6)


def pick_col(where, left, right):
    return jnp.where(where[2] == 0, left, right)


def split_parts(value):
    high = value.astype(BF16)
    return high, (value - high.astype(F32)).astype(BF16)


def opening_kernel(where, tokens, grads, joint, output, down, *refs):
    outs, first = refs[:ROWS], refs[ROWS]
    tokens_in, grads_in, joint_in, output_in, down_in, done = refs[ROWS + 1 :]
    copies = [
        pltpu.make_async_copy(source, target, done.at[i])
        for i, (source, target) in enumerate(
            [
                (joint, joint_in),
                (output, output_in),
                (tokens, tokens_in),
                (grads, grads_in),
                (down.at[:, 3 * COLS :], down_in),
            ]
        )
    ]
    for copy in copies:
        copy.start()
    copies[0].wait()
    copies[1].wait()
    for h in range(HEADS // 2):
        pair = [joint_in[h].astype(BF16), joint_in[h + HEADS // 2].astype(BF16)]
        first[h * S : (h + 1) * S, :] = jnp.concatenate(pair, axis=1)
    first[HEADS // 2 * S :, :] = output_in[...].astype(BF16)
    copies[2].wait()
    copies[3].wait()
    copies[4].wait()
    for m, out in enumerate(outs):
        out[0:PAIRS, :] = tokens_in[where[0] ^ m]
        out[PAIRS:LEN, :] = grads_in[where[0] ^ m]
        out[LEN:, :] = down_in[...].astype(BF16)


def second_shard_kernel(where, up, second):
    for q in range(3):
        second[:, q * 128 : (q + 1) * 128] = up[pl.ds(q, W, stride=3), :].astype(BF16)


def third_shard_kernel(where, down, third):
    for q in range(3):
        third[q * S : (q + 1) * S, :] = down[:, q * COLS : (q + 1) * COLS].astype(BF16)


def pair_kernel(where, b0, b1, pair):
    pair[0] = b0[...]
    pair[1] = b1[...]


def cross_kernel(where, t0, t1, t2, t3, plane):
    for m, piece in enumerate([t0, t1, t2, t3]):
        plane[m] = piece[LEN:, :]


def planes_kernel(where, b0, b1, planes):
    planes[0:ROWS] = b0[...]
    planes[ROWS:] = b1[...]


def whole_kernel(where, *refs):
    *pieces, line = refs
    for k in range(QUADS):
        line[k] = pieces[k][...] if len(pieces) == QUADS else pieces[k // 2][k % 2]


def halves_kernel(where, from_x, from_y, near_y, far_x):
    near_y[...] = from_y[0:2]
    far_x[...] = from_x[2:4]


def token_kernel(where, tokens, grads, *outs):
    for m, out in enumerate(outs):
        out[0:PAIRS, :] = tokens[where[0] ^ m]
        out[PAIRS:LEN, :] = grads[where[0] ^ m]


ORDER = (0, 2, 1, 3)


def blocks(where, pieces):
    found = [(piece, i) for piece in pieces for i in range(piece.shape[0])]
    for at, (piece, i) in enumerate(found):
        yield where[0] ^ (at // QUADS), where[1] ^ ORDER[at % QUADS], piece[i]


def cross_blocks(where, pieces):
    for j, piece in enumerate(pieces):
        for i in range(2 * ROWS):
            yield where[0] ^ (i % ROWS), where[1] ^ ORDER[2 * j + i // ROWS], piece[i]


def unpack_tokens(x):
    parts = [jnp.concatenate([x[r][:, :W], x[r][:, W:]], axis=0) for r in range(ROWS)]
    return jnp.concatenate(parts, axis=1)


def pack_tokens(value, room, k):
    for r in range(ROWS):
        both = value[:, r * W : (r + 1) * W]
        packed = jnp.concatenate([both[:PAIRS], both[PAIRS:]], axis=1).astype(BF16)
        room[r, k * PAIRS : (k + 1) * PAIRS, :] = packed


def attend_kernel(where, t0, t1, t2, t3, vecs, *refs):
    pieces, refs = refs[:5], refs[5:]
    tokens, grads, wj, wo, mixed, probs, attended, part, room, mixing, scores, parts = refs
    for m, piece in enumerate([t0, t1, t2, t3]):
        room[where[0] ^ m] = piece[0:LEN, :]
    tokens[...] = unpack_tokens([room[r, 0:PAIRS, :] for r in range(ROWS)])
    grads[...] = unpack_tokens([room[r, PAIRS:, :] for r in range(ROWS)])
    half = HEADS // 2
    for row, quad, value in blocks(where, pieces):
        for h in range(half):
            rows = value[h * S : (h + 1) * S, :]
            for k, cut in enumerate([rows[:, :W], rows[:, W:]]):
                start = pl.multiple_of((h + k * half) * 3 * HD + quad * S, 16)
                wj[row, pl.ds(start, S), :] = cut
        start = pl.multiple_of(row * W + quad * S, 16)
        wo[pl.ds(start, S), :] = value[half * S :, :]
    total = dot(wj[0], tokens[:, :W], NT)
    for r in range(1, ROWS):
        total = total + dot(wj[r], tokens[:, r * W : (r + 1) * W], NT)
    mixing[...] = total
    query_bias, value_bias = [
        pick_col(where, row_of(vecs, start, 3), row_of(vecs, start + 3, 3)) for start in (0, 6)
    ]
    zero = jnp.zeros((1, HD), F32)
    row = []
    for h in range(HEADS):
        at = slice(h * HD, (h + 1) * HD)
        row += [query_bias[:, at], zero, value_bias[:, at]]
    row = jnp.concatenate(row, axis=1)
    high, low = split_parts(row)
    rest = (row - high.astype(F32) - low.astype(F32)).astype(BF16)
    parts[...] = jnp.zeros_like(parts)
    parts[0:1, :] = high.astype(F32)
    parts[1:2, :] = low.astype(F32)
    parts[2:3, :] = rest.astype(F32)
    bias = dot(parts[...].astype(BF16), jnp.ones((8, LEN), BF16), TN)
    mixed[...] = (mixing[...] + bias).astype(BF16)
    slot = lax.broadcasted_iota(jnp.int32, (LEN, 1), 0)
    slot = jnp.where(slot < PAIRS, 2 * slot, 2 * (slot - PAIRS) + 1)
    valid = slot < where[3]
    for h in range(HEADS):
        base = h * 3 * HD
        query, keyed, valued = [mixed[base + k * HD : base + (k + 1) * HD, :] for k in range(3)]
        scores[...] = dot(keyed, query, TN)
        for q in range(2):
            at = slice(q * 128, (q + 1) * 128)
            score = jnp.where(valid, scores[:, at] * 0.125, -1e30)
            expo = jnp.exp(score - jnp.max(score, axis=0, keepdims=True))
            prob = expo * (1.0 / jnp.sum(expo, axis=0, keepdims=True))
            probs[h, :, at] = prob.astype(BF16)
        attended[h * HD : (h + 1) * HD, :] = dot(valued, probs[h], NN).astype(BF16)
    part[...] = dot(attended[...], wo[...], ((0,), (1,))).astype(BF16)


def norm_rows(resid, gain, shift_by):
    mean = jnp.sum(resid, axis=1, keepdims=True) * (1.0 / D)
    var = jnp.sum(resid * resid, axis=1, keepdims=True) * (1.0 / D) - mean * mean
    inverse = lax.rsqrt(var + NORM_EPS)
    normed = (resid - mean) * inverse
    return normed * gain + shift_by, normed, inverse


def norm_back_rows(grad, normed, inverse, gain):
    scaled = grad * gain
    total = jnp.sum(scaled, axis=1, keepdims=True) * (1.0 / D)
    cross = jnp.sum(scaled * normed, axis=1, keepdims=True) * (1.0 / D)
    return (scaled - total - normed * cross) * inverse


STRIP = 32


def strip(i):
    return pl.ds(pl.multiple_of(i * STRIP, STRIP), STRIP)


def up_kernel(where, tokens, p0, p1, vecs, *refs):
    pieces, refs = refs[:5], refs[5:]
    hidden, low, normed, inverse, act, slope, wu, pre = refs
    for row, quad, value in blocks(where, pieces):
        rows = pl.ds(pl.multiple_of(row * W, W), W)
        wu[rows, pl.ds(pl.multiple_of(quad * COLS, COLS), COLS)] = value

    bias_out, gain, shift_by = [vector_row(vecs, k) for k in (2, 3, 4)]

    def first(i):
        at = strip(i)
        resid = tokens[at, :].astype(F32) + (p0[at, :].astype(F32) + p1[at, :].astype(F32))
        out, unit, scale = norm_rows(resid + bias_out, gain, shift_by)
        hidden[at, :] = out
        low[at, :] = out.astype(BF16)
        normed[at, :] = unit
        inverse[at, :] = scale

    each(LEN // STRIP, first)
    pre[...] = dot(low[...], wu[...], NN)
    bias = pick_col(where, row_of(vecs, 48, 12), row_of(vecs, 60, 12))
    for q in range(4):
        cols = slice(q * COLS, (q + 1) * COLS)
        shift_up = bias[:, cols]

        def second(i, cols=cols, shift_up=shift_up):
            at = (strip(i), cols)
            value = pre[at] + shift_up
            phi = 0.5 * (1.0 + lax.erf(value * (0.5**0.5)))
            density = jnp.exp(-0.5 * value * value) * 0.3989422804014327
            act[at] = (value * phi).astype(BF16)
            slope[at] = phi + value * density

        each(LEN // STRIP, second)


def down_kernel(where, act, *refs):
    pieces, cross, wd, part = refs[:5], refs[5:7], refs[7], refs[8]
    for row, quad, value in blocks(where, pieces):
        rows = pl.ds(pl.multiple_of(row * W + quad * S, 16), S)
        for q in range(3):
            wd[rows, q * COLS : (q + 1) * COLS] = value[q * S : (q + 1) * S, :]
    for row, quad, value in cross_blocks(where, cross):
        rows = pl.ds(pl.multiple_of(row * W + quad * S, 16), S)
        wd[rows, 3 * COLS :] = value
    part[...] = dot(act[...], wd[...], NT).astype(BF16)


def hand_out(where, room, outs):
    r = where[0]
    to_x, to_y, last_x, last_y, own = outs
    to_x[0:2] = room[r ^ 3, 0:2]
    to_x[2:4] = room[r ^ 1, 0:2]
    to_y[0:2] = room[r ^ 3, 2:4]
    to_y[2:4] = room[r ^ 2, 2:4]
    last_x[...] = room[r ^ 1, 2:4]
    last_y[...] = room[r ^ 2, 0:2]
    own[...] = room[r]


def handed_shapes(block):
    pair, line = shape(2, *block), shape(4, *block)
    return [line] * 2 + [pair] * 2 + [line]


HANDED = handed_shapes(CHUNK)
PAIR = shape(2, *CHUNK)
PLANES = shape(2 * ROWS, *CROSS)

VROWS = 32
VECTOR = (VROWS, COLS)
CARRIED = (2 * W + 2 * VROWS, COLS)

LATE_X = 4 * W + 2 * VROWS
LATE_Y = 4 * W
FIRST_X = (LATE_X + 2 * PART[0], COLS)
FIRST_Y = (LATE_Y + 2 * PART[0], COLS)


def put_vector(out, start, value):
    high, low = split_parts(value)
    out[start : start + VROWS, :] = high
    out[start + VROWS : start + 2 * VROWS, :] = low


def get_vector(value, start):
    high = value[start : start + VROWS, :].astype(F32)
    return high + value[start + VROWS : start + 2 * VROWS, :].astype(F32)


def second_norm_kernel(where, hidden, p0, p1, vecs, grads, act, *refs):
    (result, low, grad_two, sums), handed = refs[:4], refs[4:9]
    cross_own, cross_send, room, cross = refs[9:]
    sums[...] = jnp.zeros_like(sums)
    bias_down, gain, shift_by = [vector_row(vecs, k) for k in (5, 6, 7)]

    def body(i):
        at = strip(i)
        resid = hidden[at, :] + (p0[at, :].astype(F32) + p1[at, :].astype(F32)) + bias_down
        out, unit, scale = norm_rows(resid, gain, shift_by)
        result[at, :] = out
        grad = grads[at, :].astype(F32)
        back = norm_back_rows(grad, unit, scale, gain)
        grad_two[at, :] = back
        rounded = back.astype(BF16)
        low[at, :] = rounded
        sums[0:1, :] += jnp.sum(rounded.astype(F32), axis=0, keepdims=True)
        sums[1:2, :] += jnp.sum(grad * unit, axis=0, keepdims=True)
        sums[2:3, :] += jnp.sum(grad, axis=0, keepdims=True)

    each(LEN // STRIP, body)
    for q in range(4):
        cols = slice(q * COLS, (q + 1) * COLS)
        grad = dot(low[...], act[:, cols], TN).astype(BF16)
        for r in range(ROWS):
            for z in range(QUADS):
                start = r * W + z * S
                if q < 3:
                    room[r, z, q * S : (q + 1) * S, :] = grad[start : start + S, :]
                else:
                    cross[z, r] = grad[start : start + S, :]
    hand_out(where, room, handed)
    for k, mask in enumerate([0, 2]):
        rows = slice(k * ROWS, (k + 1) * ROWS)
        cross_own[rows] = cross[where[1] ^ mask]
        cross_send[rows] = cross[where[1] ^ mask ^ 1]


def hidden_back_kernel(where, low, slope, wd, wu, grad_pre, part, sums, back):
    back[...] = dot(low[...], wd[...], NN)
    sums[...] = jnp.zeros_like(sums)
    for q in range(4):
        cols = slice(q * COLS, (q + 1) * COLS)

        def body(i, cols=cols):
            at = (strip(i), cols)
            value = (back[at] * slope[at]).astype(BF16)
            grad_pre[at] = value
            sums[0:1, cols] += jnp.sum(value.astype(F32), axis=0, keepdims=True)

        each(LEN // STRIP, body)
    part[...] = dot(grad_pre[...], wu[...], NT).astype(BF16)


def up_grad_kernel(where, low, grad_pre, *refs):
    handed, room = refs[:5], refs[5]
    for z in range(QUADS):
        grad = dot(low[...], grad_pre[:, z * COLS : (z + 1) * COLS], TN).astype(BF16)
        for r in range(ROWS):
            room[r, z] = grad[r * W : (r + 1) * W, :]
    hand_out(where, room, handed)


def first_norm_kernel(where, grad_two, p0, p1, normed, inverse, vecs, wo, mixed, probs, attended, tokens, sums_two, sums_up, *refs):
    grad_one, grad_mixed, vector, room, low, back, inner, scores, sums = refs
    sums[...] = jnp.zeros_like(sums)
    gain = vector_row(vecs, 3)

    def body(i):
        at = strip(i)
        grad = grad_two[at, :] + (p0[at, :].astype(F32) + p1[at, :].astype(F32))
        unit = normed[at, :]
        out = norm_back_rows(grad, unit, inverse[at, :], gain)
        grad_one[at, :] = out
        rounded = out.astype(BF16)
        low[at, :] = rounded
        sums[0:1, :] += jnp.sum(rounded.astype(F32), axis=0, keepdims=True)
        sums[1:2, :] += jnp.sum(grad * unit, axis=0, keepdims=True)
        sums[2:3, :] += jnp.sum(grad, axis=0, keepdims=True)

    each(LEN // STRIP, body)
    back[...] = dot(wo[...], low[...], ((0,), (1,))).astype(BF16)
    for h in range(HEADS):
        base = h * 3 * HD
        query, keyed, valued = [mixed[base + k * HD : base + (k + 1) * HD, :] for k in range(3)]
        grad_out = back[h * HD : (h + 1) * HD, :]
        inner[...] = dot(valued, grad_out, TN)
        for q in range(2):
            at = slice(q * 128, (q + 1) * 128)
            prob = probs[h, :, at].astype(F32)
            grad = inner[:, at]
            mean = jnp.sum(grad * prob, axis=0, keepdims=True)
            scores[:, at] = (prob * (grad - mean)).astype(BF16)
        grads = [
            dot(keyed, scores[...], NN) * 0.125,
            dot(query, scores[...], NT) * 0.125,
            dot(grad_out, probs[h], NT),
        ]
        for k, grad in enumerate(grads):
            grad_mixed[base + k * HD : base + (k + 1) * HD, :] = grad.astype(BF16)
    half = HEADS // 2
    for r in range(ROWS):
        cut = tokens[:, r * W : (r + 1) * W]
        grad = dot(grad_mixed[...], cut, NN).astype(BF16)
        for z in range(QUADS):
            for h in range(half):
                starts = [(h + k * half) * 3 * HD + z * S for k in range(2)]
                pair = [grad[start : start + S, :] for start in starts]
                room[r, z, h * S : (h + 1) * S, :] = jnp.concatenate(pair, axis=1)
        grad = dot(low[:, r * W : (r + 1) * W], attended[...], ((0,), (1,))).astype(BF16)
        for z in range(QUADS):
            room[r, z, half * S :, :] = grad[z * S : (z + 1) * S, :]
    left = jnp.where(where[2] == 0, 1.0, 0.0)
    right = 1.0 - left
    total = dot(jnp.ones((8, LEN), BF16), grad_mixed[...], NT)[0:1, :]
    vector[...] = jnp.zeros_like(vector)
    for k, start in enumerate([0, 2 * HD]):
        at = [h * 3 * HD + start for h in range(HEADS)]
        row = jnp.concatenate([total[:, i : i + HD] for i in at], axis=1)
        vector[2 * k : 2 * k + 1, :] = row * left
        vector[2 * k + 1 : 2 * k + 2, :] = row * right
    for k, found in enumerate([sums, sums_two]):
        for i in range(3):
            for j in range(2):
                row = 4 + 6 * k + 2 * i + j
                vector[row : row + 1, :] = found[i : i + 1, j * COLS : (j + 1) * COLS] * left
    for j in range(4):
        row = sums_up[0:1, j * COLS : (j + 1) * COLS]
        vector[16 + j : 17 + j, :] = row * left
        vector[20 + j : 21 + j, :] = row * right


def first_hand_kernel(where, room, vector, late_x, late_y, to_x, to_y, last_x, last_y, own):
    r = where[0]
    for k in range(2):
        far, near = slice(k * W, (k + 1) * W), slice((2 + k) * W, (3 + k) * W)
        to_x[far, :] = room[r ^ 3, k]
        to_x[near, :] = room[r ^ 1, k]
        to_y[far, :] = room[r ^ 3, 2 + k]
        to_y[near, :] = room[r ^ 2, 2 + k]
        for start, out, late in [(LATE_X, to_x, late_x), (LATE_Y, to_y, late_y)]:
            at = start + k * PART[0]
            out[at : at + PART[0], :] = late[k]
    last_x[...] = room[r ^ 1, 2:4]
    last_y[...] = room[r ^ 2, 0:2]
    own[...] = room[r]
    put_vector(to_x, 4 * W, vector[...])


def token_back_kernel(where, grad_mixed, wj, part):
    for r in range(ROWS):
        part[:, r * W : (r + 1) * W] = dot(grad_mixed[...], wj[r], TN).astype(BF16)


def token_sum_kernel(where, result, grad_one, p0, p1, *refs):
    total, room = refs[-2:]
    cross = [*refs[:2], refs[6]] if len(refs) > 6 else []
    outs = refs[2:6] if cross else refs[:4]

    def body(i):
        at = strip(i)
        total[at, :] = grad_one[at, :] + (p0[at, :].astype(F32) + p1[at, :].astype(F32))

    each(LEN // STRIP, body)
    pack_tokens(result, room, 0)
    pack_tokens(total, room, 1)
    for m, out in enumerate(outs):
        row = where[0] ^ m
        out[0:LEN, :] = room[row]
        if cross:
            kept, got, own = cross
            sums = kept[row] + got[row].astype(F32)
            out[LEN:, :] = sums.astype(BF16)
            if m == 0:
                own[...] = sums


def token_out_kernel(where, t0, t1, t2, t3, result, total):
    for m, piece in enumerate([t0, t1, t2, t3]):
        for k, out in enumerate([result, total]):
            for q in range(3):
                value = piece[k * PAIRS : (k + 1) * PAIRS, q * 128 : (q + 1) * 128].astype(F32)
                out[where[0] ^ m, pl.ds(q, PAIRS, stride=3), :] = value


def pass_kernel(where, last_x, last_y, from_x, from_y, to_x, to_y):
    to_x[...] = (last_x[...].astype(F32) + from_y[0:2].astype(F32)).astype(BF16)
    to_y[...] = (last_y[...].astype(F32) + from_x[0:2].astype(F32)).astype(BF16)


def carry_pass_kernel(where, last_x, last_y, carried, from_x, from_y, to_x, to_y):
    for k in range(2):
        rows = slice(k * W, (k + 1) * W)
        to_x[k] = (last_x[k].astype(F32) + from_y[rows, :].astype(F32)).astype(BF16)
        to_y[rows, :] = (last_y[k].astype(F32) + from_x[rows, :].astype(F32)).astype(BF16)
    put_vector(to_y, 2 * W, get_vector(carried, 4 * W) + get_vector(from_x, 4 * W))


def add_plane(own, from_x, from_y, last_x, last_y, room):
    for k in range(2):
        room[k] = (own[k].astype(F32) + from_x(k)) + last_y(k)
        room[2 + k] = (own[2 + k].astype(F32) + from_y(k)) + last_x(k)


def kept_blocks(ref):
    skip = ref.shape[0] - 2
    return lambda k: ref[skip + k].astype(F32)


def kept_rows(ref, start, rows=W):
    return lambda k: ref[start + k * rows : start + (k + 1) * rows, :].astype(F32)


def line_kernel(where, own, from_x, from_y, last_x, last_y, kept, *refs):
    *sends, room = refs
    add_plane(own, *[kept_blocks(v) for v in (from_x, from_y, last_x, last_y)], room)
    if sends:
        kept[...] = room[where[1]]
        for mask, send in zip(ORDER[1:], sends):
            send[...] = room[where[1] ^ mask].astype(BF16)
    else:
        kept[...] = room[...]


def near_line_kernel(where, own, from_x, from_y, late_x, late_y, kept, *refs):
    *sends, room = refs
    late = [kept_rows(late_x, LATE_X, PART[0]), kept_rows(late_y, LATE_Y, PART[0])]
    add_plane(own, kept_blocks(from_x), kept_blocks(from_y), *late, room)
    if sends:
        for k, mask in enumerate([0, 2]):
            kept[k] = room[where[1] ^ mask]
            sends[0][k] = room[where[1] ^ mask ^ 1].astype(BF16)
    else:
        kept[...] = room[...]


def far_line_kernel(where, kept, got, total, send):
    total[...] = kept[0] + got[0].astype(F32)
    send[...] = (kept[1] + got[1].astype(F32)).astype(BF16)


def cross_far_kernel(where, own, got, kept, send):
    kept[...] = own[0:ROWS].astype(F32) + got[0:ROWS].astype(F32)
    send[...] = (own[ROWS:].astype(F32) + got[ROWS:].astype(F32)).astype(BF16)


def carry_near_kernel(where, own, first_x, first_y, last_x, from_y, passed, kept, *refs):
    *sends, room = refs
    near = [kept_rows(first_x, 2 * W), kept_rows(first_y, 2 * W)]
    add_plane(own, *near, kept_blocks(last_x), kept_rows(from_y, 0), room)
    vector = get_vector(passed, 2 * W) + get_vector(from_y, 2 * W)
    if kept.ndim == 2:
        for k, mask in enumerate([0, 2]):
            rows = slice(k * W, (k + 1) * W)
            kept[rows, :] = room[where[1] ^ mask]
            sends[0][rows, :] = room[where[1] ^ mask ^ 1].astype(BF16)
        kept[2 * W :, :] = vector
        put_vector(sends[0], 2 * W, vector)
    else:
        kept[...] = room[...]
        sends[0][...] = vector


def add_vector(own, got, start):
    high, low = split_parts(own)
    return (high.astype(F32) + low.astype(F32)) + get_vector(got, start)


def carry_far_kernel(where, kept, got, total, send):
    total[0:W, :] = kept[0:W, :] + got[0:W, :].astype(F32)
    send[0:W, :] = (kept[W : 2 * W, :] + got[W : 2 * W, :].astype(F32)).astype(BF16)
    vector = add_vector(kept[2 * W :, :], got, 2 * W)
    total[W:, :] = vector
    put_vector(send, W, vector)


def adamw(weight, first, second, grad, rate, decay):
    first_new = BETA_ONE * first + (1.0 - BETA_ONE) * grad
    second_new = BETA_TWO * second + (1.0 - BETA_TWO) * grad * grad
    fix_one = 1.0 - BETA_ONE**STEP
    fix_two = 1.0 - BETA_TWO**STEP
    update = first_new / fix_one / (jnp.sqrt(second_new / fix_two) + ADAM_EPS) + decay * weight
    return (first_new, second_new, weight - rate * update)


JOINT_RATE = D ** (-0.5)
OUTPUT_RATE = (4 * D // LEN) ** (-0.5)
DOWN_RATE = FF ** (-0.5)


def first_adam_kernel(where, kept, got, jw, jf, js, ow, of, os, *refs):
    outs, vector = refs[:6], refs[6]
    grad = kept[0:W, :] + got[0:W, :].astype(F32)
    half = HEADS // 2
    for h in range(HEADS):
        rows = grad[h % half * S : (h % half + 1) * S, :]
        cut = rows[:, :W] if h < half else rows[:, W:]
        new = adamw(jw[h], jf[h], js[h], cut, JOINT_RATE, DECAY)
        for out, value in zip(outs[:3], new):
            out[h] = value
    new = adamw(ow[...], of[...], os[...], grad[half * S :, :], OUTPUT_RATE, DECAY)
    for out, value in zip(outs[3:], new):
        out[...] = value
    vector[...] = add_vector(kept[W:, :], got, W)


def vector_adam_kernel(where, mine, other, weight, first, second, *refs):
    outs, grad = refs[:3], refs[3]
    total = mine[...] + other[...]
    for q in range(3):
        grad[pl.ds(q, 24, stride=3), :] = total[0:24, q * 128 : (q + 1) * 128]
    new = adamw(weight[...], first[...], second[...], grad[...], VECTOR_RATE, 0.0)
    for out, value in zip(outs, new):
        out[...] = value


def up_adam_kernel(where, kept, r2, r1, r3, w, f, s, *outs):
    grad = (kept[...] + r1[...].astype(F32)) + (r2[...].astype(F32) + r3[...].astype(F32))
    for q in range(3):
        at = (pl.ds(q, W, stride=3), slice(None))
        cut = grad[:, q * 128 : (q + 1) * 128]
        for out, value in zip(outs, adamw(w[at], f[at], s[at], cut, JOINT_RATE, DECAY)):
            out[at] = value


def down_adam_kernel(where, kept, got, own, r1, r2, r3, w, f, s, *outs):
    far = r2[LEN:, :].astype(F32) + r3[LEN:, :].astype(F32)
    cross = (own[...] + r1[LEN:, :].astype(F32)) + far
    most = kept[...] + got[...].astype(F32)
    for q in range(4):
        at = (slice(None), slice(q * COLS, (q + 1) * COLS))
        cut = most[q * S : (q + 1) * S, :] if q < 3 else cross
        for out, value in zip(outs, adamw(w[at], f[at], s[at], cut, DOWN_RATE, DECAY)):
            out[at] = value


def gather_line(where, shard, steps):
    if steps == 1:
        return [shard] + [swap(shard, "dp", mask) for mask in ORDER[1:]]
    pair = [shape(2, *shard.shape)]
    pair = run(pair_kernel, where, [shard, swap(shard, "dp", 2)], pair)[0]
    return [pair, swap(pair, "dp", 1)]


def gather_plane(where, line, after=()):
    block = line[0].shape[-2:]
    line = run(whole_kernel, where, line, [shape(4, *block)], after=after)[0]
    from_x = swap(line, "row", 1)
    from_y = swap(line, "row", 2)
    near_y, far_x = run(halves_kernel, where, [from_x, from_y], [shape(2, *block)] * 2)
    return [line, from_x, from_y, swap(near_y, "row", 1), swap(far_x, "row", 2)]


def gather_cross(where, plane):
    planes = run(planes_kernel, where, [plane, swap(plane, "dp", 2)], [PLANES])[0]
    return [planes, swap(planes, "dp", 1)]


def scatter_first(handed):
    return [swap(value, "row", 1 + i % 2) for i, value in enumerate(handed[:-3])]


def scatter_pass(where, handed, got, after=()):
    pair = [shape(*handed[2].shape)] * 2
    return run(pass_kernel, where, handed[2:4] + got, pair, after=after)


def scatter_second(passed):
    return [swap(passed[0], "row", 1), swap(passed[1], "row", 2)]


def exchange(pieces):
    return [pieces[0]] + [swap(pieces[m], "row", m) for m in range(1, ROWS)]


def wide_lines(joint, output, up, down):
    order = jnp.array(ORDER)
    n = lax.axis_size("dp") // QUADS

    def collect(shard, axis):
        whole = lax.all_gather(shard.astype(BF16), "dp", axis=axis, tiled=True)
        return jnp.stack(jnp.split(whole, QUADS, axis=axis))

    joint = collect(joint, 1)
    half = HEADS // 2
    pair = joint.reshape(QUADS, 2, half, S, W)
    pair = jnp.transpose(pair, (0, 2, 3, 1, 4)).reshape(QUADS, half * S, 2 * W)
    first = jnp.concatenate([pair, collect(output, 0)], axis=1)
    second = collect(up, 1)
    third = collect(down, 0).reshape(QUADS, S, 4, COLS)
    third = jnp.transpose(third, (0, 2, 1, 3)).reshape(QUADS, W, COLS)
    return [jnp.take(value, order, axis=0) for value in (first, second, third)]


def wide_sums(first, second, third):
    def give(value, axis):
        whole = jnp.concatenate(list(value), axis=axis)
        return lax.psum_scatter(whole, "dp", scatter_dimension=axis, tiled=True)

    half = HEADS // 2
    pair = first[:, : half * S].reshape(QUADS, half, S, 2, W)
    joint = jnp.transpose(pair, (0, 3, 1, 2, 4)).reshape(QUADS, HEADS, S, W)
    third = jnp.transpose(third.reshape(QUADS, 4, S, COLS), (0, 2, 1, 3))
    third = third.reshape(QUADS, S, FFC)
    return give(joint, 1), give(first[:, half * S :], 0), give(second, 1), give(third, 0)


def per_device(
    tokens_in,
    lengths,
    joint_weight,
    joint_first,
    joint_second,
    output_weight,
    output_first,
    output_second,
    up_weight,
    up_first,
    up_second,
    down_weight,
    down_first,
    down_second,
    vectors,
    vector_first,
    vector_second,
    out_grad,
):
    r = lax.axis_index("row")
    col = lax.axis_index("col")
    direct = lax.axis_size("dp") == QUADS
    z = lax.axis_index("dp") if direct else jnp.int32(0)
    where = jnp.stack([r, z, col, lengths[0]]).astype(jnp.int32)

    joint = [jnp.transpose(v, (1, 2, 0)) for v in (joint_weight, joint_first, joint_second)]
    output = [v[:, 0].T for v in (output_weight, output_first, output_second)]
    down = [v[:, 0].T for v in (down_weight, down_first, down_second)]
    up = [up_weight, up_first, up_second]
    flat = up_weight.size // 128

    sent = [tokens_in.reshape(ROWS, PAIRS, 2 * W), out_grad.reshape(ROWS, PAIRS, 2 * W)]
    blocks_out = [shape(LEN + S if direct else LEN, 2 * W)] * ROWS
    if direct:
        up = [v.reshape(flat, 128) for v in up]
        one = [shape(*CHUNK)]
        *pieces, first = run(
            opening_kernel,
            where,
            sent + [joint[0], output[0], down[0]],
            blocks_out + one,
            [
                pltpu.VMEM(sent[0].shape, BF16),
                pltpu.VMEM(sent[1].shape, BF16),
                pltpu.VMEM(joint[0].shape, F32),
                pltpu.VMEM(output[0].shape, F32),
                pltpu.VMEM(CROSS, F32),
                pltpu.SemaphoreType.DMA((5,)),
            ],
            limit=56,
            fetch=True,
        )
        tokens_pieces = exchange(pieces)
        first = gather_line(where, first, 1)
        first_pieces = gather_plane(where, first, tokens_pieces[1:])
        shard = run(second_shard_kernel, where, [up[0]], one, after=first[1:])[0]
        second = gather_line(where, shard, 2)
        plane = run(cross_kernel, where, tokens_pieces, [shape(ROWS, *CROSS)])[0]
        cross = gather_cross(where, plane)
        second_pieces = gather_plane(where, second)
        after = second_pieces[:1] + cross[:1]
        shard = run(third_shard_kernel, where, [down[0]], [shape(*PART)], after=after)[0]
        third = gather_line(where, shard, 2)
        third_pieces = gather_plane(where, third, first_pieces[3:])
        third_pieces += cross
    else:
        tokens_pieces = exchange(run(token_kernel, where, sent, blocks_out))
        lines = wide_lines(joint[0], output[0], up_weight[:, 0], down[0])
        cross = lines[2][:, 3 * S :]
        lines[2] = lines[2][:, : 3 * S]
        first_pieces, second_pieces, third_pieces = [
            gather_plane(where, list(line)) for line in lines
        ]
        cross = jnp.stack([cross] + [swap(cross, "row", m) for m in range(1, ROWS)], axis=1)
        third_pieces += list(cross.reshape(2, *PLANES.shape))

    vecs = vectors.reshape(72, 128)
    tokens, grads, wj, wo, mixed, probs, attended, part = run(
        attend_kernel,
        where,
        tokens_pieces + [vecs] + first_pieces,
        [
            shape(LEN, D),
            shape(LEN, D),
            shape(ROWS, MIX, W),
            shape(D, COLS),
            shape(MIX, LEN),
            shape(HEADS, LEN, LEN),
            shape(COLS, LEN),
            shape(LEN, D),
        ],
        [
            pltpu.VMEM((ROWS, LEN, 2 * W), BF16),
            pltpu.VMEM((MIX, LEN), F32),
            pltpu.VMEM((LEN, LEN), F32),
            pltpu.VMEM((8, MIX), F32),
        ],
    )
    hidden, hidden_low, normed, inverse, act, slope, wu = run(
        up_kernel,
        where,
        [tokens, part, swap(part, "col", 1), vecs] + second_pieces,
        [
            shape(LEN, D, dtype=F32),
            shape(LEN, D),
            shape(LEN, D, dtype=F32),
            shape(LEN, 1, dtype=F32),
            shape(LEN, FFC),
            shape(LEN, FFC, dtype=F32),
            shape(D, FFC),
        ],
        [pltpu.VMEM((LEN, FFC), F32)],
        after=third_pieces[6:],
    )
    wd, part = run(
        down_kernel, where, [act] + third_pieces, [shape(D, FFC), shape(LEN, D)]
    )
    out = run(
        second_norm_kernel,
        where,
        [hidden, part, swap(part, "col", 1), vecs, grads, act],
        [shape(LEN, D, dtype=F32), shape(LEN, D), shape(LEN, D, dtype=F32)]
        + [shape(8, D, dtype=F32)]
        + handed_shapes(PART)
        + [PLANES] * 2,
        [
            pltpu.VMEM((ROWS, QUADS) + PART, BF16),
            pltpu.VMEM((QUADS, ROWS) + CROSS, BF16),
        ],
    )
    (result, grad_low, grad_two, sums_two), third_handed, cross = out[:4], out[4:9], out[9:]
    third_got = scatter_first(third_handed)
    grad_pre, part, sums_up = run(
        hidden_back_kernel,
        where,
        [grad_low, slope, wd, wu],
        [shape(LEN, FFC), shape(LEN, D), shape(8, FFC, dtype=F32)],
        [pltpu.VMEM((LEN, FFC), F32)],
    )
    third_passed = scatter_pass(where, third_handed, third_got)
    second_handed = run(
        up_grad_kernel,
        where,
        [hidden_low, grad_pre],
        HANDED,
        [pltpu.VMEM((ROWS, QUADS) + CHUNK, BF16)],
    )
    grad_one, grad_mixed, vector, room = run(
        first_norm_kernel,
        where,
        [
            grad_two,
            part,
            swap(part, "col", 1),
            normed,
            inverse,
            vecs,
            wo,
            mixed,
            probs,
            attended,
            tokens,
            sums_two,
            sums_up,
        ],
        [shape(LEN, D, dtype=F32), shape(MIX, LEN), shape(*VECTOR, dtype=F32)]
        + [shape(ROWS, QUADS, *CHUNK)],
        [
            pltpu.VMEM((LEN, D), BF16),
            pltpu.VMEM((COLS, LEN), BF16),
            pltpu.VMEM((LEN, LEN), F32),
            pltpu.VMEM((LEN, LEN), BF16),
            pltpu.VMEM((8, D), F32),
        ],
        after=third_got,
    )
    cross_got = [swap(cross[1], "dp", 1)] if direct else []
    first_handed = run(
        first_hand_kernel,
        where,
        [room, vector] + third_passed,
        [shape(*FIRST_X), shape(*FIRST_Y)] + HANDED[2:],
        after=cross_got,
    )
    first_got = scatter_first(first_handed)

    def like(values):
        return [shape(*v.shape, dtype=F32) for v in values]

    def sums(dims, split):
        return [shape(*dims, dtype=F32), shape(*split)]

    if direct:
        plane = (ROWS,) + CROSS
        cross = run(cross_far_kernel, where, cross[:1] + cross_got, sums(plane, plane))
        cross_sum = [cross[0], swap(cross[1], "dp", 2)]
    else:
        cross_sum = []
    (part,) = run(
        token_back_kernel, where, [grad_mixed, wj], [shape(LEN, D)], after=first_handed[:1]
    )
    own = [shape(*CROSS, dtype=F32)] if direct else []
    pieces = run(
        token_sum_kernel,
        where,
        [result, grad_one, part, swap(part, "col", 1)] + cross_sum,
        blocks_out + own,
        [pltpu.VMEM((LEN, D), F32), pltpu.VMEM((ROWS, LEN, 2 * W), BF16)],
    )
    first_passed = run(
        carry_pass_kernel,
        where,
        first_handed[2:4] + first_handed[:1] + first_got,
        [PAIR, shape(*CARRIED)],
        after=pieces[:1],
    )
    first_last = scatter_second(first_passed)

    lines = [pltpu.VMEM((4,) + CHUNK, F32)]
    wide = [shape(4, *CHUNK, dtype=F32)]
    third_sum = run(
        near_line_kernel,
        where,
        third_handed[-1:] + third_got + first_got,
        sums((2,) + PART, (2,) + PART) if direct else [shape(4, *PART, dtype=F32)],
        [pltpu.VMEM((4,) + PART, F32)],
    )
    if direct:
        got = swap(third_sum[1], "dp", 1)
        third_sum = run(far_line_kernel, where, [third_sum[0], got], sums(PART, PART))
        third_sum[1] = swap(third_sum[1], "dp", 2)
        ready = third_sum[1:] + pieces[:1]
    else:
        ready = pieces[:1]
    second_got = scatter_first(second_handed)
    second_passed = scatter_pass(where, second_handed, second_got, ready)
    second_last = scatter_second(second_passed)
    first_sum = run(
        carry_near_kernel,
        where,
        first_handed[-1:] + first_got + first_last + first_passed[1:],
        sums((2 * W + VROWS, COLS), CARRIED) if direct else wide + [shape(*VECTOR, dtype=F32)],
        lines,
        after=second_passed,
    )
    second_sum = run(
        line_kernel,
        where,
        second_handed[-1:] + second_got + second_last,
        sums(CHUNK, CHUNK) + [shape(*CHUNK)] * 2 if direct else wide,
        lines,
    )
    if direct:
        got = swap(first_sum[1], "dp", 1)
        first_sum = run(
            carry_far_kernel,
            where,
            [first_sum[0], got],
            sums((W + VROWS, COLS), (W + 2 * VROWS, COLS)),
        )
        got = swap(first_sum[1], "dp", 2)
        state = joint + output
        new = run(
            first_adam_kernel,
            where,
            [first_sum[0], got] + state,
            like(state) + [shape(*VECTOR, dtype=F32)],
        )
        joint_new, output_new, vector = new[:3], new[3:6], new[6]

    flat_out = [shape(ROWS, 3 * PAIRS, 128, dtype=F32)] * 2
    got = exchange(pieces[:ROWS])
    out = run(token_out_kernel, where, got, flat_out)
    layer_out, tokens_grad = [v.reshape(tokens_in.shape) for v in out]

    def step_vectors(vector):
        state = [v.reshape(72, 128) for v in (vectors, vector_first, vector_second)]
        new = run(
            vector_adam_kernel,
            where,
            [vector, swap(vector, "col", 1)] + state,
            like(state),
            [pltpu.VMEM((72, 128), F32)],
        )
        return [v.reshape(vectors.shape) for v in new]

    if direct:
        down_new = run(
            down_adam_kernel, where, third_sum + pieces[ROWS:] + got[1:] + down, like(down)
        )
        vector_new = step_vectors(vector)
        got = [swap(v, "dp", mask) for v, mask in zip(second_sum[1:], ORDER[1:])]
        after = out[:1] + vector_new[:1] + down_new[:1]
        up_new = run(up_adam_kernel, where, second_sum[:1] + got + up, like(up), after=after)
        up_new = [v.reshape(up_weight.shape) for v in up_new]
    else:
        kept, sent = [v.reshape(2, ROWS, *CROSS) for v in cross]
        cross = jnp.stack([kept, sent], axis=1).reshape(QUADS, ROWS, *CROSS)
        cross = lax.psum_scatter(cross.astype(F32), "row", scatter_dimension=1)
        third = jnp.concatenate([third_sum[0], cross], axis=1)
        grads = wide_sums(first_sum[0], second_sum[0], third)
        joint_new = adamw(*joint, grads[0], JOINT_RATE, DECAY)
        output_new = adamw(*output, grads[1], OUTPUT_RATE, DECAY)
        up_new = adamw(*up, grads[2][:, None], JOINT_RATE, DECAY)
        down_new = adamw(*down, grads[3], DOWN_RATE, DECAY)
        vector_new = step_vectors(lax.psum(first_sum[1], "dp"))

    return (
        layer_out,
        tokens_grad,
        *[jnp.transpose(v, (2, 0, 1)) for v in joint_new],
        *[v.T[:, None] for v in output_new],
        *up_new,
        *[v.T[:, None] for v in down_new],
        *vector_new,
    )


def solution(mesh):
    first = P("row", "col", "dp")
    second = P("col", "row", "dp")
    tokens = P("dp", "row", None)
    weights = (first,) * 3 + (second,) * 3 + (first,) * 3 + (second,) * 3 + (P(),) * 3
    in_specs = (tokens, P(("dp", "row"))) + weights + (tokens,)
    out_specs = (tokens, tokens) + weights
    return jax.shard_map(
        per_device, mesh=mesh, in_specs=in_specs, out_specs=out_specs, check_vma=False
    )
```

```python
from functools import partial

import jax
import jax.numpy as jnp
from jax import lax
from jax.experimental import pallas as pl
from jax.experimental.pallas import tpu as pltpu
from jax.sharding import PartitionSpec as P

D = 768
H = 12
HD = 64
FF = 3072
LEN = 256
STEP = 10

NORM_EPS = 1e-12
BETA_ONE = 0.9
BETA_TWO = 0.999
ADAM_EPS = 1e-08
DECAY = 0.01
VECTOR_RATE = 0.2

F32 = jnp.float32
BF16 = jnp.bfloat16

ROWS = 4
QUADS = 4
W = D // ROWS
S = W // QUADS
COLS = D // 2
HEADS = COLS // HD
FFC = FF // 2
MIX = HEADS * 3 * HD
PAIRS = LEN // 2
CHUNK = (W, COLS)
PART = (3 * S, COLS)
CROSS = (S, COLS)
MIB = 1024 * 1024


def swap(value, axis, mask):
    n = lax.axis_size(axis)
    return lax.ppermute(value, axis, [(i, i ^ mask) for i in range(n)])


def shape(*dims, dtype=BF16):
    return jax.ShapeDtypeStruct(dims, dtype)


def run(kernel, where, args, outs, scratch=(), limit=8, after=(), fetch=False):
    vmem = pl.BlockSpec(memory_space=pltpu.VMEM)
    first, late = 1 + len(args), len(after)

    def body(*refs):
        kernel(*refs[:first], *refs[first + late :])

    out = pl.pallas_call(
        body,
        out_shape=outs,
        in_specs=[pl.BlockSpec(memory_space=pltpu.SMEM)]
        + [pl.BlockSpec(memory_space=pl.ANY) if fetch else vmem] * len(args)
        + [pl.BlockSpec(memory_space=pl.ANY)] * late,
        out_specs=[vmem] * len(outs),
        scratch_shapes=list(scratch),
        compiler_params=pltpu.CompilerParams(vmem_limit_bytes=limit * MIB),
    )(where, *args, *after)
    return list(out)


def dot(left, right, dims):
    return lax.dot_general(left, right, (dims, ((), ())), preferred_element_type=F32)


NN = ((1,), (0,))
NT = ((1,), (1,))
TN = ((0,), (0,))


def each(count, body):
    def step(i, carry):
        body(i)
        return carry

    lax.fori_loop(0, count, step, 0)


def row_of(vecs, start, count):
    return jnp.concatenate([vecs[start + i : start + i + 1, :] for i in range(count)], axis=1)


def vector_row(vecs, k):
    return row_of(vecs, 6 * k, 6)


def pick_col(where, left, right):
    return jnp.where(where[2] == 0, left, right)


def split_parts(value):
    high = value.astype(BF16)
    return high, (value - high.astype(F32)).astype(BF16)


def opening_kernel(where, tokens, grads, joint, output, down, *refs):
    outs, first = refs[:ROWS], refs[ROWS]
    tokens_in, grads_in, joint_in, output_in, down_in, done = refs[ROWS + 1 :]
    copies = [
        pltpu.make_async_copy(source, target, done.at[i])
        for i, (source, target) in enumerate(
            [
                (joint, joint_in),
                (output, output_in),
                (tokens, tokens_in),
                (grads, grads_in),
                (down.at[:, 3 * COLS :], down_in),
            ]
        )
    ]
    for copy in copies:
        copy.start()
    copies[0].wait()
    copies[1].wait()
    for h in range(HEADS // 2):
        pair = [joint_in[h].astype(BF16), joint_in[h + HEADS // 2].astype(BF16)]
        first[h * S : (h + 1) * S, :] = jnp.concatenate(pair, axis=1)
    first[HEADS // 2 * S :, :] = output_in[...].astype(BF16)
    copies[2].wait()
    copies[3].wait()
    copies[4].wait()
    for m, out in enumerate(outs):
        out[0:PAIRS, :] = tokens_in[where[0] ^ m]
        out[PAIRS:LEN, :] = grads_in[where[0] ^ m]
        out[LEN:, :] = down_in[...].astype(BF16)


def second_shard_kernel(where, up, second):
    for q in range(3):
        second[:, q * 128 : (q + 1) * 128] = up[pl.ds(q, W, stride=3), :].astype(BF16)


def third_shard_kernel(where, down, third):
    for q in range(3):
        third[q * S : (q + 1) * S, :] = down[:, q * COLS : (q + 1) * COLS].astype(BF16)


def pair_kernel(where, b0, b1, pair):
    pair[0] = b0[...]
    pair[1] = b1[...]


def cross_kernel(where, t0, t1, t2, t3, plane):
    for m, piece in enumerate([t0, t1, t2, t3]):
        plane[m] = piece[LEN:, :]


def planes_kernel(where, b0, b1, planes):
    planes[0:ROWS] = b0[...]
    planes[ROWS:] = b1[...]


def whole_kernel(where, *refs):
    *pieces, line = refs
    for k in range(QUADS):
        line[k] = pieces[k][...] if len(pieces) == QUADS else pieces[k // 2][k % 2]


def halves_kernel(where, from_x, from_y, near_y, far_x):
    near_y[...] = from_y[0:2]
    far_x[...] = from_x[2:4]


def token_kernel(where, tokens, grads, *outs):
    for m, out in enumerate(outs):
        out[0:PAIRS, :] = tokens[where[0] ^ m]
        out[PAIRS:LEN, :] = grads[where[0] ^ m]


ORDER = (0, 2, 1, 3)


def blocks(where, pieces):
    found = [(piece, i) for piece in pieces for i in range(piece.shape[0])]
    for at, (piece, i) in enumerate(found):
        yield where[0] ^ (at // QUADS), where[1] ^ ORDER[at % QUADS], piece[i]


def cross_blocks(where, pieces):
    for j, piece in enumerate(pieces):
        for i in range(2 * ROWS):
            yield where[0] ^ (i % ROWS), where[1] ^ ORDER[2 * j + i // ROWS], piece[i]


def unpack_tokens(x):
    parts = [jnp.concatenate([x[r][:, :W], x[r][:, W:]], axis=0) for r in range(ROWS)]
    return jnp.concatenate(parts, axis=1)


def pack_tokens(value, room, k):
    for r in range(ROWS):
        both = value[:, r * W : (r + 1) * W]
        packed = jnp.concatenate([both[:PAIRS], both[PAIRS:]], axis=1).astype(BF16)
        room[r, k * PAIRS : (k + 1) * PAIRS, :] = packed


def attend_kernel(where, t0, t1, t2, t3, vecs, *refs):
    pieces, refs = refs[:5], refs[5:]
    tokens, grads, wj, wo, mixed, probs, attended, part, room, mixing, scores, parts = refs
    for m, piece in enumerate([t0, t1, t2, t3]):
        room[where[0] ^ m] = piece[0:LEN, :]
    tokens[...] = unpack_tokens([room[r, 0:PAIRS, :] for r in range(ROWS)])
    grads[...] = unpack_tokens([room[r, PAIRS:, :] for r in range(ROWS)])
    half = HEADS // 2
    for row, quad, value in blocks(where, pieces):
        for h in range(half):
            rows = value[h * S : (h + 1) * S, :]
            for k, cut in enumerate([rows[:, :W], rows[:, W:]]):
                start = pl.multiple_of((h + k * half) * 3 * HD + quad * S, 16)
                wj[row, pl.ds(start, S), :] = cut
        start = pl.multiple_of(row * W + quad * S, 16)
        wo[pl.ds(start, S), :] = value[half * S :, :]
    total = dot(wj[0], tokens[:, :W], NT)
    for r in range(1, ROWS):
        total = total + dot(wj[r], tokens[:, r * W : (r + 1) * W], NT)
    mixing[...] = total
    query_bias, value_bias = [
        pick_col(where, row_of(vecs, start, 3), row_of(vecs, start + 3, 3)) for start in (0, 6)
    ]
    zero = jnp.zeros((1, HD), F32)
    row = []
    for h in range(HEADS):
        at = slice(h * HD, (h + 1) * HD)
        row += [query_bias[:, at], zero, value_bias[:, at]]
    row = jnp.concatenate(row, axis=1)
    high, low = split_parts(row)
    rest = (row - high.astype(F32) - low.astype(F32)).astype(BF16)
    parts[...] = jnp.zeros_like(parts)
    parts[0:1, :] = high.astype(F32)
    parts[1:2, :] = low.astype(F32)
    parts[2:3, :] = rest.astype(F32)
    bias = dot(parts[...].astype(BF16), jnp.ones((8, LEN), BF16), TN)
    mixed[...] = (mixing[...] + bias).astype(BF16)
    slot = lax.broadcasted_iota(jnp.int32, (LEN, 1), 0)
    slot = jnp.where(slot < PAIRS, 2 * slot, 2 * (slot - PAIRS) + 1)
    valid = slot < where[3]
    for h in range(HEADS):
        base = h * 3 * HD
        query, keyed, valued = [mixed[base + k * HD : base + (k + 1) * HD, :] for k in range(3)]
        scores[...] = dot(keyed, query, TN)
        for q in range(2):
            at = slice(q * 128, (q + 1) * 128)
            score = jnp.where(valid, scores[:, at] * 0.125, -1e30)
            expo = jnp.exp(score - jnp.max(score, axis=0, keepdims=True))
            prob = expo * (1.0 / jnp.sum(expo, axis=0, keepdims=True))
            probs[h, :, at] = prob.astype(BF16)
        attended[h * HD : (h + 1) * HD, :] = dot(valued, probs[h], NN).astype(BF16)
    part[...] = dot(attended[...], wo[...], ((0,), (1,))).astype(BF16)


def norm_rows(resid, gain, shift_by):
    mean = jnp.sum(resid, axis=1, keepdims=True) * (1.0 / D)
    var = jnp.sum(resid * resid, axis=1, keepdims=True) * (1.0 / D) - mean * mean
    inverse = lax.rsqrt(var + NORM_EPS)
    normed = (resid - mean) * inverse
    return normed * gain + shift_by, normed, inverse


def norm_back_rows(grad, normed, inverse, gain):
    scaled = grad * gain
    total = jnp.sum(scaled, axis=1, keepdims=True) * (1.0 / D)
    cross = jnp.sum(scaled * normed, axis=1, keepdims=True) * (1.0 / D)
    return (scaled - total - normed * cross) * inverse


STRIP = 32


def strip(i):
    return pl.ds(pl.multiple_of(i * STRIP, STRIP), STRIP)


def up_kernel(where, tokens, p0, p1, vecs, *refs):
    pieces, refs = refs[:5], refs[5:]
    hidden, low, normed, inverse, act, slope, wu, pre = refs
    for row, quad, value in blocks(where, pieces):
        rows = pl.ds(pl.multiple_of(row * W, W), W)
        wu[rows, pl.ds(pl.multiple_of(quad * COLS, COLS), COLS)] = value

    bias_out, gain, shift_by = [vector_row(vecs, k) for k in (2, 3, 4)]

    def first(i):
        at = strip(i)
        resid = tokens[at, :].astype(F32) + (p0[at, :].astype(F32) + p1[at, :].astype(F32))
        out, unit, scale = norm_rows(resid + bias_out, gain, shift_by)
        hidden[at, :] = out
        low[at, :] = out.astype(BF16)
        normed[at, :] = unit
        inverse[at, :] = scale

    each(LEN // STRIP, first)
    pre[...] = dot(low[...], wu[...], NN)
    bias = pick_col(where, row_of(vecs, 48, 12), row_of(vecs, 60, 12))
    for q in range(4):
        cols = slice(q * COLS, (q + 1) * COLS)
        shift_up = bias[:, cols]

        def second(i, cols=cols, shift_up=shift_up):
            at = (strip(i), cols)
            value = pre[at] + shift_up
            phi = 0.5 * (1.0 + lax.erf(value * (0.5**0.5)))
            density = jnp.exp(-0.5 * value * value) * 0.3989422804014327
            act[at] = (value * phi).astype(BF16)
            slope[at] = phi + value * density

        each(LEN // STRIP, second)


def down_kernel(where, act, *refs):
    pieces, cross, wd, part = refs[:5], refs[5:7], refs[7], refs[8]
    for row, quad, value in blocks(where, pieces):
        rows = pl.ds(pl.multiple_of(row * W + quad * S, 16), S)
        for q in range(3):
            wd[rows, q * COLS : (q + 1) * COLS] = value[q * S : (q + 1) * S, :]
    for row, quad, value in cross_blocks(where, cross):
        rows = pl.ds(pl.multiple_of(row * W + quad * S, 16), S)
        wd[rows, 3 * COLS :] = value
    part[...] = dot(act[...], wd[...], NT).astype(BF16)


def hand_out(where, room, outs):
    r = where[0]
    to_x, to_y, last_x, last_y, own = outs
    to_x[0:2] = room[r ^ 3, 0:2]
    to_x[2:4] = room[r ^ 1, 0:2]
    to_y[0:2] = room[r ^ 3, 2:4]
    to_y[2:4] = room[r ^ 2, 2:4]
    last_x[...] = room[r ^ 1, 2:4]
    last_y[...] = room[r ^ 2, 0:2]
    own[...] = room[r]


def handed_shapes(block):
    pair, line = shape(2, *block), shape(4, *block)
    return [line] * 2 + [pair] * 2 + [line]


HANDED = handed_shapes(CHUNK)
PAIR = shape(2, *CHUNK)
PLANES = shape(2 * ROWS, *CROSS)

VROWS = 32
VECTOR = (VROWS, COLS)
CARRIED = (2 * W + 2 * VROWS, COLS)

LATE_X = 4 * W + 2 * VROWS
LATE_Y = 4 * W
FIRST_X = (LATE_X + 2 * PART[0], COLS)
FIRST_Y = (LATE_Y + 2 * PART[0], COLS)


def put_vector(out, start, value):
    high, low = split_parts(value)
    out[start : start + VROWS, :] = high
    out[start + VROWS : start + 2 * VROWS, :] = low


def get_vector(value, start):
    high = value[start : start + VROWS, :].astype(F32)
    return high + value[start + VROWS : start + 2 * VROWS, :].astype(F32)


def second_norm_kernel(where, hidden, p0, p1, vecs, grads, act, *refs):
    (result, low, grad_two, sums), handed = refs[:4], refs[4:9]
    cross_own, cross_send, room, cross = refs[9:]
    sums[...] = jnp.zeros_like(sums)
    bias_down, gain, shift_by = [vector_row(vecs, k) for k in (5, 6, 7)]

    def body(i):
        at = strip(i)
        resid = hidden[at, :] + (p0[at, :].astype(F32) + p1[at, :].astype(F32)) + bias_down
        out, unit, scale = norm_rows(resid, gain, shift_by)
        result[at, :] = out
        grad = grads[at, :].astype(F32)
        back = norm_back_rows(grad, unit, scale, gain)
        grad_two[at, :] = back
        rounded = back.astype(BF16)
        low[at, :] = rounded
        sums[0:1, :] += jnp.sum(rounded.astype(F32), axis=0, keepdims=True)
        sums[1:2, :] += jnp.sum(grad * unit, axis=0, keepdims=True)
        sums[2:3, :] += jnp.sum(grad, axis=0, keepdims=True)

    each(LEN // STRIP, body)
    for q in range(4):
        cols = slice(q * COLS, (q + 1) * COLS)
        grad = dot(low[...], act[:, cols], TN).astype(BF16)
        for r in range(ROWS):
            for z in range(QUADS):
                start = r * W + z * S
                if q < 3:
                    room[r, z, q * S : (q + 1) * S, :] = grad[start : start + S, :]
                else:
                    cross[z, r] = grad[start : start + S, :]
    hand_out(where, room, handed)
    for k, mask in enumerate([0, 2]):
        rows = slice(k * ROWS, (k + 1) * ROWS)
        cross_own[rows] = cross[where[1] ^ mask]
        cross_send[rows] = cross[where[1] ^ mask ^ 1]


def hidden_back_kernel(where, low, slope, wd, wu, grad_pre, part, sums, back):
    back[...] = dot(low[...], wd[...], NN)
    sums[...] = jnp.zeros_like(sums)
    for q in range(4):
        cols = slice(q * COLS, (q + 1) * COLS)

        def body(i, cols=cols):
            at = (strip(i), cols)
            value = (back[at] * slope[at]).astype(BF16)
            grad_pre[at] = value
            sums[0:1, cols] += jnp.sum(value.astype(F32), axis=0, keepdims=True)

        each(LEN // STRIP, body)
    part[...] = dot(grad_pre[...], wu[...], NT).astype(BF16)


def up_grad_kernel(where, low, grad_pre, *refs):
    handed, room = refs[:5], refs[5]
    for z in range(QUADS):
        grad = dot(low[...], grad_pre[:, z * COLS : (z + 1) * COLS], TN).astype(BF16)
        for r in range(ROWS):
            room[r, z] = grad[r * W : (r + 1) * W, :]
    hand_out(where, room, handed)


def first_norm_kernel(
    where, grad_two, p0, p1, normed, inverse, vecs, wo, mixed, probs, *refs
):
    grad_one, grad_mixed, low, sums, back, inner, scores = refs
    sums[...] = jnp.zeros_like(sums)
    gain = vector_row(vecs, 3)

    def body(i):
        at = strip(i)
        grad = grad_two[at, :] + (p0[at, :].astype(F32) + p1[at, :].astype(F32))
        unit = normed[at, :]
        out = norm_back_rows(grad, unit, inverse[at, :], gain)
        grad_one[at, :] = out
        rounded = out.astype(BF16)
        low[at, :] = rounded
        sums[0:1, :] += jnp.sum(rounded.astype(F32), axis=0, keepdims=True)
        sums[1:2, :] += jnp.sum(grad * unit, axis=0, keepdims=True)
        sums[2:3, :] += jnp.sum(grad, axis=0, keepdims=True)

    each(LEN // STRIP, body)
    back[...] = dot(wo[...], low[...], ((0,), (1,))).astype(BF16)
    for h in range(HEADS):
        base = h * 3 * HD
        query, keyed, valued = [mixed[base + k * HD : base + (k + 1) * HD, :] for k in range(3)]
        grad_out = back[h * HD : (h + 1) * HD, :]
        inner[...] = dot(valued, grad_out, TN)
        for q in range(2):
            at = slice(q * 128, (q + 1) * 128)
            prob = probs[h, :, at].astype(F32)
            grad = inner[:, at]
            mean = jnp.sum(grad * prob, axis=0, keepdims=True)
            scores[:, at] = (prob * (grad - mean)).astype(BF16)
        grads = [
            dot(keyed, scores[...], NN) * 0.125,
            dot(query, scores[...], NT) * 0.125,
            dot(grad_out, probs[h], NT),
        ]
        for k, grad in enumerate(grads):
            grad_mixed[base + k * HD : base + (k + 1) * HD, :] = grad.astype(BF16)


def first_grad_kernel(where, grad_mixed, low, sums, attended, tokens, sums_two, sums_up, *refs):
    vector, room = refs
    half = HEADS // 2
    for r in range(ROWS):
        cut = tokens[:, r * W : (r + 1) * W]
        grad = dot(grad_mixed[...], cut, NN).astype(BF16)
        for z in range(QUADS):
            for h in range(half):
                starts = [(h + k * half) * 3 * HD + z * S for k in range(2)]
                pair = [grad[start : start + S, :] for start in starts]
                room[r, z, h * S : (h + 1) * S, :] = jnp.concatenate(pair, axis=1)
        grad = dot(low[:, r * W : (r + 1) * W], attended[...], ((0,), (1,))).astype(BF16)
        for z in range(QUADS):
            room[r, z, half * S :, :] = grad[z * S : (z + 1) * S, :]
    left = jnp.where(where[2] == 0, 1.0, 0.0)
    right = 1.0 - left
    total = dot(jnp.ones((8, LEN), BF16), grad_mixed[...], NT)[0:1, :]
    vector[...] = jnp.zeros_like(vector)
    for k, start in enumerate([0, 2 * HD]):
        at = [h * 3 * HD + start for h in range(HEADS)]
        row = jnp.concatenate([total[:, i : i + HD] for i in at], axis=1)
        vector[2 * k : 2 * k + 1, :] = row * left
        vector[2 * k + 1 : 2 * k + 2, :] = row * right
    for k, found in enumerate([sums, sums_two]):
        for i in range(3):
            for j in range(2):
                row = 4 + 6 * k + 2 * i + j
                vector[row : row + 1, :] = found[i : i + 1, j * COLS : (j + 1) * COLS] * left
    for j in range(4):
        row = sums_up[0:1, j * COLS : (j + 1) * COLS]
        vector[16 + j : 17 + j, :] = row * left
        vector[20 + j : 21 + j, :] = row * right


def first_hand_kernel(where, room, vector, late_x, late_y, to_x, to_y, last_x, last_y, own):
    r = where[0]
    for k in range(2):
        far, near = slice(k * W, (k + 1) * W), slice((2 + k) * W, (3 + k) * W)
        to_x[far, :] = room[r ^ 3, k]
        to_x[near, :] = room[r ^ 1, k]
        to_y[far, :] = room[r ^ 3, 2 + k]
        to_y[near, :] = room[r ^ 2, 2 + k]
        for start, out, late in [(LATE_X, to_x, late_x), (LATE_Y, to_y, late_y)]:
            at = start + k * PART[0]
            out[at : at + PART[0], :] = late[k]
    last_x[...] = room[r ^ 1, 2:4]
    last_y[...] = room[r ^ 2, 0:2]
    own[...] = room[r]
    put_vector(to_x, 4 * W, vector[...])


def token_back_kernel(where, grad_mixed, wj, part):
    for r in range(ROWS):
        part[:, r * W : (r + 1) * W] = dot(grad_mixed[...], wj[r], TN).astype(BF16)


def token_sum_kernel(where, result, grad_one, p0, p1, *refs):
    total, room = refs[-2:]
    cross = [*refs[:2], refs[6]] if len(refs) > 6 else []
    outs = refs[2:6] if cross else refs[:4]

    def body(i):
        at = strip(i)
        total[at, :] = grad_one[at, :] + (p0[at, :].astype(F32) + p1[at, :].astype(F32))

    each(LEN // STRIP, body)
    pack_tokens(result, room, 0)
    pack_tokens(total, room, 1)
    for m, out in enumerate(outs):
        row = where[0] ^ m
        out[0:LEN, :] = room[row]
        if cross:
            kept, got, own = cross
            sums = kept[row] + got[row].astype(F32)
            out[LEN:, :] = sums.astype(BF16)
            if m == 0:
                own[...] = sums


def token_out_kernel(where, t0, t1, t2, t3, result, total):
    for m, piece in enumerate([t0, t1, t2, t3]):
        for k, out in enumerate([result, total]):
            for q in range(3):
                value = piece[k * PAIRS : (k + 1) * PAIRS, q * 128 : (q + 1) * 128].astype(F32)
                out[where[0] ^ m, pl.ds(q, PAIRS, stride=3), :] = value


def pass_kernel(where, last_x, last_y, from_x, from_y, to_x, to_y):
    to_x[...] = (last_x[...].astype(F32) + from_y[0:2].astype(F32)).astype(BF16)
    to_y[...] = (last_y[...].astype(F32) + from_x[0:2].astype(F32)).astype(BF16)


def carry_pass_kernel(where, last_x, last_y, carried, from_x, from_y, to_x, to_y):
    for k in range(2):
        rows = slice(k * W, (k + 1) * W)
        to_x[k] = (last_x[k].astype(F32) + from_y[rows, :].astype(F32)).astype(BF16)
        to_y[rows, :] = (last_y[k].astype(F32) + from_x[rows, :].astype(F32)).astype(BF16)
    put_vector(to_y, 2 * W, get_vector(carried, 4 * W) + get_vector(from_x, 4 * W))


def add_plane(own, from_x, from_y, last_x, last_y, room):
    for k in range(2):
        room[k] = (own[k].astype(F32) + from_x(k)) + last_y(k)
        room[2 + k] = (own[2 + k].astype(F32) + from_y(k)) + last_x(k)


def kept_blocks(ref):
    skip = ref.shape[0] - 2
    return lambda k: ref[skip + k].astype(F32)


def kept_rows(ref, start, rows=W):
    return lambda k: ref[start + k * rows : start + (k + 1) * rows, :].astype(F32)


def line_kernel(where, own, from_x, from_y, last_x, last_y, kept, *refs):
    *sends, room = refs
    add_plane(own, *[kept_blocks(v) for v in (from_x, from_y, last_x, last_y)], room)
    if sends:
        kept[...] = room[where[1]]
        for mask, send in zip(ORDER[1:], sends):
            send[...] = room[where[1] ^ mask].astype(BF16)
    else:
        kept[...] = room[...]


def near_line_kernel(where, own, from_x, from_y, late_x, late_y, kept, *refs):
    *sends, room = refs
    late = [kept_rows(late_x, LATE_X, PART[0]), kept_rows(late_y, LATE_Y, PART[0])]
    add_plane(own, kept_blocks(from_x), kept_blocks(from_y), *late, room)
    if sends:
        for k, mask in enumerate([0, 2]):
            kept[k] = room[where[1] ^ mask]
            sends[0][k] = room[where[1] ^ mask ^ 1].astype(BF16)
    else:
        kept[...] = room[...]


def far_line_kernel(where, kept, got, total, send):
    total[...] = kept[0] + got[0].astype(F32)
    send[...] = (kept[1] + got[1].astype(F32)).astype(BF16)


def cross_far_kernel(where, own, got, kept, send):
    kept[...] = own[0:ROWS].astype(F32) + got[0:ROWS].astype(F32)
    send[...] = (own[ROWS:].astype(F32) + got[ROWS:].astype(F32)).astype(BF16)


def carry_near_kernel(where, own, first_x, first_y, last_x, from_y, passed, kept, *refs):
    *sends, room = refs
    near = [kept_rows(first_x, 2 * W), kept_rows(first_y, 2 * W)]
    add_plane(own, *near, kept_blocks(last_x), kept_rows(from_y, 0), room)
    vector = get_vector(passed, 2 * W) + get_vector(from_y, 2 * W)
    if kept.ndim == 2:
        for k, mask in enumerate([0, 2]):
            rows = slice(k * W, (k + 1) * W)
            kept[rows, :] = room[where[1] ^ mask]
            sends[0][rows, :] = room[where[1] ^ mask ^ 1].astype(BF16)
        kept[2 * W :, :] = vector
        put_vector(sends[0], 2 * W, vector)
    else:
        kept[...] = room[...]
        sends[0][...] = vector


def add_vector(own, got, start):
    high, low = split_parts(own)
    return (high.astype(F32) + low.astype(F32)) + get_vector(got, start)


def carry_far_kernel(where, kept, got, total, send):
    total[0:W, :] = kept[0:W, :] + got[0:W, :].astype(F32)
    send[0:W, :] = (kept[W : 2 * W, :] + got[W : 2 * W, :].astype(F32)).astype(BF16)
    vector = add_vector(kept[2 * W :, :], got, 2 * W)
    total[W:, :] = vector
    put_vector(send, W, vector)


def adamw(weight, first, second, grad, rate, decay):
    first_new = BETA_ONE * first + (1.0 - BETA_ONE) * grad
    second_new = BETA_TWO * second + (1.0 - BETA_TWO) * grad * grad
    fix_one = 1.0 - BETA_ONE**STEP
    fix_two = 1.0 - BETA_TWO**STEP
    update = first_new / fix_one / (jnp.sqrt(second_new / fix_two) + ADAM_EPS) + decay * weight
    return (first_new, second_new, weight - rate * update)


JOINT_RATE = D ** (-0.5)
OUTPUT_RATE = (4 * D // LEN) ** (-0.5)
DOWN_RATE = FF ** (-0.5)


def first_adam_kernel(where, kept, got, jw, jf, js, ow, of, os, *refs):
    outs, vector = refs[:6], refs[6]
    grad = kept[0:W, :] + got[0:W, :].astype(F32)
    half = HEADS // 2
    for h in range(HEADS):
        rows = grad[h % half * S : (h % half + 1) * S, :]
        cut = rows[:, :W] if h < half else rows[:, W:]
        new = adamw(jw[h], jf[h], js[h], cut, JOINT_RATE, DECAY)
        for out, value in zip(outs[:3], new):
            out[h] = value
    new = adamw(ow[...], of[...], os[...], grad[half * S :, :], OUTPUT_RATE, DECAY)
    for out, value in zip(outs[3:], new):
        out[...] = value
    vector[...] = add_vector(kept[W:, :], got, W)


def vector_adam_kernel(where, mine, other, weight, first, second, *refs):
    outs, grad = refs[:3], refs[3]
    total = mine[...] + other[...]
    for q in range(3):
        grad[pl.ds(q, 24, stride=3), :] = total[0:24, q * 128 : (q + 1) * 128]
    new = adamw(weight[...], first[...], second[...], grad[...], VECTOR_RATE, 0.0)
    for out, value in zip(outs, new):
        out[...] = value


def up_adam_kernel(where, kept, r2, r1, r3, w, f, s, *outs):
    grad = (kept[...] + r1[...].astype(F32)) + (r2[...].astype(F32) + r3[...].astype(F32))
    for q in range(3):
        at = (pl.ds(q, W, stride=3), slice(None))
        cut = grad[:, q * 128 : (q + 1) * 128]
        for out, value in zip(outs, adamw(w[at], f[at], s[at], cut, JOINT_RATE, DECAY)):
            out[at] = value


def down_adam_kernel(where, kept, got, own, r1, r2, r3, w, f, s, *outs):
    far = r2[LEN:, :].astype(F32) + r3[LEN:, :].astype(F32)
    cross = (own[...] + r1[LEN:, :].astype(F32)) + far
    most = kept[...] + got[...].astype(F32)
    for q in range(4):
        at = (slice(None), slice(q * COLS, (q + 1) * COLS))
        cut = most[q * S : (q + 1) * S, :] if q < 3 else cross
        for out, value in zip(outs, adamw(w[at], f[at], s[at], cut, DOWN_RATE, DECAY)):
            out[at] = value


def gather_line(where, shard, steps):
    if steps == 1:
        return [shard] + [swap(shard, "dp", mask) for mask in ORDER[1:]]
    pair = [shape(2, *shard.shape)]
    pair = run(pair_kernel, where, [shard, swap(shard, "dp", 2)], pair)[0]
    return [pair, swap(pair, "dp", 1)]


def gather_plane(where, line, after=()):
    block = line[0].shape[-2:]
    line = run(whole_kernel, where, line, [shape(4, *block)], after=after)[0]
    from_x = swap(line, "row", 1)
    from_y = swap(line, "row", 2)
    near_y, far_x = run(halves_kernel, where, [from_x, from_y], [shape(2, *block)] * 2)
    return [line, from_x, from_y, swap(near_y, "row", 1), swap(far_x, "row", 2)]


def gather_cross(where, plane):
    planes = run(planes_kernel, where, [plane, swap(plane, "dp", 2)], [PLANES])[0]
    return [planes, swap(planes, "dp", 1)]


def scatter_first(handed):
    return [swap(value, "row", 1 + i % 2) for i, value in enumerate(handed[:-3])]


def scatter_pass(where, handed, got, after=()):
    pair = [shape(*handed[2].shape)] * 2
    return run(pass_kernel, where, handed[2:4] + got, pair, after=after)


def scatter_second(passed):
    return [swap(passed[0], "row", 1), swap(passed[1], "row", 2)]


def exchange(pieces):
    return [pieces[0]] + [swap(pieces[m], "row", m) for m in range(1, ROWS)]


def wide_lines(joint, output, up, down):
    order = jnp.array(ORDER)
    n = lax.axis_size("dp") // QUADS

    def collect(shard, axis):
        whole = lax.all_gather(shard.astype(BF16), "dp", axis=axis, tiled=True)
        return jnp.stack(jnp.split(whole, QUADS, axis=axis))

    joint = collect(joint, 1)
    half = HEADS // 2
    pair = joint.reshape(QUADS, 2, half, S, W)
    pair = jnp.transpose(pair, (0, 2, 3, 1, 4)).reshape(QUADS, half * S, 2 * W)
    first = jnp.concatenate([pair, collect(output, 0)], axis=1)
    second = collect(up, 1)
    third = collect(down, 0).reshape(QUADS, S, 4, COLS)
    third = jnp.transpose(third, (0, 2, 1, 3)).reshape(QUADS, W, COLS)
    return [jnp.take(value, order, axis=0) for value in (first, second, third)]


def wide_sums(first, second, third):
    def give(value, axis):
        whole = jnp.concatenate(list(value), axis=axis)
        return lax.psum_scatter(whole, "dp", scatter_dimension=axis, tiled=True)

    half = HEADS // 2
    pair = first[:, : half * S].reshape(QUADS, half, S, 2, W)
    joint = jnp.transpose(pair, (0, 3, 1, 2, 4)).reshape(QUADS, HEADS, S, W)
    third = jnp.transpose(third.reshape(QUADS, 4, S, COLS), (0, 2, 1, 3))
    third = third.reshape(QUADS, S, FFC)
    return give(joint, 1), give(first[:, half * S :], 0), give(second, 1), give(third, 0)


def per_device(
    tokens_in,
    lengths,
    joint_weight,
    joint_first,
    joint_second,
    output_weight,
    output_first,
    output_second,
    up_weight,
    up_first,
    up_second,
    down_weight,
    down_first,
    down_second,
    vectors,
    vector_first,
    vector_second,
    out_grad,
):
    r = lax.axis_index("row")
    col = lax.axis_index("col")
    direct = lax.axis_size("dp") == QUADS
    z = lax.axis_index("dp") if direct else jnp.int32(0)
    where = jnp.stack([r, z, col, lengths[0]]).astype(jnp.int32)

    joint = [jnp.transpose(v, (1, 2, 0)) for v in (joint_weight, joint_first, joint_second)]
    output = [v[:, 0].T for v in (output_weight, output_first, output_second)]
    down = [v[:, 0].T for v in (down_weight, down_first, down_second)]
    up = [up_weight, up_first, up_second]
    flat = up_weight.size // 128

    sent = [tokens_in.reshape(ROWS, PAIRS, 2 * W), out_grad.reshape(ROWS, PAIRS, 2 * W)]
    blocks_out = [shape(LEN + S if direct else LEN, 2 * W)] * ROWS
    if direct:
        up = [v.reshape(flat, 128) for v in up]
        one = [shape(*CHUNK)]
        *pieces, first = run(
            opening_kernel,
            where,
            sent + [joint[0], output[0], down[0]],
            blocks_out + one,
            [
                pltpu.VMEM(sent[0].shape, BF16),
                pltpu.VMEM(sent[1].shape, BF16),
                pltpu.VMEM(joint[0].shape, F32),
                pltpu.VMEM(output[0].shape, F32),
                pltpu.VMEM(CROSS, F32),
                pltpu.SemaphoreType.DMA((5,)),
            ],
            limit=56,
            fetch=True,
        )
        tokens_pieces = exchange(pieces)
        first = gather_line(where, first, 1)
        first_pieces = gather_plane(where, first, tokens_pieces[1:])
        shard = run(second_shard_kernel, where, [up[0]], one, after=first[1:])[0]
        second = gather_line(where, shard, 2)
        plane = run(cross_kernel, where, tokens_pieces, [shape(ROWS, *CROSS)])[0]
        cross = gather_cross(where, plane)
        second_pieces = gather_plane(where, second)
        after = second_pieces[:1] + cross[:1]
        shard = run(third_shard_kernel, where, [down[0]], [shape(*PART)], after=after)[0]
        third = gather_line(where, shard, 2)
        third_pieces = gather_plane(where, third, first_pieces[3:])
        third_pieces += cross
    else:
        tokens_pieces = exchange(run(token_kernel, where, sent, blocks_out))
        lines = wide_lines(joint[0], output[0], up_weight[:, 0], down[0])
        cross = lines[2][:, 3 * S :]
        lines[2] = lines[2][:, : 3 * S]
        first_pieces, second_pieces, third_pieces = [
            gather_plane(where, list(line)) for line in lines
        ]
        cross = jnp.stack([cross] + [swap(cross, "row", m) for m in range(1, ROWS)], axis=1)
        third_pieces += list(cross.reshape(2, *PLANES.shape))

    vecs = vectors.reshape(72, 128)
    tokens, grads, wj, wo, mixed, probs, attended, part = run(
        attend_kernel,
        where,
        tokens_pieces + [vecs] + first_pieces,
        [
            shape(LEN, D),
            shape(LEN, D),
            shape(ROWS, MIX, W),
            shape(D, COLS),
            shape(MIX, LEN),
            shape(HEADS, LEN, LEN),
            shape(COLS, LEN),
            shape(LEN, D),
        ],
        [
            pltpu.VMEM((ROWS, LEN, 2 * W), BF16),
            pltpu.VMEM((MIX, LEN), F32),
            pltpu.VMEM((LEN, LEN), F32),
            pltpu.VMEM((8, MIX), F32),
        ],
    )
    hidden, hidden_low, normed, inverse, act, slope, wu = run(
        up_kernel,
        where,
        [tokens, part, swap(part, "col", 1), vecs] + second_pieces,
        [
            shape(LEN, D, dtype=F32),
            shape(LEN, D),
            shape(LEN, D, dtype=F32),
            shape(LEN, 1, dtype=F32),
            shape(LEN, FFC),
            shape(LEN, FFC, dtype=F32),
            shape(D, FFC),
        ],
        [pltpu.VMEM((LEN, FFC), F32)],
        after=third_pieces[6:],
    )
    wd, part = run(
        down_kernel, where, [act] + third_pieces, [shape(D, FFC), shape(LEN, D)]
    )
    out = run(
        second_norm_kernel,
        where,
        [hidden, part, swap(part, "col", 1), vecs, grads, act],
        [shape(LEN, D, dtype=F32), shape(LEN, D), shape(LEN, D, dtype=F32)]
        + [shape(8, D, dtype=F32)]
        + handed_shapes(PART)
        + [PLANES] * 2,
        [
            pltpu.VMEM((ROWS, QUADS) + PART, BF16),
            pltpu.VMEM((QUADS, ROWS) + CROSS, BF16),
        ],
    )
    (result, grad_low, grad_two, sums_two), third_handed, cross = out[:4], out[4:9], out[9:]
    third_got = scatter_first(third_handed)
    grad_pre, part, sums_up = run(
        hidden_back_kernel,
        where,
        [grad_low, slope, wd, wu],
        [shape(LEN, FFC), shape(LEN, D), shape(8, FFC, dtype=F32)],
        [pltpu.VMEM((LEN, FFC), F32)],
    )
    third_passed = scatter_pass(where, third_handed, third_got)
    second_handed = run(
        up_grad_kernel,
        where,
        [hidden_low, grad_pre],
        HANDED,
        [pltpu.VMEM((ROWS, QUADS) + CHUNK, BF16)],
    )
    grad_one, grad_mixed, low, sums_one = run(
        first_norm_kernel,
        where,
        [
            grad_two,
            part,
            swap(part, "col", 1),
            normed,
            inverse,
            vecs,
            wo,
            mixed,
            probs,
        ],
        [
            shape(LEN, D, dtype=F32),
            shape(MIX, LEN),
            shape(LEN, D),
            shape(8, D, dtype=F32),
        ],
        [
            pltpu.VMEM((COLS, LEN), BF16),
            pltpu.VMEM((LEN, LEN), F32),
            pltpu.VMEM((LEN, LEN), BF16),
        ],
    )
    vector, room = run(
        first_grad_kernel,
        where,
        [grad_mixed, low, sums_one, attended, tokens, sums_two, sums_up],
        [shape(*VECTOR, dtype=F32), shape(ROWS, QUADS, *CHUNK)],
    )
    cross_got = [swap(cross[1], "dp", 1)] if direct else []
    first_handed = run(
        first_hand_kernel,
        where,
        [room, vector] + third_passed,
        [shape(*FIRST_X), shape(*FIRST_Y)] + HANDED[2:],
        after=cross_got,
    )
    first_got = scatter_first(first_handed)

    def like(values):
        return [shape(*v.shape, dtype=F32) for v in values]

    def sums(dims, split):
        return [shape(*dims, dtype=F32), shape(*split)]

    if direct:
        plane = (ROWS,) + CROSS
        cross = run(cross_far_kernel, where, cross[:1] + cross_got, sums(plane, plane))
        cross_sum = [cross[0], swap(cross[1], "dp", 2)]
    else:
        cross_sum = []
    (part,) = run(
        token_back_kernel, where, [grad_mixed, wj], [shape(LEN, D)], after=first_handed[:1]
    )
    own = [shape(*CROSS, dtype=F32)] if direct else []
    pieces = run(
        token_sum_kernel,
        where,
        [result, grad_one, part, swap(part, "col", 1)] + cross_sum,
        blocks_out + own,
        [pltpu.VMEM((LEN, D), F32), pltpu.VMEM((ROWS, LEN, 2 * W), BF16)],
    )
    first_passed = run(
        carry_pass_kernel,
        where,
        first_handed[2:4] + first_handed[:1] + first_got,
        [PAIR, shape(*CARRIED)],
        after=pieces[:1],
    )
    first_last = scatter_second(first_passed)

    lines = [pltpu.VMEM((4,) + CHUNK, F32)]
    wide = [shape(4, *CHUNK, dtype=F32)]
    third_sum = run(
        near_line_kernel,
        where,
        third_handed[-1:] + third_got + first_got,
        sums((2,) + PART, (2,) + PART) if direct else [shape(4, *PART, dtype=F32)],
        [pltpu.VMEM((4,) + PART, F32)],
    )
    if direct:
        got = swap(third_sum[1], "dp", 1)
        third_sum = run(far_line_kernel, where, [third_sum[0], got], sums(PART, PART))
        third_sum[1] = swap(third_sum[1], "dp", 2)
        ready = third_sum[1:] + pieces[:1]
    else:
        ready = pieces[:1]
    second_got = scatter_first(second_handed)
    second_passed = scatter_pass(where, second_handed, second_got, ready)
    second_last = scatter_second(second_passed)
    first_sum = run(
        carry_near_kernel,
        where,
        first_handed[-1:] + first_got + first_last + first_passed[1:],
        sums((2 * W + VROWS, COLS), CARRIED) if direct else wide + [shape(*VECTOR, dtype=F32)],
        lines,
        after=second_passed,
    )
    second_sum = run(
        line_kernel,
        where,
        second_handed[-1:] + second_got + second_last,
        sums(CHUNK, CHUNK) + [shape(*CHUNK)] * 2 if direct else wide,
        lines,
    )
    if direct:
        got = swap(first_sum[1], "dp", 1)
        first_sum = run(
            carry_far_kernel,
            where,
            [first_sum[0], got],
            sums((W + VROWS, COLS), (W + 2 * VROWS, COLS)),
        )
        got = swap(first_sum[1], "dp", 2)
        state = joint + output
        new = run(
            first_adam_kernel,
            where,
            [first_sum[0], got] + state,
            like(state) + [shape(*VECTOR, dtype=F32)],
        )
        joint_new, output_new, vector = new[:3], new[3:6], new[6]

    flat_out = [shape(ROWS, 3 * PAIRS, 128, dtype=F32)] * 2
    got = exchange(pieces[:ROWS])
    out = run(token_out_kernel, where, got, flat_out)
    layer_out, tokens_grad = [v.reshape(tokens_in.shape) for v in out]

    def step_vectors(vector):
        state = [v.reshape(72, 128) for v in (vectors, vector_first, vector_second)]
        new = run(
            vector_adam_kernel,
            where,
            [vector, swap(vector, "col", 1)] + state,
            like(state),
            [pltpu.VMEM((72, 128), F32)],
        )
        return [v.reshape(vectors.shape) for v in new]

    if direct:
        down_new = run(
            down_adam_kernel, where, third_sum + pieces[ROWS:] + got[1:] + down, like(down)
        )
        vector_new = step_vectors(vector)
        got = [swap(v, "dp", mask) for v, mask in zip(second_sum[1:], ORDER[1:])]
        after = out[:1] + vector_new[:1] + down_new[:1]
        up_new = run(up_adam_kernel, where, second_sum[:1] + got + up, like(up), after=after)
        up_new = [v.reshape(up_weight.shape) for v in up_new]
    else:
        kept, sent = [v.reshape(2, ROWS, *CROSS) for v in cross]
        cross = jnp.stack([kept, sent], axis=1).reshape(QUADS, ROWS, *CROSS)
        cross = lax.psum_scatter(cross.astype(F32), "row", scatter_dimension=1)
        third = jnp.concatenate([third_sum[0], cross], axis=1)
        grads = wide_sums(first_sum[0], second_sum[0], third)
        joint_new = adamw(*joint, grads[0], JOINT_RATE, DECAY)
        output_new = adamw(*output, grads[1], OUTPUT_RATE, DECAY)
        up_new = adamw(*up, grads[2][:, None], JOINT_RATE, DECAY)
        down_new = adamw(*down, grads[3], DOWN_RATE, DECAY)
        vector_new = step_vectors(lax.psum(first_sum[1], "dp"))

    return (
        layer_out,
        tokens_grad,
        *[jnp.transpose(v, (2, 0, 1)) for v in joint_new],
        *[v.T[:, None] for v in output_new],
        *up_new,
        *[v.T[:, None] for v in down_new],
        *vector_new,
    )


def solution(mesh):
    first = P("row", "col", "dp")
    second = P("col", "row", "dp")
    tokens = P("dp", "row", None)
    weights = (first,) * 3 + (second,) * 3 + (first,) * 3 + (second,) * 3 + (P(),) * 3
    in_specs = (tokens, P(("dp", "row"))) + weights + (tokens,)
    out_specs = (tokens, tokens) + weights
    return jax.shard_map(
        per_device, mesh=mesh, in_specs=in_specs, out_specs=out_specs, check_vma=False
    )
```

```python
from functools import partial

import jax
import jax.numpy as jnp
from jax import lax
from jax.experimental import pallas as pl
from jax.experimental.pallas import tpu as pltpu
from jax.sharding import PartitionSpec as P

D = 768
H = 12
HD = 64
FF = 3072
LEN = 256
STEP = 10

NORM_EPS = 1e-12
BETA_ONE = 0.9
BETA_TWO = 0.999
ADAM_EPS = 1e-08
DECAY = 0.01
VECTOR_RATE = 0.2

F32 = jnp.float32
BF16 = jnp.bfloat16

ROWS = 4
QUADS = 4
W = D // ROWS
S = W // QUADS
COLS = D // 2
HEADS = COLS // HD
FFC = FF // 2
MIX = HEADS * 3 * HD
PAIRS = LEN // 2
CHUNK = (W, COLS)
PART = (3 * S, COLS)
CROSS = (S, COLS)
MIB = 1024 * 1024


def swap(value, axis, mask):
    n = lax.axis_size(axis)
    return lax.ppermute(value, axis, [(i, i ^ mask) for i in range(n)])


def shape(*dims, dtype=BF16):
    return jax.ShapeDtypeStruct(dims, dtype)


def run(kernel, where, args, outs, scratch=(), limit=8, after=(), fetch=False):
    vmem = pl.BlockSpec(memory_space=pltpu.VMEM)
    first, late = 1 + len(args), len(after)

    def body(*refs):
        kernel(*refs[:first], *refs[first + late :])

    out = pl.pallas_call(
        body,
        out_shape=outs,
        in_specs=[pl.BlockSpec(memory_space=pltpu.SMEM)]
        + [pl.BlockSpec(memory_space=pl.ANY) if fetch else vmem] * len(args)
        + [pl.BlockSpec(memory_space=pl.ANY)] * late,
        out_specs=[vmem] * len(outs),
        scratch_shapes=list(scratch),
        compiler_params=pltpu.CompilerParams(vmem_limit_bytes=limit * MIB),
    )(where, *args, *after)
    return list(out)


def dot(left, right, dims):
    return lax.dot_general(left, right, (dims, ((), ())), preferred_element_type=F32)


NN = ((1,), (0,))
NT = ((1,), (1,))
TN = ((0,), (0,))


def each(count, body):
    def step(i, carry):
        body(i)
        return carry

    lax.fori_loop(0, count, step, 0)


def row_of(vecs, start, count):
    return jnp.concatenate([vecs[start + i : start + i + 1, :] for i in range(count)], axis=1)


def vector_row(vecs, k):
    return row_of(vecs, 6 * k, 6)


def pick_col(where, left, right):
    return jnp.where(where[2] == 0, left, right)


def split_parts(value):
    high = value.astype(BF16)
    return high, (value - high.astype(F32)).astype(BF16)


def opening_kernel(where, tokens, grads, joint, output, down, *refs):
    outs, first = refs[:ROWS], refs[ROWS]
    tokens_in, grads_in, joint_in, output_in, down_in, done = refs[ROWS + 1 :]
    copies = [
        pltpu.make_async_copy(source, target, done.at[i])
        for i, (source, target) in enumerate(
            [
                (joint, joint_in),
                (output, output_in),
                (tokens, tokens_in),
                (grads, grads_in),
                (down.at[:, 3 * COLS :], down_in),
            ]
        )
    ]
    for copy in copies:
        copy.start()
    copies[0].wait()
    copies[1].wait()
    for h in range(HEADS // 2):
        pair = [joint_in[h].astype(BF16), joint_in[h + HEADS // 2].astype(BF16)]
        first[h * S : (h + 1) * S, :] = jnp.concatenate(pair, axis=1)
    first[HEADS // 2 * S :, :] = output_in[...].astype(BF16)
    copies[2].wait()
    copies[3].wait()
    copies[4].wait()
    for m, out in enumerate(outs):
        out[0:PAIRS, :] = tokens_in[where[0] ^ m]
        out[PAIRS:LEN, :] = grads_in[where[0] ^ m]
        out[LEN:, :] = down_in[...].astype(BF16)


def second_shard_kernel(where, up, second):
    for q in range(3):
        second[:, q * 128 : (q + 1) * 128] = up[pl.ds(q, W, stride=3), :].astype(BF16)


def third_shard_kernel(where, down, third):
    for q in range(3):
        third[q * S : (q + 1) * S, :] = down[:, q * COLS : (q + 1) * COLS].astype(BF16)


def pair_kernel(where, b0, b1, pair):
    pair[0] = b0[...]
    pair[1] = b1[...]


def cross_kernel(where, t0, t1, t2, t3, plane):
    for m, piece in enumerate([t0, t1, t2, t3]):
        plane[m] = piece[LEN:, :]


def planes_kernel(where, b0, b1, planes):
    planes[0:ROWS] = b0[...]
    planes[ROWS:] = b1[...]


def whole_kernel(where, *refs):
    *pieces, line = refs
    for k in range(QUADS):
        line[k] = pieces[k][...] if len(pieces) == QUADS else pieces[k // 2][k % 2]


def halves_kernel(where, from_x, from_y, near_y, far_x):
    near_y[...] = from_y[0:2]
    far_x[...] = from_x[2:4]


def token_kernel(where, tokens, grads, *outs):
    for m, out in enumerate(outs):
        out[0:PAIRS, :] = tokens[where[0] ^ m]
        out[PAIRS:LEN, :] = grads[where[0] ^ m]


ORDER = (0, 2, 1, 3)


def blocks(where, pieces):
    found = [(piece, i) for piece in pieces for i in range(piece.shape[0])]
    for at, (piece, i) in enumerate(found):
        yield where[0] ^ (at // QUADS), where[1] ^ ORDER[at % QUADS], piece[i]


def cross_blocks(where, pieces):
    for j, piece in enumerate(pieces):
        for i in range(2 * ROWS):
            yield where[0] ^ (i % ROWS), where[1] ^ ORDER[2 * j + i // ROWS], piece[i]


def unpack_tokens(x):
    parts = [jnp.concatenate([x[r][:, :W], x[r][:, W:]], axis=0) for r in range(ROWS)]
    return jnp.concatenate(parts, axis=1)


def pack_tokens(value, room, k):
    for r in range(ROWS):
        both = value[:, r * W : (r + 1) * W]
        packed = jnp.concatenate([both[:PAIRS], both[PAIRS:]], axis=1).astype(BF16)
        room[r, k * PAIRS : (k + 1) * PAIRS, :] = packed


def attend_kernel(where, t0, t1, t2, t3, vecs, *refs):
    pieces, refs = refs[:5], refs[5:]
    tokens, grads, wj, wo, mixed, probs, attended, part, room, mixing, scores, parts = refs
    for m, piece in enumerate([t0, t1, t2, t3]):
        room[where[0] ^ m] = piece[0:LEN, :]
    tokens[...] = unpack_tokens([room[r, 0:PAIRS, :] for r in range(ROWS)])
    grads[...] = unpack_tokens([room[r, PAIRS:, :] for r in range(ROWS)])
    half = HEADS // 2
    for row, quad, value in blocks(where, pieces):
        for h in range(half):
            rows = value[h * S : (h + 1) * S, :]
            for k, cut in enumerate([rows[:, :W], rows[:, W:]]):
                start = pl.multiple_of((h + k * half) * 3 * HD + quad * S, 16)
                wj[row, pl.ds(start, S), :] = cut
        start = pl.multiple_of(row * W + quad * S, 16)
        wo[pl.ds(start, S), :] = value[half * S :, :]
    total = dot(wj[0], tokens[:, :W], NT)
    for r in range(1, ROWS):
        total = total + dot(wj[r], tokens[:, r * W : (r + 1) * W], NT)
    mixing[...] = total
    query_bias, value_bias = [
        pick_col(where, row_of(vecs, start, 3), row_of(vecs, start + 3, 3)) for start in (0, 6)
    ]
    zero = jnp.zeros((1, HD), F32)
    row = []
    for h in range(HEADS):
        at = slice(h * HD, (h + 1) * HD)
        row += [query_bias[:, at], zero, value_bias[:, at]]
    row = jnp.concatenate(row, axis=1)
    high, low = split_parts(row)
    rest = (row - high.astype(F32) - low.astype(F32)).astype(BF16)
    parts[...] = jnp.zeros_like(parts)
    parts[0:1, :] = high.astype(F32)
    parts[1:2, :] = low.astype(F32)
    parts[2:3, :] = rest.astype(F32)
    bias = dot(parts[...].astype(BF16), jnp.ones((8, LEN), BF16), TN)
    mixed[...] = (mixing[...] + bias).astype(BF16)
    slot = lax.broadcasted_iota(jnp.int32, (LEN, 1), 0)
    slot = jnp.where(slot < PAIRS, 2 * slot, 2 * (slot - PAIRS) + 1)
    valid = slot < where[3]
    for h in range(HEADS):
        base = h * 3 * HD
        query, keyed, valued = [mixed[base + k * HD : base + (k + 1) * HD, :] for k in range(3)]
        scores[...] = dot(keyed, query, TN)
        for q in range(2):
            at = slice(q * 128, (q + 1) * 128)
            score = jnp.where(valid, scores[:, at] * 0.125, -1e30)
            expo = jnp.exp(score - jnp.max(score, axis=0, keepdims=True))
            prob = expo * (1.0 / jnp.sum(expo, axis=0, keepdims=True))
            probs[h, :, at] = prob.astype(BF16)
        attended[h * HD : (h + 1) * HD, :] = dot(valued, probs[h], NN).astype(BF16)
    part[...] = dot(attended[...], wo[...], ((0,), (1,))).astype(BF16)


def norm_rows(resid, gain, shift_by):
    mean = jnp.sum(resid, axis=1, keepdims=True) * (1.0 / D)
    var = jnp.sum(resid * resid, axis=1, keepdims=True) * (1.0 / D) - mean * mean
    inverse = lax.rsqrt(var + NORM_EPS)
    normed = (resid - mean) * inverse
    return normed * gain + shift_by, normed, inverse


def norm_back_rows(grad, normed, inverse, gain):
    scaled = grad * gain
    total = jnp.sum(scaled, axis=1, keepdims=True) * (1.0 / D)
    cross = jnp.sum(scaled * normed, axis=1, keepdims=True) * (1.0 / D)
    return (scaled - total - normed * cross) * inverse


STRIP = 32


def strip(i):
    return pl.ds(pl.multiple_of(i * STRIP, STRIP), STRIP)


def up_kernel(where, tokens, p0, p1, vecs, *refs):
    pieces, refs = refs[:5], refs[5:]
    hidden, low, normed, inverse, act, slope, wu, pre = refs
    for row, quad, value in blocks(where, pieces):
        rows = pl.ds(pl.multiple_of(row * W, W), W)
        wu[rows, pl.ds(pl.multiple_of(quad * COLS, COLS), COLS)] = value

    bias_out, gain, shift_by = [vector_row(vecs, k) for k in (2, 3, 4)]

    def first(i):
        at = strip(i)
        resid = tokens[at, :].astype(F32) + (p0[at, :].astype(F32) + p1[at, :].astype(F32))
        out, unit, scale = norm_rows(resid + bias_out, gain, shift_by)
        hidden[at, :] = out
        low[at, :] = out.astype(BF16)
        normed[at, :] = unit
        inverse[at, :] = scale

    each(LEN // STRIP, first)
    pre[...] = dot(low[...], wu[...], NN)
    bias = pick_col(where, row_of(vecs, 48, 12), row_of(vecs, 60, 12))
    for q in range(4):
        cols = slice(q * COLS, (q + 1) * COLS)
        shift_up = bias[:, cols]

        def second(i, cols=cols, shift_up=shift_up):
            at = (strip(i), cols)
            value = pre[at] + shift_up
            phi = 0.5 * (1.0 + lax.erf(value * (0.5**0.5)))
            density = jnp.exp(-0.5 * value * value) * 0.3989422804014327
            act[at] = (value * phi).astype(BF16)
            slope[at] = phi + value * density

        each(LEN // STRIP, second)


def down_kernel(where, act, *refs):
    pieces, cross, wd, part = refs[:5], refs[5:7], refs[7], refs[8]
    for row, quad, value in blocks(where, pieces):
        rows = pl.ds(pl.multiple_of(row * W + quad * S, 16), S)
        for q in range(3):
            wd[rows, q * COLS : (q + 1) * COLS] = value[q * S : (q + 1) * S, :]
    for row, quad, value in cross_blocks(where, cross):
        rows = pl.ds(pl.multiple_of(row * W + quad * S, 16), S)
        wd[rows, 3 * COLS :] = value
    part[...] = dot(act[...], wd[...], NT).astype(BF16)


def hand_out(where, room, outs):
    r = where[0]
    to_x, to_y, last_x, last_y, own = outs
    to_x[0:2] = room[r ^ 3, 0:2]
    to_x[2:4] = room[r ^ 1, 0:2]
    to_y[0:2] = room[r ^ 3, 2:4]
    to_y[2:4] = room[r ^ 2, 2:4]
    last_x[...] = room[r ^ 1, 2:4]
    last_y[...] = room[r ^ 2, 0:2]
    own[...] = room[r]


def handed_shapes(block):
    pair, line = shape(2, *block), shape(4, *block)
    return [line] * 2 + [pair] * 2 + [line]


HANDED = handed_shapes(CHUNK)
PAIR = shape(2, *CHUNK)
PLANES = shape(2 * ROWS, *CROSS)

VROWS = 32
VECTOR = (VROWS, COLS)
CARRIED = (2 * W + 2 * VROWS, COLS)

LATE_X = 4 * W + 2 * VROWS
LATE_Y = 4 * W
FIRST_X = (LATE_X + 2 * PART[0], COLS)
FIRST_Y = (LATE_Y + 2 * PART[0], COLS)


def put_vector(out, start, value):
    high, low = split_parts(value)
    out[start : start + VROWS, :] = high
    out[start + VROWS : start + 2 * VROWS, :] = low


def get_vector(value, start):
    high = value[start : start + VROWS, :].astype(F32)
    return high + value[start + VROWS : start + 2 * VROWS, :].astype(F32)


def second_norm_kernel(where, hidden, p0, p1, vecs, grads, act, *refs):
    (result, low, grad_two, sums), handed = refs[:4], refs[4:9]
    cross_own, cross_send, room, cross = refs[9:]
    sums[...] = jnp.zeros_like(sums)
    bias_down, gain, shift_by = [vector_row(vecs, k) for k in (5, 6, 7)]

    def body(i):
        at = strip(i)
        resid = hidden[at, :] + (p0[at, :].astype(F32) + p1[at, :].astype(F32)) + bias_down
        out, unit, scale = norm_rows(resid, gain, shift_by)
        result[at, :] = out
        grad = grads[at, :].astype(F32)
        back = norm_back_rows(grad, unit, scale, gain)
        grad_two[at, :] = back
        rounded = back.astype(BF16)
        low[at, :] = rounded
        sums[0:1, :] += jnp.sum(rounded.astype(F32), axis=0, keepdims=True)
        sums[1:2, :] += jnp.sum(grad * unit, axis=0, keepdims=True)
        sums[2:3, :] += jnp.sum(grad, axis=0, keepdims=True)

    each(LEN // STRIP, body)
    for q in range(4):
        cols = slice(q * COLS, (q + 1) * COLS)
        grad = dot(low[...], act[:, cols], TN).astype(BF16)
        for r in range(ROWS):
            for z in range(QUADS):
                start = r * W + z * S
                if q < 3:
                    room[r, z, q * S : (q + 1) * S, :] = grad[start : start + S, :]
                else:
                    cross[z, r] = grad[start : start + S, :]
    hand_out(where, room, handed)
    hand_cross(where, cross, cross_own, cross_send)


def hidden_back_kernel(where, low, slope, wd, wu, grad_pre, part, sums, back):
    back[...] = dot(low[...], wd[...], NN)
    sums[...] = jnp.zeros_like(sums)
    for q in range(4):
        cols = slice(q * COLS, (q + 1) * COLS)

        def body(i, cols=cols):
            at = (strip(i), cols)
            value = (back[at] * slope[at]).astype(BF16)
            grad_pre[at] = value
            sums[0:1, cols] += jnp.sum(value.astype(F32), axis=0, keepdims=True)

        each(LEN // STRIP, body)
    part[...] = dot(grad_pre[...], wu[...], NT).astype(BF16)


def hand_cross(where, cross, own, send):
    for k, mask in enumerate([0, 2]):
        rows = slice(k * ROWS, (k + 1) * ROWS)
        own[rows] = cross[where[1] ^ mask]
        send[rows] = cross[where[1] ^ mask ^ 1]


def up_grad_kernel(where, low, grad_pre, *refs):
    handed, (cross_own, cross_send, room, cross) = refs[:5], refs[5:]
    for z in range(QUADS):
        grad = dot(low[...], grad_pre[:, z * COLS : (z + 1) * COLS], TN).astype(BF16)
        for r in range(ROWS):
            room[r, z] = grad[r * W : r * W + PART[0], :]
            cross[z, r] = grad[r * W + PART[0] : (r + 1) * W, :]
    hand_out(where, room, handed)
    hand_cross(where, cross, cross_own, cross_send)


def first_norm_kernel(
    where, grad_two, p0, p1, normed, inverse, vecs, wo, mixed, probs, *refs
):
    grad_one, grad_mixed, low, sums, back, inner, scores = refs
    sums[...] = jnp.zeros_like(sums)
    gain = vector_row(vecs, 3)

    def body(i):
        at = strip(i)
        grad = grad_two[at, :] + (p0[at, :].astype(F32) + p1[at, :].astype(F32))
        unit = normed[at, :]
        out = norm_back_rows(grad, unit, inverse[at, :], gain)
        grad_one[at, :] = out
        rounded = out.astype(BF16)
        low[at, :] = rounded
        sums[0:1, :] += jnp.sum(rounded.astype(F32), axis=0, keepdims=True)
        sums[1:2, :] += jnp.sum(grad * unit, axis=0, keepdims=True)
        sums[2:3, :] += jnp.sum(grad, axis=0, keepdims=True)

    each(LEN // STRIP, body)
    back[...] = dot(wo[...], low[...], ((0,), (1,))).astype(BF16)
    for h in range(HEADS):
        base = h * 3 * HD
        query, keyed, valued = [mixed[base + k * HD : base + (k + 1) * HD, :] for k in range(3)]
        grad_out = back[h * HD : (h + 1) * HD, :]
        inner[...] = dot(valued, grad_out, TN)
        for q in range(2):
            at = slice(q * 128, (q + 1) * 128)
            prob = probs[h, :, at].astype(F32)
            grad = inner[:, at]
            mean = jnp.sum(grad * prob, axis=0, keepdims=True)
            scores[:, at] = (prob * (grad - mean)).astype(BF16)
        grads = [
            dot(keyed, scores[...], NN) * 0.125,
            dot(query, scores[...], NT) * 0.125,
            dot(grad_out, probs[h], NT),
        ]
        for k, grad in enumerate(grads):
            grad_mixed[base + k * HD : base + (k + 1) * HD, :] = grad.astype(BF16)


def first_grad_kernel(where, grad_mixed, low, sums, attended, tokens, sums_two, sums_up, *refs):
    vector, room = refs
    half = HEADS // 2
    for r in range(ROWS):
        cut = tokens[:, r * W : (r + 1) * W]
        grad = dot(grad_mixed[...], cut, NN).astype(BF16)
        for z in range(QUADS):
            for h in range(half):
                starts = [(h + k * half) * 3 * HD + z * S for k in range(2)]
                pair = [grad[start : start + S, :] for start in starts]
                room[r, z, h * S : (h + 1) * S, :] = jnp.concatenate(pair, axis=1)
        grad = dot(low[:, r * W : (r + 1) * W], attended[...], ((0,), (1,))).astype(BF16)
        for z in range(QUADS):
            room[r, z, half * S :, :] = grad[z * S : (z + 1) * S, :]
    left = jnp.where(where[2] == 0, 1.0, 0.0)
    right = 1.0 - left
    total = dot(jnp.ones((8, LEN), BF16), grad_mixed[...], NT)[0:1, :]
    vector[...] = jnp.zeros_like(vector)
    for k, start in enumerate([0, 2 * HD]):
        at = [h * 3 * HD + start for h in range(HEADS)]
        row = jnp.concatenate([total[:, i : i + HD] for i in at], axis=1)
        vector[2 * k : 2 * k + 1, :] = row * left
        vector[2 * k + 1 : 2 * k + 2, :] = row * right
    for k, found in enumerate([sums, sums_two]):
        for i in range(3):
            for j in range(2):
                row = 4 + 6 * k + 2 * i + j
                vector[row : row + 1, :] = found[i : i + 1, j * COLS : (j + 1) * COLS] * left
    for j in range(4):
        row = sums_up[0:1, j * COLS : (j + 1) * COLS]
        vector[16 + j : 17 + j, :] = row * left
        vector[20 + j : 21 + j, :] = row * right


def first_hand_kernel(where, room, vector, late_x, late_y, to_x, to_y, last_x, last_y, own):
    r = where[0]
    for k in range(2):
        far, near = slice(k * W, (k + 1) * W), slice((2 + k) * W, (3 + k) * W)
        to_x[far, :] = room[r ^ 3, k]
        to_x[near, :] = room[r ^ 1, k]
        to_y[far, :] = room[r ^ 3, 2 + k]
        to_y[near, :] = room[r ^ 2, 2 + k]
        for start, out, late in [(LATE_X, to_x, late_x), (LATE_Y, to_y, late_y)]:
            at = start + k * PART[0]
            out[at : at + PART[0], :] = late[k]
    last_x[...] = room[r ^ 1, 2:4]
    last_y[...] = room[r ^ 2, 0:2]
    own[...] = room[r]
    put_vector(to_x, 4 * W, vector[...])


def token_back_kernel(where, grad_mixed, wj, part):
    for r in range(ROWS):
        part[:, r * W : (r + 1) * W] = dot(grad_mixed[...], wj[r], TN).astype(BF16)


def token_sum_kernel(where, result, grad_one, p0, p1, *refs):
    total, room = refs[-2:]
    count = (len(refs) - 6) // 3
    sums, outs, owns = refs[: 2 * count], refs[2 * count : 2 * count + 4], refs[2 * count + 4 : -2]

    def body(i):
        at = strip(i)
        total[at, :] = grad_one[at, :] + (p0[at, :].astype(F32) + p1[at, :].astype(F32))

    each(LEN // STRIP, body)
    pack_tokens(result, room, 0)
    pack_tokens(total, room, 1)
    for m, out in enumerate(outs):
        row = where[0] ^ m
        out[0:LEN, :] = room[row]
        for i, own in enumerate(owns):
            block = sums[2 * i][row] + sums[2 * i + 1][row].astype(F32)
            out[LEN + i * S : LEN + (i + 1) * S, :] = block.astype(BF16)
            if m == 0:
                own[...] = block


def token_out_kernel(where, t0, t1, t2, t3, result, total):
    for m, piece in enumerate([t0, t1, t2, t3]):
        for k, out in enumerate([result, total]):
            for q in range(3):
                value = piece[k * PAIRS : (k + 1) * PAIRS, q * 128 : (q + 1) * 128].astype(F32)
                out[where[0] ^ m, pl.ds(q, PAIRS, stride=3), :] = value


def pass_kernel(where, last_x, last_y, from_x, from_y, to_x, to_y):
    to_x[...] = (last_x[...].astype(F32) + from_y[0:2].astype(F32)).astype(BF16)
    to_y[...] = (last_y[...].astype(F32) + from_x[0:2].astype(F32)).astype(BF16)


def carry_pass_kernel(where, last_x, last_y, carried, from_x, from_y, to_x, to_y):
    for k in range(2):
        rows = slice(k * W, (k + 1) * W)
        to_x[k] = (last_x[k].astype(F32) + from_y[rows, :].astype(F32)).astype(BF16)
        to_y[rows, :] = (last_y[k].astype(F32) + from_x[rows, :].astype(F32)).astype(BF16)
    put_vector(to_y, 2 * W, get_vector(carried, 4 * W) + get_vector(from_x, 4 * W))


def add_plane(own, from_x, from_y, last_x, last_y, room):
    for k in range(2):
        room[k] = (own[k].astype(F32) + from_x(k)) + last_y(k)
        room[2 + k] = (own[2 + k].astype(F32) + from_y(k)) + last_x(k)


def kept_blocks(ref):
    skip = ref.shape[0] - 2
    return lambda k: ref[skip + k].astype(F32)


def kept_rows(ref, start, rows=W):
    return lambda k: ref[start + k * rows : start + (k + 1) * rows, :].astype(F32)


def line_kernel(where, own, from_x, from_y, last_x, last_y, kept, *refs):
    *sends, room = refs
    add_plane(own, *[kept_blocks(v) for v in (from_x, from_y, last_x, last_y)], room)
    if sends:
        kept[...] = room[where[1]]
        for mask, send in zip(ORDER[1:], sends):
            send[...] = room[where[1] ^ mask].astype(BF16)
    else:
        kept[...] = room[...]


def near_line_kernel(where, own, from_x, from_y, late_x, late_y, kept, *refs):
    *sends, room = refs
    late = [kept_rows(late_x, LATE_X, PART[0]), kept_rows(late_y, LATE_Y, PART[0])]
    add_plane(own, kept_blocks(from_x), kept_blocks(from_y), *late, room)
    if sends:
        for k, mask in enumerate([0, 2]):
            kept[k] = room[where[1] ^ mask]
            sends[0][k] = room[where[1] ^ mask ^ 1].astype(BF16)
    else:
        kept[...] = room[...]


def far_line_kernel(where, kept, got, total, send):
    total[...] = kept[0] + got[0].astype(F32)
    send[...] = (kept[1] + got[1].astype(F32)).astype(BF16)


def cross_far_kernel(where, own, got, kept, send):
    kept[...] = own[0:ROWS].astype(F32) + got[0:ROWS].astype(F32)
    send[...] = (own[ROWS:].astype(F32) + got[ROWS:].astype(F32)).astype(BF16)


def carry_near_kernel(where, own, first_x, first_y, last_x, from_y, passed, kept, *refs):
    *sends, room = refs
    near = [kept_rows(first_x, 2 * W), kept_rows(first_y, 2 * W)]
    add_plane(own, *near, kept_blocks(last_x), kept_rows(from_y, 0), room)
    vector = get_vector(passed, 2 * W) + get_vector(from_y, 2 * W)
    if kept.ndim == 2:
        for k, mask in enumerate([0, 2]):
            rows = slice(k * W, (k + 1) * W)
            kept[rows, :] = room[where[1] ^ mask]
            sends[0][rows, :] = room[where[1] ^ mask ^ 1].astype(BF16)
        kept[2 * W :, :] = vector
        put_vector(sends[0], 2 * W, vector)
    else:
        kept[...] = room[...]
        sends[0][...] = vector


def add_vector(own, got, start):
    high, low = split_parts(own)
    return (high.astype(F32) + low.astype(F32)) + get_vector(got, start)


def carry_far_kernel(where, kept, got, total, send):
    total[0:W, :] = kept[0:W, :] + got[0:W, :].astype(F32)
    send[0:W, :] = (kept[W : 2 * W, :] + got[W : 2 * W, :].astype(F32)).astype(BF16)
    vector = add_vector(kept[2 * W :, :], got, 2 * W)
    total[W:, :] = vector
    put_vector(send, W, vector)


def adamw(weight, first, second, grad, rate, decay):
    first_new = BETA_ONE * first + (1.0 - BETA_ONE) * grad
    second_new = BETA_TWO * second + (1.0 - BETA_TWO) * grad * grad
    fix_one = 1.0 - BETA_ONE**STEP
    fix_two = 1.0 - BETA_TWO**STEP
    update = first_new / fix_one / (jnp.sqrt(second_new / fix_two) + ADAM_EPS) + decay * weight
    return (first_new, second_new, weight - rate * update)


JOINT_RATE = D ** (-0.5)
OUTPUT_RATE = (4 * D // LEN) ** (-0.5)
DOWN_RATE = FF ** (-0.5)


def first_adam_kernel(where, kept, got, jw, jf, js, ow, of, os, *refs):
    outs, vector = refs[:6], refs[6]
    grad = kept[0:W, :] + got[0:W, :].astype(F32)
    half = HEADS // 2
    for h in range(HEADS):
        rows = grad[h % half * S : (h % half + 1) * S, :]
        cut = rows[:, :W] if h < half else rows[:, W:]
        new = adamw(jw[h], jf[h], js[h], cut, JOINT_RATE, DECAY)
        for out, value in zip(outs[:3], new):
            out[h] = value
    new = adamw(ow[...], of[...], os[...], grad[half * S :, :], OUTPUT_RATE, DECAY)
    for out, value in zip(outs[3:], new):
        out[...] = value
    vector[...] = add_vector(kept[W:, :], got, W)


def vector_adam_kernel(where, mine, other, weight, first, second, *refs):
    outs, grad = refs[:3], refs[3]
    total = mine[...] + other[...]
    for q in range(3):
        grad[pl.ds(q, 24, stride=3), :] = total[0:24, q * 128 : (q + 1) * 128]
    new = adamw(weight[...], first[...], second[...], grad[...], VECTOR_RATE, 0.0)
    for out, value in zip(outs, new):
        out[...] = value


def sum_rows(own, r1, r2, r3, start):
    rows = slice(start, start + S)
    far = r2[rows, :].astype(F32) + r3[rows, :].astype(F32)
    return (own[...] + r1[rows, :].astype(F32)) + far


def up_adam_kernel(where, kept, r2, r1, r3, own, c1, c2, c3, w, f, s, *outs):
    grad = (kept[...] + r1[...].astype(F32)) + (r2[...].astype(F32) + r3[...].astype(F32))
    grad = jnp.concatenate([grad, sum_rows(own, c1, c2, c3, LEN + S)], axis=0)
    for q in range(3):
        at = (pl.ds(q, W, stride=3), slice(None))
        cut = grad[:, q * 128 : (q + 1) * 128]
        for out, value in zip(outs, adamw(w[at], f[at], s[at], cut, JOINT_RATE, DECAY)):
            out[at] = value


def down_adam_kernel(where, kept, got, own, r1, r2, r3, w, f, s, *outs):
    cross = sum_rows(own, r1, r2, r3, LEN)
    most = kept[...] + got[...].astype(F32)
    for q in range(4):
        at = (slice(None), slice(q * COLS, (q + 1) * COLS))
        cut = most[q * S : (q + 1) * S, :] if q < 3 else cross
        for out, value in zip(outs, adamw(w[at], f[at], s[at], cut, DOWN_RATE, DECAY)):
            out[at] = value


def gather_line(where, shard, steps):
    if steps == 1:
        return [shard] + [swap(shard, "dp", mask) for mask in ORDER[1:]]
    pair = [shape(2, *shard.shape)]
    pair = run(pair_kernel, where, [shard, swap(shard, "dp", 2)], pair)[0]
    return [pair, swap(pair, "dp", 1)]


def gather_plane(where, line, after=()):
    block = line[0].shape[-2:]
    line = run(whole_kernel, where, line, [shape(4, *block)], after=after)[0]
    from_x = swap(line, "row", 1)
    from_y = swap(line, "row", 2)
    near_y, far_x = run(halves_kernel, where, [from_x, from_y], [shape(2, *block)] * 2)
    return [line, from_x, from_y, swap(near_y, "row", 1), swap(far_x, "row", 2)]


def gather_cross(where, plane):
    planes = run(planes_kernel, where, [plane, swap(plane, "dp", 2)], [PLANES])[0]
    return [planes, swap(planes, "dp", 1)]


def scatter_first(handed):
    return [swap(value, "row", 1 + i % 2) for i, value in enumerate(handed[:-3])]


def scatter_pass(where, handed, got, after=()):
    pair = [shape(*handed[2].shape)] * 2
    return run(pass_kernel, where, handed[2:4] + got, pair, after=after)


def scatter_second(passed):
    return [swap(passed[0], "row", 1), swap(passed[1], "row", 2)]


def exchange(pieces):
    return [pieces[0]] + [swap(pieces[m], "row", m) for m in range(1, ROWS)]


def wide_lines(joint, output, up, down):
    order = jnp.array(ORDER)
    n = lax.axis_size("dp") // QUADS

    def collect(shard, axis):
        whole = lax.all_gather(shard.astype(BF16), "dp", axis=axis, tiled=True)
        return jnp.stack(jnp.split(whole, QUADS, axis=axis))

    joint = collect(joint, 1)
    half = HEADS // 2
    pair = joint.reshape(QUADS, 2, half, S, W)
    pair = jnp.transpose(pair, (0, 2, 3, 1, 4)).reshape(QUADS, half * S, 2 * W)
    first = jnp.concatenate([pair, collect(output, 0)], axis=1)
    second = collect(up, 1)
    third = collect(down, 0).reshape(QUADS, S, 4, COLS)
    third = jnp.transpose(third, (0, 2, 1, 3)).reshape(QUADS, W, COLS)
    return [jnp.take(value, order, axis=0) for value in (first, second, third)]


def wide_sums(first, second, third):
    def give(value, axis):
        whole = jnp.concatenate(list(value), axis=axis)
        return lax.psum_scatter(whole, "dp", scatter_dimension=axis, tiled=True)

    half = HEADS // 2
    pair = first[:, : half * S].reshape(QUADS, half, S, 2, W)
    joint = jnp.transpose(pair, (0, 3, 1, 2, 4)).reshape(QUADS, HEADS, S, W)
    third = jnp.transpose(third.reshape(QUADS, 4, S, COLS), (0, 2, 1, 3))
    third = third.reshape(QUADS, S, FFC)
    return give(joint, 1), give(first[:, half * S :], 0), give(second, 1), give(third, 0)


def per_device(
    tokens_in,
    lengths,
    joint_weight,
    joint_first,
    joint_second,
    output_weight,
    output_first,
    output_second,
    up_weight,
    up_first,
    up_second,
    down_weight,
    down_first,
    down_second,
    vectors,
    vector_first,
    vector_second,
    out_grad,
):
    r = lax.axis_index("row")
    col = lax.axis_index("col")
    direct = lax.axis_size("dp") == QUADS
    z = lax.axis_index("dp") if direct else jnp.int32(0)
    where = jnp.stack([r, z, col, lengths[0]]).astype(jnp.int32)

    joint = [jnp.transpose(v, (1, 2, 0)) for v in (joint_weight, joint_first, joint_second)]
    output = [v[:, 0].T for v in (output_weight, output_first, output_second)]
    down = [v[:, 0].T for v in (down_weight, down_first, down_second)]
    up = [up_weight, up_first, up_second]
    flat = up_weight.size // 128

    sent = [tokens_in.reshape(ROWS, PAIRS, 2 * W), out_grad.reshape(ROWS, PAIRS, 2 * W)]
    blocks_out = [shape(LEN + S if direct else LEN, 2 * W)] * ROWS
    if direct:
        up = [v.reshape(flat, 128) for v in up]
        one = [shape(*CHUNK)]
        *pieces, first = run(
            opening_kernel,
            where,
            sent + [joint[0], output[0], down[0]],
            blocks_out + one,
            [
                pltpu.VMEM(sent[0].shape, BF16),
                pltpu.VMEM(sent[1].shape, BF16),
                pltpu.VMEM(joint[0].shape, F32),
                pltpu.VMEM(output[0].shape, F32),
                pltpu.VMEM(CROSS, F32),
                pltpu.SemaphoreType.DMA((5,)),
            ],
            limit=56,
            fetch=True,
        )
        tokens_pieces = exchange(pieces)
        first = gather_line(where, first, 1)
        first_pieces = gather_plane(where, first, tokens_pieces[1:])
        shard = run(second_shard_kernel, where, [up[0]], one, after=first[1:])[0]
        second = gather_line(where, shard, 2)
        plane = run(cross_kernel, where, tokens_pieces, [shape(ROWS, *CROSS)])[0]
        cross = gather_cross(where, plane)
        second_pieces = gather_plane(where, second)
        after = second_pieces[:1] + cross[:1]
        shard = run(third_shard_kernel, where, [down[0]], [shape(*PART)], after=after)[0]
        third = gather_line(where, shard, 2)
        third_pieces = gather_plane(where, third, first_pieces[3:])
        third_pieces += cross
    else:
        tokens_pieces = exchange(run(token_kernel, where, sent, blocks_out))
        lines = wide_lines(joint[0], output[0], up_weight[:, 0], down[0])
        cross = lines[2][:, 3 * S :]
        lines[2] = lines[2][:, : 3 * S]
        first_pieces, second_pieces, third_pieces = [
            gather_plane(where, list(line)) for line in lines
        ]
        cross = jnp.stack([cross] + [swap(cross, "row", m) for m in range(1, ROWS)], axis=1)
        third_pieces += list(cross.reshape(2, *PLANES.shape))

    vecs = vectors.reshape(72, 128)
    tokens, grads, wj, wo, mixed, probs, attended, part = run(
        attend_kernel,
        where,
        tokens_pieces + [vecs] + first_pieces,
        [
            shape(LEN, D),
            shape(LEN, D),
            shape(ROWS, MIX, W),
            shape(D, COLS),
            shape(MIX, LEN),
            shape(HEADS, LEN, LEN),
            shape(COLS, LEN),
            shape(LEN, D),
        ],
        [
            pltpu.VMEM((ROWS, LEN, 2 * W), BF16),
            pltpu.VMEM((MIX, LEN), F32),
            pltpu.VMEM((LEN, LEN), F32),
            pltpu.VMEM((8, MIX), F32),
        ],
    )
    hidden, hidden_low, normed, inverse, act, slope, wu = run(
        up_kernel,
        where,
        [tokens, part, swap(part, "col", 1), vecs] + second_pieces,
        [
            shape(LEN, D, dtype=F32),
            shape(LEN, D),
            shape(LEN, D, dtype=F32),
            shape(LEN, 1, dtype=F32),
            shape(LEN, FFC),
            shape(LEN, FFC, dtype=F32),
            shape(D, FFC),
        ],
        [pltpu.VMEM((LEN, FFC), F32)],
        after=third_pieces[6:],
    )
    wd, part = run(
        down_kernel, where, [act] + third_pieces, [shape(D, FFC), shape(LEN, D)]
    )
    out = run(
        second_norm_kernel,
        where,
        [hidden, part, swap(part, "col", 1), vecs, grads, act],
        [shape(LEN, D, dtype=F32), shape(LEN, D), shape(LEN, D, dtype=F32)]
        + [shape(8, D, dtype=F32)]
        + handed_shapes(PART)
        + [PLANES] * 2,
        [
            pltpu.VMEM((ROWS, QUADS) + PART, BF16),
            pltpu.VMEM((QUADS, ROWS) + CROSS, BF16),
        ],
    )
    (result, grad_low, grad_two, sums_two), third_handed, cross = out[:4], out[4:9], out[9:]
    third_got = scatter_first(third_handed)
    grad_pre, part, sums_up = run(
        hidden_back_kernel,
        where,
        [grad_low, slope, wd, wu],
        [shape(LEN, FFC), shape(LEN, D), shape(8, FFC, dtype=F32)],
        [pltpu.VMEM((LEN, FFC), F32)],
    )
    third_passed = scatter_pass(where, third_handed, third_got)
    rooms = [
        pltpu.VMEM((ROWS, QUADS) + PART, BF16),
        pltpu.VMEM((QUADS, ROWS) + CROSS, BF16),
    ]
    out = run(
        up_grad_kernel,
        where,
        [hidden_low, grad_pre],
        handed_shapes(PART) + [PLANES] * 2,
        rooms,
    )
    second_handed, cross_up = out[:5], out[5:]
    grad_one, grad_mixed, low, sums_one = run(
        first_norm_kernel,
        where,
        [
            grad_two,
            part,
            swap(part, "col", 1),
            normed,
            inverse,
            vecs,
            wo,
            mixed,
            probs,
        ],
        [
            shape(LEN, D, dtype=F32),
            shape(MIX, LEN),
            shape(LEN, D),
            shape(8, D, dtype=F32),
        ],
        [
            pltpu.VMEM((COLS, LEN), BF16),
            pltpu.VMEM((LEN, LEN), F32),
            pltpu.VMEM((LEN, LEN), BF16),
        ],
    )
    vector, room = run(
        first_grad_kernel,
        where,
        [grad_mixed, low, sums_one, attended, tokens, sums_two, sums_up],
        [shape(*VECTOR, dtype=F32), shape(ROWS, QUADS, *CHUNK)],
    )
    cross_got = [swap(cross[1], "dp", 1)] if direct else []
    first_handed = run(
        first_hand_kernel,
        where,
        [room, vector] + third_passed,
        [shape(*FIRST_X), shape(*FIRST_Y)] + HANDED[2:],
        after=cross_got,
    )
    first_got = scatter_first(first_handed)

    def like(values):
        return [shape(*v.shape, dtype=F32) for v in values]

    def sums(dims, split):
        return [shape(*dims, dtype=F32), shape(*split)]

    cross_sum = []
    if direct:
        plane = (ROWS,) + CROSS
        for own, got in [(cross[0], cross_got[0]), (cross_up[0], swap(cross_up[1], "dp", 1))]:
            near = run(cross_far_kernel, where, [own, got], sums(plane, plane))
            cross_sum += [near[0], swap(near[1], "dp", 2)]
    (part,) = run(
        token_back_kernel, where, [grad_mixed, wj], [shape(LEN, D)], after=first_got
    )
    other = swap(part, "col", 1)
    own = [shape(*CROSS, dtype=F32)] * 2 if direct else []
    pieces = run(
        token_sum_kernel,
        where,
        [result, grad_one, part, other] + cross_sum,
        [shape(LEN + 2 * S if direct else LEN, 2 * W)] * ROWS + own,
        [pltpu.VMEM((LEN, D), F32), pltpu.VMEM((ROWS, LEN, 2 * W), BF16)],
    )
    first_passed = run(
        carry_pass_kernel,
        where,
        first_handed[2:4] + first_handed[:1] + first_got,
        [PAIR, shape(*CARRIED)],
        after=cross_sum[1:2],
    )
    first_last = scatter_second(first_passed)

    lines = [pltpu.VMEM((4,) + CHUNK, F32)]
    wide = [shape(4, *CHUNK, dtype=F32)]
    third_sum = run(
        near_line_kernel,
        where,
        third_handed[-1:] + third_got + first_got,
        sums((2,) + PART, (2,) + PART) if direct else [shape(4, *PART, dtype=F32)],
        [pltpu.VMEM((4,) + PART, F32)],
    )
    if direct:
        got = swap(third_sum[1], "dp", 1)
        third_sum = run(far_line_kernel, where, [third_sum[0], got], sums(PART, PART))
        third_sum[1] = swap(third_sum[1], "dp", 2)
        ready = third_sum[1:] + cross_sum[3:4]
    else:
        ready = pieces[:1]
    second_got = scatter_first(second_handed)
    second_passed = scatter_pass(where, second_handed, second_got, ready)
    second_last = scatter_second(second_passed)
    first_sum = run(
        carry_near_kernel,
        where,
        first_handed[-1:] + first_got + first_last + first_passed[1:],
        sums((2 * W + VROWS, COLS), CARRIED) if direct else wide + [shape(*VECTOR, dtype=F32)],
        lines,
        after=second_passed,
    )
    second_sum = run(
        line_kernel,
        where,
        second_handed[-1:] + second_got + second_last,
        sums(PART, PART) + [shape(*PART)] * 2 if direct else [shape(4, *PART, dtype=F32)],
        [pltpu.VMEM((4,) + PART, F32)],
    )
    if direct:
        got = swap(first_sum[1], "dp", 1)
        first_sum = run(
            carry_far_kernel,
            where,
            [first_sum[0], got],
            sums((W + VROWS, COLS), (W + 2 * VROWS, COLS)),
        )
        got = swap(first_sum[1], "dp", 2)
        state = joint + output
        new = run(
            first_adam_kernel,
            where,
            [first_sum[0], got] + state,
            like(state) + [shape(*VECTOR, dtype=F32)],
        )
        joint_new, output_new, vector = new[:3], new[3:6], new[6]

    flat_out = [shape(ROWS, 3 * PAIRS, 128, dtype=F32)] * 2
    got = exchange(pieces[:ROWS])
    out = run(token_out_kernel, where, got, flat_out)
    layer_out, tokens_grad = [v.reshape(tokens_in.shape) for v in out]

    def step_vectors(vector):
        state = [v.reshape(72, 128) for v in (vectors, vector_first, vector_second)]
        new = run(
            vector_adam_kernel,
            where,
            [vector, swap(vector, "col", 1)] + state,
            like(state),
            [pltpu.VMEM((72, 128), F32)],
        )
        return [v.reshape(vectors.shape) for v in new]

    if direct:
        down_new = run(
            down_adam_kernel, where, third_sum + pieces[ROWS : ROWS + 1] + got[1:] + down, like(down)
        )
        vector_new = step_vectors(vector)
        rows_got = pieces[ROWS + 1 :] + got[1:]
        got = [swap(v, "dp", mask) for v, mask in zip(second_sum[1:], ORDER[1:])]
        after = out[:1] + vector_new[:1] + down_new[:1]
        up_new = run(up_adam_kernel, where, second_sum[:1] + got + rows_got + up, like(up), after=after)
        up_new = [v.reshape(up_weight.shape) for v in up_new]
    else:

        def sum_cross(pair):
            kept, sent = [v.reshape(2, ROWS, *CROSS) for v in pair]
            both = jnp.stack([kept, sent], axis=1).reshape(QUADS, ROWS, *CROSS)
            return lax.psum_scatter(both.astype(F32), "row", scatter_dimension=1)

        second = jnp.concatenate([second_sum[0], sum_cross(cross_up)], axis=1)
        third = jnp.concatenate([third_sum[0], sum_cross(cross)], axis=1)
        grads = wide_sums(first_sum[0], second, third)
        joint_new = adamw(*joint, grads[0], JOINT_RATE, DECAY)
        output_new = adamw(*output, grads[1], OUTPUT_RATE, DECAY)
        up_new = adamw(*up, grads[2][:, None], JOINT_RATE, DECAY)
        down_new = adamw(*down, grads[3], DOWN_RATE, DECAY)
        vector_new = step_vectors(lax.psum(first_sum[1], "dp"))

    return (
        layer_out,
        tokens_grad,
        *[jnp.transpose(v, (2, 0, 1)) for v in joint_new],
        *[v.T[:, None] for v in output_new],
        *up_new,
        *[v.T[:, None] for v in down_new],
        *vector_new,
    )


def solution(mesh):
    first = P("row", "col", "dp")
    second = P("col", "row", "dp")
    tokens = P("dp", "row", None)
    weights = (first,) * 3 + (second,) * 3 + (first,) * 3 + (second,) * 3 + (P(),) * 3
    in_specs = (tokens, P(("dp", "row"))) + weights + (tokens,)
    out_specs = (tokens, tokens) + weights
    return jax.shard_map(
        per_device, mesh=mesh, in_specs=in_specs, out_specs=out_specs, check_vma=False
    )
```

```python
from functools import partial

import jax
import jax.numpy as jnp
from jax import lax
from jax.experimental import pallas as pl
from jax.experimental.pallas import tpu as pltpu
from jax.sharding import PartitionSpec as P

D = 768
H = 12
HD = 64
FF = 3072
LEN = 256
STEP = 10

NORM_EPS = 1e-12
BETA_ONE = 0.9
BETA_TWO = 0.999
ADAM_EPS = 1e-08
DECAY = 0.01
VECTOR_RATE = 0.2

F32 = jnp.float32
BF16 = jnp.bfloat16

ROWS = 4
QUADS = 4
W = D // ROWS
S = W // QUADS
COLS = D // 2
HEADS = COLS // HD
FFC = FF // 2
MIX = HEADS * 3 * HD
PAIRS = LEN // 2
CHUNK = (W, COLS)
PART = (3 * S, COLS)
CROSS = (S, COLS)
MIB = 1024 * 1024


def swap(value, axis, mask):
    n = lax.axis_size(axis)
    return lax.ppermute(value, axis, [(i, i ^ mask) for i in range(n)])


def shape(*dims, dtype=BF16):
    return jax.ShapeDtypeStruct(dims, dtype)


def run(kernel, where, args, outs, scratch=(), limit=8, after=(), fetch=False):
    vmem = pl.BlockSpec(memory_space=pltpu.VMEM)
    first, late = 1 + len(args), len(after)

    def body(*refs):
        kernel(*refs[:first], *refs[first + late :])

    out = pl.pallas_call(
        body,
        out_shape=outs,
        in_specs=[pl.BlockSpec(memory_space=pltpu.SMEM)]
        + [pl.BlockSpec(memory_space=pl.ANY) if fetch else vmem] * len(args)
        + [pl.BlockSpec(memory_space=pl.ANY)] * late,
        out_specs=[vmem] * len(outs),
        scratch_shapes=list(scratch),
        compiler_params=pltpu.CompilerParams(vmem_limit_bytes=limit * MIB),
    )(where, *args, *after)
    return list(out)


def dot(left, right, dims):
    return lax.dot_general(left, right, (dims, ((), ())), preferred_element_type=F32)


NN = ((1,), (0,))
NT = ((1,), (1,))
TN = ((0,), (0,))


def each(count, body):
    def step(i, carry):
        body(i)
        return carry

    lax.fori_loop(0, count, step, 0)


def row_of(vecs, start, count):
    return jnp.concatenate([vecs[start + i : start + i + 1, :] for i in range(count)], axis=1)


def vector_row(vecs, k):
    return row_of(vecs, 6 * k, 6)


def pick_col(where, left, right):
    return jnp.where(where[2] == 0, left, right)


def split_parts(value):
    high = value.astype(BF16)
    return high, (value - high.astype(F32)).astype(BF16)


def opening_kernel(where, tokens, grads, joint, output, down, *refs):
    outs, first = refs[:ROWS], refs[ROWS]
    tokens_in, grads_in, joint_in, output_in, down_in, done = refs[ROWS + 1 :]
    copies = [
        pltpu.make_async_copy(source, target, done.at[i])
        for i, (source, target) in enumerate(
            [
                (joint, joint_in),
                (output, output_in),
                (tokens, tokens_in),
                (grads, grads_in),
                (down.at[:, 3 * COLS :], down_in),
            ]
        )
    ]
    for copy in copies:
        copy.start()
    copies[0].wait()
    copies[1].wait()
    for h in range(HEADS // 2):
        pair = [joint_in[h].astype(BF16), joint_in[h + HEADS // 2].astype(BF16)]
        first[h * S : (h + 1) * S, :] = jnp.concatenate(pair, axis=1)
    first[HEADS // 2 * S :, :] = output_in[...].astype(BF16)
    copies[2].wait()
    copies[3].wait()
    copies[4].wait()
    for m, out in enumerate(outs):
        out[0:PAIRS, :] = tokens_in[where[0] ^ m]
        out[PAIRS:LEN, :] = grads_in[where[0] ^ m]
        out[LEN:, :] = down_in[...].astype(BF16)


def second_shard_kernel(where, up, second):
    for q in range(3):
        second[:, q * 128 : (q + 1) * 128] = up[pl.ds(q, W, stride=3), :].astype(BF16)


def third_shard_kernel(where, down, third):
    for q in range(3):
        third[q * S : (q + 1) * S, :] = down[:, q * COLS : (q + 1) * COLS].astype(BF16)


def pair_kernel(where, b0, b1, pair):
    pair[0] = b0[...]
    pair[1] = b1[...]


def cross_kernel(where, t0, t1, t2, t3, plane):
    for m, piece in enumerate([t0, t1, t2, t3]):
        plane[m] = piece[LEN:, :]


def planes_kernel(where, b0, b1, planes):
    planes[0:ROWS] = b0[...]
    planes[ROWS:] = b1[...]


def whole_kernel(where, *refs):
    *pieces, line = refs
    for k in range(QUADS):
        line[k] = pieces[k][...] if len(pieces) == QUADS else pieces[k // 2][k % 2]


def halves_kernel(where, from_x, from_y, near_y, far_x):
    near_y[...] = from_y[0:2]
    far_x[...] = from_x[2:4]


def token_kernel(where, tokens, grads, *outs):
    for m, out in enumerate(outs):
        out[0:PAIRS, :] = tokens[where[0] ^ m]
        out[PAIRS:LEN, :] = grads[where[0] ^ m]


ORDER = (0, 2, 1, 3)


def blocks(where, pieces):
    found = [(piece, i) for piece in pieces for i in range(piece.shape[0])]
    for at, (piece, i) in enumerate(found):
        yield where[0] ^ (at // QUADS), where[1] ^ ORDER[at % QUADS], piece[i]


def cross_blocks(where, pieces):
    for j, piece in enumerate(pieces):
        for i in range(2 * ROWS):
            yield where[0] ^ (i % ROWS), where[1] ^ ORDER[2 * j + i // ROWS], piece[i]


def unpack_tokens(x):
    parts = [jnp.concatenate([x[r][:, :W], x[r][:, W:]], axis=0) for r in range(ROWS)]
    return jnp.concatenate(parts, axis=1)


def pack_tokens(value, room, k):
    for r in range(ROWS):
        both = value[:, r * W : (r + 1) * W]
        packed = jnp.concatenate([both[:PAIRS], both[PAIRS:]], axis=1).astype(BF16)
        room[r, k * PAIRS : (k + 1) * PAIRS, :] = packed


def attend_kernel(where, t0, t1, t2, t3, vecs, *refs):
    pieces, refs = refs[:5], refs[5:]
    tokens, grads, wj, wo, mixed, probs, attended, part, room, mixing, scores, parts = refs
    for m, piece in enumerate([t0, t1, t2, t3]):
        room[where[0] ^ m] = piece[0:LEN, :]
    tokens[...] = unpack_tokens([room[r, 0:PAIRS, :] for r in range(ROWS)])
    grads[...] = unpack_tokens([room[r, PAIRS:, :] for r in range(ROWS)])
    half = HEADS // 2
    for row, quad, value in blocks(where, pieces):
        for h in range(half):
            rows = value[h * S : (h + 1) * S, :]
            for k, cut in enumerate([rows[:, :W], rows[:, W:]]):
                start = pl.multiple_of((h + k * half) * 3 * HD + quad * S, 16)
                wj[row, pl.ds(start, S), :] = cut
        start = pl.multiple_of(row * W + quad * S, 16)
        wo[pl.ds(start, S), :] = value[half * S :, :]
    total = dot(wj[0], tokens[:, :W], NT)
    for r in range(1, ROWS):
        total = total + dot(wj[r], tokens[:, r * W : (r + 1) * W], NT)
    mixing[...] = total
    query_bias, value_bias = [
        pick_col(where, row_of(vecs, start, 3), row_of(vecs, start + 3, 3)) for start in (0, 6)
    ]
    zero = jnp.zeros((1, HD), F32)
    row = []
    for h in range(HEADS):
        at = slice(h * HD, (h + 1) * HD)
        row += [query_bias[:, at], zero, value_bias[:, at]]
    row = jnp.concatenate(row, axis=1)
    high, low = split_parts(row)
    rest = (row - high.astype(F32) - low.astype(F32)).astype(BF16)
    parts[...] = jnp.zeros_like(parts)
    parts[0:1, :] = high.astype(F32)
    parts[1:2, :] = low.astype(F32)
    parts[2:3, :] = rest.astype(F32)
    bias = dot(parts[...].astype(BF16), jnp.ones((8, LEN), BF16), TN)
    mixed[...] = (mixing[...] + bias).astype(BF16)
    slot = lax.broadcasted_iota(jnp.int32, (LEN, 1), 0)
    slot = jnp.where(slot < PAIRS, 2 * slot, 2 * (slot - PAIRS) + 1)
    valid = slot < where[3]
    for h in range(HEADS):
        base = h * 3 * HD
        query, keyed, valued = [mixed[base + k * HD : base + (k + 1) * HD, :] for k in range(3)]
        scores[...] = dot(keyed, query, TN)
        for q in range(2):
            at = slice(q * 128, (q + 1) * 128)
            score = jnp.where(valid, scores[:, at] * 0.125, -1e30)
            expo = jnp.exp(score - jnp.max(score, axis=0, keepdims=True))
            prob = expo * (1.0 / jnp.sum(expo, axis=0, keepdims=True))
            probs[h, :, at] = prob.astype(BF16)
        attended[h * HD : (h + 1) * HD, :] = dot(valued, probs[h], NN).astype(BF16)
    part[...] = dot(attended[...], wo[...], ((0,), (1,))).astype(BF16)


def norm_rows(resid, gain, shift_by):
    mean = jnp.sum(resid, axis=1, keepdims=True) * (1.0 / D)
    var = jnp.sum(resid * resid, axis=1, keepdims=True) * (1.0 / D) - mean * mean
    inverse = lax.rsqrt(var + NORM_EPS)
    normed = (resid - mean) * inverse
    return normed * gain + shift_by, normed, inverse


def norm_back_rows(grad, normed, inverse, gain):
    scaled = grad * gain
    total = jnp.sum(scaled, axis=1, keepdims=True) * (1.0 / D)
    cross = jnp.sum(scaled * normed, axis=1, keepdims=True) * (1.0 / D)
    return (scaled - total - normed * cross) * inverse


STRIP = 32


def strip(i):
    return pl.ds(pl.multiple_of(i * STRIP, STRIP), STRIP)


def up_kernel(where, tokens, p0, p1, vecs, *refs):
    pieces, refs = refs[:5], refs[5:]
    hidden, low, normed, inverse, act, slope, wu, pre = refs
    for row, quad, value in blocks(where, pieces):
        rows = pl.ds(pl.multiple_of(row * W, W), W)
        wu[rows, pl.ds(pl.multiple_of(quad * COLS, COLS), COLS)] = value

    bias_out, gain, shift_by = [vector_row(vecs, k) for k in (2, 3, 4)]

    def first(i):
        at = strip(i)
        resid = tokens[at, :].astype(F32) + (p0[at, :].astype(F32) + p1[at, :].astype(F32))
        out, unit, scale = norm_rows(resid + bias_out, gain, shift_by)
        hidden[at, :] = out
        low[at, :] = out.astype(BF16)
        normed[at, :] = unit
        inverse[at, :] = scale

    each(LEN // STRIP, first)
    pre[...] = dot(low[...], wu[...], NN)
    bias = pick_col(where, row_of(vecs, 48, 12), row_of(vecs, 60, 12))
    for q in range(4):
        cols = slice(q * COLS, (q + 1) * COLS)
        shift_up = bias[:, cols]

        def second(i, cols=cols, shift_up=shift_up):
            at = (strip(i), cols)
            value = pre[at] + shift_up
            phi = 0.5 * (1.0 + lax.erf(value * (0.5**0.5)))
            density = jnp.exp(-0.5 * value * value) * 0.3989422804014327
            act[at] = (value * phi).astype(BF16)
            slope[at] = phi + value * density

        each(LEN // STRIP, second)


def down_kernel(where, act, *refs):
    pieces, cross, wd, part = refs[:5], refs[5:7], refs[7], refs[8]
    for row, quad, value in blocks(where, pieces):
        rows = pl.ds(pl.multiple_of(row * W + quad * S, 16), S)
        for q in range(3):
            wd[rows, q * COLS : (q + 1) * COLS] = value[q * S : (q + 1) * S, :]
    for row, quad, value in cross_blocks(where, cross):
        rows = pl.ds(pl.multiple_of(row * W + quad * S, 16), S)
        wd[rows, 3 * COLS :] = value
    part[...] = dot(act[...], wd[...], NT).astype(BF16)


def hand_out(where, room, outs):
    r = where[0]
    to_x, to_y, last_x, last_y, own = outs
    to_x[0:2] = room[r ^ 3, 0:2]
    to_x[2:4] = room[r ^ 1, 0:2]
    to_y[0:2] = room[r ^ 3, 2:4]
    to_y[2:4] = room[r ^ 2, 2:4]
    last_x[...] = room[r ^ 1, 2:4]
    last_y[...] = room[r ^ 2, 0:2]
    own[...] = room[r]


def handed_shapes(block):
    pair, line = shape(2, *block), shape(4, *block)
    return [line] * 2 + [pair] * 2 + [line]


HANDED = handed_shapes(CHUNK)
PAIR = shape(2, *CHUNK)
PLANES = shape(2 * ROWS, *CROSS)

VROWS = 32
VECTOR = (VROWS, COLS)
CARRIED = (2 * W + 2 * VROWS, COLS)

LATE_X = 4 * W + 2 * VROWS
LATE_Y = 4 * W
FIRST_X = (LATE_X + 2 * PART[0], COLS)
FIRST_Y = (LATE_Y + 2 * PART[0], COLS)


def put_vector(out, start, value):
    high, low = split_parts(value)
    out[start : start + VROWS, :] = high
    out[start + VROWS : start + 2 * VROWS, :] = low


def get_vector(value, start):
    high = value[start : start + VROWS, :].astype(F32)
    return high + value[start + VROWS : start + 2 * VROWS, :].astype(F32)


def second_norm_kernel(where, hidden, p0, p1, vecs, grads, act, *refs):
    (result, low, grad_two, sums), handed = refs[:4], refs[4:9]
    cross_own, cross_send, room, cross = refs[9:]
    sums[...] = jnp.zeros_like(sums)
    bias_down, gain, shift_by = [vector_row(vecs, k) for k in (5, 6, 7)]

    def body(i):
        at = strip(i)
        resid = hidden[at, :] + (p0[at, :].astype(F32) + p1[at, :].astype(F32)) + bias_down
        out, unit, scale = norm_rows(resid, gain, shift_by)
        result[at, :] = out
        grad = grads[at, :].astype(F32)
        back = norm_back_rows(grad, unit, scale, gain)
        grad_two[at, :] = back
        rounded = back.astype(BF16)
        low[at, :] = rounded
        sums[0:1, :] += jnp.sum(rounded.astype(F32), axis=0, keepdims=True)
        sums[1:2, :] += jnp.sum(grad * unit, axis=0, keepdims=True)
        sums[2:3, :] += jnp.sum(grad, axis=0, keepdims=True)

    each(LEN // STRIP, body)
    for q in range(4):
        cols = slice(q * COLS, (q + 1) * COLS)
        grad = dot(low[...], act[:, cols], TN).astype(BF16)
        for r in range(ROWS):
            for z in range(QUADS):
                start = r * W + z * S
                if q < 3:
                    room[r, z, q * S : (q + 1) * S, :] = grad[start : start + S, :]
                else:
                    cross[z, r] = grad[start : start + S, :]
    hand_out(where, room, handed)
    hand_cross(where, cross, cross_own, cross_send)


def hidden_back_kernel(where, low, slope, wd, wu, grad_pre, part, sums, back):
    back[...] = dot(low[...], wd[...], NN)
    sums[...] = jnp.zeros_like(sums)
    for q in range(4):
        cols = slice(q * COLS, (q + 1) * COLS)

        def body(i, cols=cols):
            at = (strip(i), cols)
            value = (back[at] * slope[at]).astype(BF16)
            grad_pre[at] = value
            sums[0:1, cols] += jnp.sum(value.astype(F32), axis=0, keepdims=True)

        each(LEN // STRIP, body)
    part[...] = dot(grad_pre[...], wu[...], NT).astype(BF16)


def hand_cross(where, cross, own, send):
    for k, mask in enumerate([0, 2]):
        rows = slice(k * ROWS, (k + 1) * ROWS)
        own[rows] = cross[where[1] ^ mask]
        send[rows] = cross[where[1] ^ mask ^ 1]


def up_grad_kernel(where, low, grad_pre, *refs):
    handed, (cross_own, cross_send, room, cross) = refs[:5], refs[5:]
    for z in range(QUADS):
        grad = dot(low[...], grad_pre[:, z * COLS : (z + 1) * COLS], TN).astype(BF16)
        for r in range(ROWS):
            room[r, z] = grad[r * W : r * W + PART[0], :]
            cross[z, r] = grad[r * W + PART[0] : (r + 1) * W, :]
    hand_out(where, room, handed)
    hand_cross(where, cross, cross_own, cross_send)


def first_norm_kernel(
    where, grad_two, p0, p1, normed, inverse, vecs, wo, mixed, probs, *refs
):
    grad_one, grad_mixed, low, sums, back, inner, scores = refs
    sums[...] = jnp.zeros_like(sums)
    gain = vector_row(vecs, 3)

    def body(i):
        at = strip(i)
        grad = grad_two[at, :] + (p0[at, :].astype(F32) + p1[at, :].astype(F32))
        unit = normed[at, :]
        out = norm_back_rows(grad, unit, inverse[at, :], gain)
        grad_one[at, :] = out
        rounded = out.astype(BF16)
        low[at, :] = rounded
        sums[0:1, :] += jnp.sum(rounded.astype(F32), axis=0, keepdims=True)
        sums[1:2, :] += jnp.sum(grad * unit, axis=0, keepdims=True)
        sums[2:3, :] += jnp.sum(grad, axis=0, keepdims=True)

    each(LEN // STRIP, body)
    back[...] = dot(wo[...], low[...], ((0,), (1,))).astype(BF16)
    for h in range(HEADS):
        base = h * 3 * HD
        query, keyed, valued = [mixed[base + k * HD : base + (k + 1) * HD, :] for k in range(3)]
        grad_out = back[h * HD : (h + 1) * HD, :]
        inner[...] = dot(valued, grad_out, TN)
        for q in range(2):
            at = slice(q * 128, (q + 1) * 128)
            prob = probs[h, :, at].astype(F32)
            grad = inner[:, at]
            mean = jnp.sum(grad * prob, axis=0, keepdims=True)
            scores[:, at] = (prob * (grad - mean)).astype(BF16)
        grads = [
            dot(keyed, scores[...], NN) * 0.125,
            dot(query, scores[...], NT) * 0.125,
            dot(grad_out, probs[h], NT),
        ]
        for k, grad in enumerate(grads):
            grad_mixed[base + k * HD : base + (k + 1) * HD, :] = grad.astype(BF16)


def first_grad_kernel(where, grad_mixed, low, sums, attended, tokens, sums_two, sums_up, *refs):
    vector, room = refs
    half = HEADS // 2
    for r in range(ROWS):
        cut = tokens[:, r * W : (r + 1) * W]
        grad = dot(grad_mixed[...], cut, NN).astype(BF16)
        for z in range(QUADS):
            for h in range(half):
                starts = [(h + k * half) * 3 * HD + z * S for k in range(2)]
                pair = [grad[start : start + S, :] for start in starts]
                room[r, z, h * S : (h + 1) * S, :] = jnp.concatenate(pair, axis=1)
        grad = dot(low[:, r * W : (r + 1) * W], attended[...], ((0,), (1,))).astype(BF16)
        for z in range(QUADS):
            room[r, z, half * S :, :] = grad[z * S : (z + 1) * S, :]
    left = jnp.where(where[2] == 0, 1.0, 0.0)
    right = 1.0 - left
    total = dot(jnp.ones((8, LEN), BF16), grad_mixed[...], NT)[0:1, :]
    vector[...] = jnp.zeros_like(vector)
    for k, start in enumerate([0, 2 * HD]):
        at = [h * 3 * HD + start for h in range(HEADS)]
        row = jnp.concatenate([total[:, i : i + HD] for i in at], axis=1)
        vector[2 * k : 2 * k + 1, :] = row * left
        vector[2 * k + 1 : 2 * k + 2, :] = row * right
    for k, found in enumerate([sums, sums_two]):
        for i in range(3):
            for j in range(2):
                row = 4 + 6 * k + 2 * i + j
                vector[row : row + 1, :] = found[i : i + 1, j * COLS : (j + 1) * COLS] * left
    for j in range(4):
        row = sums_up[0:1, j * COLS : (j + 1) * COLS]
        vector[16 + j : 17 + j, :] = row * left
        vector[20 + j : 21 + j, :] = row * right


def first_hand_kernel(where, room, vector, late_x, late_y, to_x, to_y, last_x, last_y, own):
    r = where[0]
    for k in range(2):
        far, near = slice(k * W, (k + 1) * W), slice((2 + k) * W, (3 + k) * W)
        to_x[far, :] = room[r ^ 3, k]
        to_x[near, :] = room[r ^ 1, k]
        to_y[far, :] = room[r ^ 3, 2 + k]
        to_y[near, :] = room[r ^ 2, 2 + k]
        for start, out, late in [(LATE_X, to_x, late_x), (LATE_Y, to_y, late_y)]:
            at = start + k * PART[0]
            out[at : at + PART[0], :] = late[k]
    last_x[...] = room[r ^ 1, 2:4]
    last_y[...] = room[r ^ 2, 0:2]
    own[...] = room[r]
    put_vector(to_x, 4 * W, vector[...])


def token_back_kernel(where, grad_mixed, wj, part):
    for r in range(ROWS):
        part[:, r * W : (r + 1) * W] = dot(grad_mixed[...], wj[r], TN).astype(BF16)


def token_sum_kernel(where, result, grad_one, p0, p1, *refs):
    total, room = refs[-2:]
    count = (len(refs) - 6) // 3
    sums, outs, owns = refs[: 2 * count], refs[2 * count : 2 * count + 4], refs[2 * count + 4 : -2]

    def body(i):
        at = strip(i)
        total[at, :] = grad_one[at, :] + (p0[at, :].astype(F32) + p1[at, :].astype(F32))

    each(LEN // STRIP, body)
    pack_tokens(result, room, 0)
    pack_tokens(total, room, 1)
    for m, out in enumerate(outs):
        row = where[0] ^ m
        out[0:LEN, :] = room[row]
        for i, own in enumerate(owns):
            block = sums[2 * i][row] + sums[2 * i + 1][row].astype(F32)
            out[LEN + i * S : LEN + (i + 1) * S, :] = block.astype(BF16)
            if m == 0:
                own[...] = block


def token_out_kernel(where, t0, t1, t2, t3, result, total):
    for m, piece in enumerate([t0, t1, t2, t3]):
        for k, out in enumerate([result, total]):
            for q in range(3):
                value = piece[k * PAIRS : (k + 1) * PAIRS, q * 128 : (q + 1) * 128].astype(F32)
                out[where[0] ^ m, pl.ds(q, PAIRS, stride=3), :] = value


def pass_kernel(where, last_x, last_y, from_x, from_y, to_x, to_y):
    to_x[...] = (last_x[...].astype(F32) + from_y[0:2].astype(F32)).astype(BF16)
    to_y[...] = (last_y[...].astype(F32) + from_x[0:2].astype(F32)).astype(BF16)


def carry_pass_kernel(where, last_x, last_y, carried, from_x, from_y, to_x, to_y):
    for k in range(2):
        rows = slice(k * W, (k + 1) * W)
        to_x[k] = (last_x[k].astype(F32) + from_y[rows, :].astype(F32)).astype(BF16)
        to_y[rows, :] = (last_y[k].astype(F32) + from_x[rows, :].astype(F32)).astype(BF16)
    put_vector(to_y, 2 * W, get_vector(carried, 4 * W) + get_vector(from_x, 4 * W))


def add_plane(own, from_x, from_y, last_x, last_y, room):
    for k in range(2):
        room[k] = (own[k].astype(F32) + from_x(k)) + last_y(k)
        room[2 + k] = (own[2 + k].astype(F32) + from_y(k)) + last_x(k)


def kept_blocks(ref):
    skip = ref.shape[0] - 2
    return lambda k: ref[skip + k].astype(F32)


def kept_rows(ref, start, rows=W):
    return lambda k: ref[start + k * rows : start + (k + 1) * rows, :].astype(F32)


def line_kernel(where, own, from_x, from_y, last_x, last_y, kept, *refs):
    *sends, room = refs
    add_plane(own, *[kept_blocks(v) for v in (from_x, from_y, last_x, last_y)], room)
    if sends:
        kept[...] = room[where[1]]
        for mask, send in zip(ORDER[1:], sends):
            send[...] = room[where[1] ^ mask].astype(BF16)
    else:
        kept[...] = room[...]


def near_line_kernel(where, own, from_x, from_y, late_x, late_y, kept, *refs):
    *sends, room = refs
    late = [kept_rows(late_x, LATE_X, PART[0]), kept_rows(late_y, LATE_Y, PART[0])]
    add_plane(own, kept_blocks(from_x), kept_blocks(from_y), *late, room)
    if sends:
        for k, mask in enumerate([0, 2]):
            kept[k] = room[where[1] ^ mask]
            sends[0][k] = room[where[1] ^ mask ^ 1].astype(BF16)
    else:
        kept[...] = room[...]


def far_line_kernel(where, kept, got, total, send):
    total[...] = kept[0] + got[0].astype(F32)
    send[...] = (kept[1] + got[1].astype(F32)).astype(BF16)


def cross_far_kernel(where, own, got, kept, send):
    kept[...] = own[0:ROWS].astype(F32) + got[0:ROWS].astype(F32)
    send[...] = (own[ROWS:].astype(F32) + got[ROWS:].astype(F32)).astype(BF16)


def carry_near_kernel(where, own, first_x, first_y, last_x, from_y, passed, kept, *refs):
    *sends, room = refs
    near = [kept_rows(first_x, 2 * W), kept_rows(first_y, 2 * W)]
    add_plane(own, *near, kept_blocks(last_x), kept_rows(from_y, 0), room)
    vector = get_vector(passed, 2 * W) + get_vector(from_y, 2 * W)
    if kept.ndim == 2:
        for k, mask in enumerate([0, 2]):
            rows = slice(k * W, (k + 1) * W)
            kept[rows, :] = room[where[1] ^ mask]
            sends[0][rows, :] = room[where[1] ^ mask ^ 1].astype(BF16)
        kept[2 * W :, :] = vector
        put_vector(sends[0], 2 * W, vector)
    else:
        kept[...] = room[...]
        sends[0][...] = vector


def add_vector(own, got, start):
    high, low = split_parts(own)
    return (high.astype(F32) + low.astype(F32)) + get_vector(got, start)


def carry_far_kernel(where, kept, got, total, send):
    total[0:W, :] = kept[0:W, :] + got[0:W, :].astype(F32)
    send[0:W, :] = (kept[W : 2 * W, :] + got[W : 2 * W, :].astype(F32)).astype(BF16)
    vector = add_vector(kept[2 * W :, :], got, 2 * W)
    total[W:, :] = vector
    put_vector(send, W, vector)


def adamw(weight, first, second, grad, rate, decay):
    first_new = BETA_ONE * first + (1.0 - BETA_ONE) * grad
    second_new = BETA_TWO * second + (1.0 - BETA_TWO) * grad * grad
    fix_one = 1.0 - BETA_ONE**STEP
    fix_two = 1.0 - BETA_TWO**STEP
    update = first_new / fix_one / (jnp.sqrt(second_new / fix_two) + ADAM_EPS) + decay * weight
    return (first_new, second_new, weight - rate * update)


JOINT_RATE = D ** (-0.5)
OUTPUT_RATE = (4 * D // LEN) ** (-0.5)
DOWN_RATE = FF ** (-0.5)


def first_adam_kernel(where, kept, got, jw, jf, js, ow, of, os, *refs):
    outs, vector = refs[:6], refs[6]
    grad = kept[0:W, :] + got[0:W, :].astype(F32)
    half = HEADS // 2
    for h in range(HEADS):
        rows = grad[h % half * S : (h % half + 1) * S, :]
        cut = rows[:, :W] if h < half else rows[:, W:]
        new = adamw(jw[h], jf[h], js[h], cut, JOINT_RATE, DECAY)
        for out, value in zip(outs[:3], new):
            out[h] = value
    new = adamw(ow[...], of[...], os[...], grad[half * S :, :], OUTPUT_RATE, DECAY)
    for out, value in zip(outs[3:], new):
        out[...] = value
    vector[...] = add_vector(kept[W:, :], got, W)


def vector_adam_kernel(where, mine, other, weight, first, second, *refs):
    outs, grad = refs[:3], refs[3]
    total = mine[...] + other[...]
    for q in range(3):
        grad[pl.ds(q, 24, stride=3), :] = total[0:24, q * 128 : (q + 1) * 128]
    new = adamw(weight[...], first[...], second[...], grad[...], VECTOR_RATE, 0.0)
    for out, value in zip(outs, new):
        out[...] = value


def sum_rows(own, r1, r2, r3, start):
    rows = slice(start, start + S)
    far = r2[rows, :].astype(F32) + r3[rows, :].astype(F32)
    return (own[...] + r1[rows, :].astype(F32)) + far


def up_adam_kernel(where, kept, r2, r1, r3, own, c1, c2, c3, w, f, s, *outs):
    grad = (kept[...] + r1[...].astype(F32)) + (r2[...].astype(F32) + r3[...].astype(F32))
    grad = jnp.concatenate([grad, sum_rows(own, c1, c2, c3, LEN + S)], axis=0)
    for q in range(3):
        at = (pl.ds(q, W, stride=3), slice(None))
        cut = grad[:, q * 128 : (q + 1) * 128]
        for out, value in zip(outs, adamw(w[at], f[at], s[at], cut, JOINT_RATE, DECAY)):
            out[at] = value


def down_adam_kernel(where, kept, got, own, r1, r2, r3, w, f, s, *outs):
    cross = sum_rows(own, r1, r2, r3, LEN)
    most = kept[...] + got[...].astype(F32)
    for q in range(4):
        at = (slice(None), slice(q * COLS, (q + 1) * COLS))
        cut = most[q * S : (q + 1) * S, :] if q < 3 else cross
        for out, value in zip(outs, adamw(w[at], f[at], s[at], cut, DOWN_RATE, DECAY)):
            out[at] = value


def gather_line(where, shard, steps):
    if steps == 1:
        return [shard] + [swap(shard, "dp", mask) for mask in ORDER[1:]]
    pair = [shape(2, *shard.shape)]
    pair = run(pair_kernel, where, [shard, swap(shard, "dp", 2)], pair)[0]
    return [pair, swap(pair, "dp", 1)]


def gather_plane(where, line, after=()):
    block = line[0].shape[-2:]
    line = run(whole_kernel, where, line, [shape(4, *block)], after=after)[0]
    from_x = swap(line, "row", 1)
    from_y = swap(line, "row", 2)
    near_y, far_x = run(halves_kernel, where, [from_x, from_y], [shape(2, *block)] * 2)
    return [line, from_x, from_y, swap(near_y, "row", 1), swap(far_x, "row", 2)]


def gather_cross(where, plane):
    planes = run(planes_kernel, where, [plane, swap(plane, "dp", 2)], [PLANES])[0]
    return [planes, swap(planes, "dp", 1)]


def scatter_first(handed):
    return [swap(value, "row", 1 + i % 2) for i, value in enumerate(handed[:-3])]


def scatter_pass(where, handed, got, after=()):
    pair = [shape(*handed[2].shape)] * 2
    return run(pass_kernel, where, handed[2:4] + got, pair, after=after)


def scatter_second(passed):
    return [swap(passed[0], "row", 1), swap(passed[1], "row", 2)]


def exchange(pieces):
    return [pieces[0]] + [swap(pieces[m], "row", m) for m in range(1, ROWS)]


def wide_lines(joint, output, up, down):
    order = jnp.array(ORDER)
    n = lax.axis_size("dp") // QUADS

    def collect(shard, axis):
        whole = lax.all_gather(shard.astype(BF16), "dp", axis=axis, tiled=True)
        return jnp.stack(jnp.split(whole, QUADS, axis=axis))

    joint = collect(joint, 1)
    half = HEADS // 2
    pair = joint.reshape(QUADS, 2, half, S, W)
    pair = jnp.transpose(pair, (0, 2, 3, 1, 4)).reshape(QUADS, half * S, 2 * W)
    first = jnp.concatenate([pair, collect(output, 0)], axis=1)
    second = collect(up, 1)
    third = collect(down, 0).reshape(QUADS, S, 4, COLS)
    third = jnp.transpose(third, (0, 2, 1, 3)).reshape(QUADS, W, COLS)
    return [jnp.take(value, order, axis=0) for value in (first, second, third)]


def wide_sums(first, second, third):
    def give(value, axis):
        whole = jnp.concatenate(list(value), axis=axis)
        return lax.psum_scatter(whole, "dp", scatter_dimension=axis, tiled=True)

    half = HEADS // 2
    pair = first[:, : half * S].reshape(QUADS, half, S, 2, W)
    joint = jnp.transpose(pair, (0, 3, 1, 2, 4)).reshape(QUADS, HEADS, S, W)
    third = jnp.transpose(third.reshape(QUADS, 4, S, COLS), (0, 2, 1, 3))
    third = third.reshape(QUADS, S, FFC)
    return give(joint, 1), give(first[:, half * S :], 0), give(second, 1), give(third, 0)


def per_device(
    tokens_in,
    lengths,
    joint_weight,
    joint_first,
    joint_second,
    output_weight,
    output_first,
    output_second,
    up_weight,
    up_first,
    up_second,
    down_weight,
    down_first,
    down_second,
    vectors,
    vector_first,
    vector_second,
    out_grad,
):
    r = lax.axis_index("row")
    col = lax.axis_index("col")
    direct = lax.axis_size("dp") == QUADS
    z = lax.axis_index("dp") if direct else jnp.int32(0)
    where = jnp.stack([r, z, col, lengths[0]]).astype(jnp.int32)

    joint = [jnp.transpose(v, (1, 2, 0)) for v in (joint_weight, joint_first, joint_second)]
    output = [v[:, 0].T for v in (output_weight, output_first, output_second)]
    down = [v[:, 0].T for v in (down_weight, down_first, down_second)]
    up = [up_weight, up_first, up_second]
    flat = up_weight.size // 128

    sent = [tokens_in.reshape(ROWS, PAIRS, 2 * W), out_grad.reshape(ROWS, PAIRS, 2 * W)]
    blocks_out = [shape(LEN + S if direct else LEN, 2 * W)] * ROWS
    if direct:
        up = [v.reshape(flat, 128) for v in up]
        one = [shape(*CHUNK)]
        *pieces, first = run(
            opening_kernel,
            where,
            sent + [joint[0], output[0], down[0]],
            blocks_out + one,
            [
                pltpu.VMEM(sent[0].shape, BF16),
                pltpu.VMEM(sent[1].shape, BF16),
                pltpu.VMEM(joint[0].shape, F32),
                pltpu.VMEM(output[0].shape, F32),
                pltpu.VMEM(CROSS, F32),
                pltpu.SemaphoreType.DMA((5,)),
            ],
            limit=56,
            fetch=True,
        )
        tokens_pieces = exchange(pieces)
        first = gather_line(where, first, 1)
        first_pieces = gather_plane(where, first, tokens_pieces[1:])
        shard = run(second_shard_kernel, where, [up[0]], one, after=first[1:])[0]
        second = gather_line(where, shard, 2)
        plane = run(cross_kernel, where, tokens_pieces, [shape(ROWS, *CROSS)])[0]
        cross = gather_cross(where, plane)
        second_pieces = gather_plane(where, second)
        after = second_pieces[:1] + cross[:1]
        shard = run(third_shard_kernel, where, [down[0]], [shape(*PART)], after=after)[0]
        third = gather_line(where, shard, 2)
        third_pieces = gather_plane(where, third, first_pieces[3:])
        third_pieces += cross
    else:
        tokens_pieces = exchange(run(token_kernel, where, sent, blocks_out))
        lines = wide_lines(joint[0], output[0], up_weight[:, 0], down[0])
        cross = lines[2][:, 3 * S :]
        lines[2] = lines[2][:, : 3 * S]
        first_pieces, second_pieces, third_pieces = [
            gather_plane(where, list(line)) for line in lines
        ]
        cross = jnp.stack([cross] + [swap(cross, "row", m) for m in range(1, ROWS)], axis=1)
        third_pieces += list(cross.reshape(2, *PLANES.shape))

    vecs = vectors.reshape(72, 128)
    tokens, grads, wj, wo, mixed, probs, attended, part = run(
        attend_kernel,
        where,
        tokens_pieces + [vecs] + first_pieces,
        [
            shape(LEN, D),
            shape(LEN, D),
            shape(ROWS, MIX, W),
            shape(D, COLS),
            shape(MIX, LEN),
            shape(HEADS, LEN, LEN),
            shape(COLS, LEN),
            shape(LEN, D),
        ],
        [
            pltpu.VMEM((ROWS, LEN, 2 * W), BF16),
            pltpu.VMEM((MIX, LEN), F32),
            pltpu.VMEM((LEN, LEN), F32),
            pltpu.VMEM((8, MIX), F32),
        ],
    )
    hidden, hidden_low, normed, inverse, act, slope, wu = run(
        up_kernel,
        where,
        [tokens, part, swap(part, "col", 1), vecs] + second_pieces,
        [
            shape(LEN, D, dtype=F32),
            shape(LEN, D),
            shape(LEN, D, dtype=F32),
            shape(LEN, 1, dtype=F32),
            shape(LEN, FFC),
            shape(LEN, FFC, dtype=F32),
            shape(D, FFC),
        ],
        [pltpu.VMEM((LEN, FFC), F32)],
        after=third_pieces[6:],
    )
    wd, part = run(
        down_kernel, where, [act] + third_pieces, [shape(D, FFC), shape(LEN, D)]
    )
    out = run(
        second_norm_kernel,
        where,
        [hidden, part, swap(part, "col", 1), vecs, grads, act],
        [shape(LEN, D, dtype=F32), shape(LEN, D), shape(LEN, D, dtype=F32)]
        + [shape(8, D, dtype=F32)]
        + handed_shapes(PART)
        + [PLANES] * 2,
        [
            pltpu.VMEM((ROWS, QUADS) + PART, BF16),
            pltpu.VMEM((QUADS, ROWS) + CROSS, BF16),
        ],
    )
    (result, grad_low, grad_two, sums_two), third_handed, cross = out[:4], out[4:9], out[9:]
    third_got = scatter_first(third_handed)
    grad_pre, part, sums_up = run(
        hidden_back_kernel,
        where,
        [grad_low, slope, wd, wu],
        [shape(LEN, FFC), shape(LEN, D), shape(8, FFC, dtype=F32)],
        [pltpu.VMEM((LEN, FFC), F32)],
    )
    third_passed = scatter_pass(where, third_handed, third_got)
    rooms = [
        pltpu.VMEM((ROWS, QUADS) + PART, BF16),
        pltpu.VMEM((QUADS, ROWS) + CROSS, BF16),
    ]
    out = run(
        up_grad_kernel,
        where,
        [hidden_low, grad_pre],
        handed_shapes(PART) + [PLANES] * 2,
        rooms,
    )
    second_handed, cross_up = out[:5], out[5:]
    grad_one, grad_mixed, low, sums_one = run(
        first_norm_kernel,
        where,
        [
            grad_two,
            part,
            swap(part, "col", 1),
            normed,
            inverse,
            vecs,
            wo,
            mixed,
            probs,
        ],
        [
            shape(LEN, D, dtype=F32),
            shape(MIX, LEN),
            shape(LEN, D),
            shape(8, D, dtype=F32),
        ],
        [
            pltpu.VMEM((COLS, LEN), BF16),
            pltpu.VMEM((LEN, LEN), F32),
            pltpu.VMEM((LEN, LEN), BF16),
        ],
    )
    vector, room = run(
        first_grad_kernel,
        where,
        [grad_mixed, low, sums_one, attended, tokens, sums_two, sums_up],
        [shape(*VECTOR, dtype=F32), shape(ROWS, QUADS, *CHUNK)],
    )
    cross_got = [swap(cross[1], "dp", 1)] if direct else []
    first_handed = run(
        first_hand_kernel,
        where,
        [room, vector] + third_passed,
        [shape(*FIRST_X), shape(*FIRST_Y)] + HANDED[2:],
        after=cross_got,
    )
    first_got = scatter_first(first_handed)

    def like(values):
        return [shape(*v.shape, dtype=F32) for v in values]

    def sums(dims, split):
        return [shape(*dims, dtype=F32), shape(*split)]

    cross_sum = []
    if direct:
        plane = (ROWS,) + CROSS
        for own, got in [(cross[0], cross_got[0]), (cross_up[0], swap(cross_up[1], "dp", 1))]:
            near = run(cross_far_kernel, where, [own, got], sums(plane, plane))
            cross_sum += [near[0], swap(near[1], "dp", 2)]
    (part,) = run(
        token_back_kernel, where, [grad_mixed, wj], [shape(LEN, D)], after=first_got
    )
    other = swap(part, "col", 1)
    first_passed = run(
        carry_pass_kernel,
        where,
        first_handed[2:4] + first_handed[:1] + first_got,
        [PAIR, shape(*CARRIED)],
        after=cross_sum[1:2],
    )
    first_last = scatter_second(first_passed)

    lines = [pltpu.VMEM((4,) + CHUNK, F32)]
    wide = [shape(4, *CHUNK, dtype=F32)]
    third_sum = run(
        near_line_kernel,
        where,
        third_handed[-1:] + third_got + first_got,
        sums((2,) + PART, (2,) + PART) if direct else [shape(4, *PART, dtype=F32)],
        [pltpu.VMEM((4,) + PART, F32)],
    )
    if direct:
        got = swap(third_sum[1], "dp", 1)
        third_sum = run(far_line_kernel, where, [third_sum[0], got], sums(PART, PART))
        third_sum[1] = swap(third_sum[1], "dp", 2)
        ready = third_sum[:1] + cross_sum[3:4]
    else:
        ready = []
    second_got = scatter_first(second_handed)
    second_passed = scatter_pass(where, second_handed, second_got, ready)
    second_last = scatter_second(second_passed)
    own = [shape(*CROSS, dtype=F32)] * 2 if direct else []
    pieces = run(
        token_sum_kernel,
        where,
        [result, grad_one, part, other] + cross_sum,
        [shape(LEN + 2 * S if direct else LEN, 2 * W)] * ROWS + own,
        [pltpu.VMEM((LEN, D), F32), pltpu.VMEM((ROWS, LEN, 2 * W), BF16)],
        after=second_last,
    )
    first_sum = run(
        carry_near_kernel,
        where,
        first_handed[-1:] + first_got + first_last + first_passed[1:],
        sums((2 * W + VROWS, COLS), CARRIED) if direct else wide + [shape(*VECTOR, dtype=F32)],
        lines,
        after=second_passed + third_sum[1:],
    )
    second_sum = run(
        line_kernel,
        where,
        second_handed[-1:] + second_got + second_last,
        sums(PART, PART) + [shape(*PART)] * 2 if direct else [shape(4, *PART, dtype=F32)],
        [pltpu.VMEM((4,) + PART, F32)],
    )
    if direct:
        got = swap(first_sum[1], "dp", 1)
        first_sum = run(
            carry_far_kernel,
            where,
            [first_sum[0], got],
            sums((W + VROWS, COLS), (W + 2 * VROWS, COLS)),
        )
        got = swap(first_sum[1], "dp", 2)
        state = joint + output
        new = run(
            first_adam_kernel,
            where,
            [first_sum[0], got] + state,
            like(state) + [shape(*VECTOR, dtype=F32)],
        )
        joint_new, output_new, vector = new[:3], new[3:6], new[6]

    flat_out = [shape(ROWS, 3 * PAIRS, 128, dtype=F32)] * 2
    got = exchange(pieces[:ROWS])
    out = run(token_out_kernel, where, got, flat_out)
    layer_out, tokens_grad = [v.reshape(tokens_in.shape) for v in out]

    def step_vectors(vector):
        state = [v.reshape(72, 128) for v in (vectors, vector_first, vector_second)]
        new = run(
            vector_adam_kernel,
            where,
            [vector, swap(vector, "col", 1)] + state,
            like(state),
            [pltpu.VMEM((72, 128), F32)],
        )
        return [v.reshape(vectors.shape) for v in new]

    if direct:
        down_new = run(
            down_adam_kernel, where, third_sum + pieces[ROWS : ROWS + 1] + got[1:] + down, like(down)
        )
        vector_new = step_vectors(vector)
        rows_got = pieces[ROWS + 1 :] + got[1:]
        got = [swap(v, "dp", mask) for v, mask in zip(second_sum[1:], ORDER[1:])]
        after = out[:1] + vector_new[:1] + down_new[:1]
        up_new = run(up_adam_kernel, where, second_sum[:1] + got + rows_got + up, like(up), after=after)
        up_new = [v.reshape(up_weight.shape) for v in up_new]
    else:

        def sum_cross(pair):
            kept, sent = [v.reshape(2, ROWS, *CROSS) for v in pair]
            both = jnp.stack([kept, sent], axis=1).reshape(QUADS, ROWS, *CROSS)
            return lax.psum_scatter(both.astype(F32), "row", scatter_dimension=1)

        second = jnp.concatenate([second_sum[0], sum_cross(cross_up)], axis=1)
        third = jnp.concatenate([third_sum[0], sum_cross(cross)], axis=1)
        grads = wide_sums(first_sum[0], second, third)
        joint_new = adamw(*joint, grads[0], JOINT_RATE, DECAY)
        output_new = adamw(*output, grads[1], OUTPUT_RATE, DECAY)
        up_new = adamw(*up, grads[2][:, None], JOINT_RATE, DECAY)
        down_new = adamw(*down, grads[3], DOWN_RATE, DECAY)
        vector_new = step_vectors(lax.psum(first_sum[1], "dp"))

    return (
        layer_out,
        tokens_grad,
        *[jnp.transpose(v, (2, 0, 1)) for v in joint_new],
        *[v.T[:, None] for v in output_new],
        *up_new,
        *[v.T[:, None] for v in down_new],
        *vector_new,
    )


def solution(mesh):
    first = P("row", "col", "dp")
    second = P("col", "row", "dp")
    tokens = P("dp", "row", None)
    weights = (first,) * 3 + (second,) * 3 + (first,) * 3 + (second,) * 3 + (P(),) * 3
    in_specs = (tokens, P(("dp", "row"))) + weights + (tokens,)
    out_specs = (tokens, tokens) + weights
    return jax.shard_map(
        per_device, mesh=mesh, in_specs=in_specs, out_specs=out_specs, check_vma=False
    )
```

```python
from functools import partial

import jax
import jax.numpy as jnp
from jax import lax
from jax.experimental import pallas as pl
from jax.experimental.pallas import tpu as pltpu
from jax.sharding import PartitionSpec as P

D = 768
H = 12
HD = 64
FF = 3072
LEN = 256
STEP = 10

NORM_EPS = 1e-12
BETA_ONE = 0.9
BETA_TWO = 0.999
ADAM_EPS = 1e-08
DECAY = 0.01
VECTOR_RATE = 0.2

F32 = jnp.float32
BF16 = jnp.bfloat16

ROWS = 4
QUADS = 4
W = D // ROWS
S = W // QUADS
COLS = D // 2
HEADS = COLS // HD
FFC = FF // 2
MIX = HEADS * 3 * HD
PAIRS = LEN // 2
CHUNK = (W, COLS)
PART = (3 * S, COLS)
CROSS = (S, COLS)
MIB = 1024 * 1024


def swap(value, axis, mask):
    n = lax.axis_size(axis)
    return lax.ppermute(value, axis, [(i, i ^ mask) for i in range(n)])


def shape(*dims, dtype=BF16):
    return jax.ShapeDtypeStruct(dims, dtype)


def run(kernel, where, args, outs, scratch=(), limit=8, after=(), fetch=False):
    vmem = pl.BlockSpec(memory_space=pltpu.VMEM)
    first, late = 1 + len(args), len(after)

    def body(*refs):
        kernel(*refs[:first], *refs[first + late :])

    out = pl.pallas_call(
        body,
        out_shape=outs,
        in_specs=[pl.BlockSpec(memory_space=pltpu.SMEM)]
        + [pl.BlockSpec(memory_space=pl.ANY) if fetch else vmem] * len(args)
        + [pl.BlockSpec(memory_space=pl.ANY)] * late,
        out_specs=[vmem] * len(outs),
        scratch_shapes=list(scratch),
        compiler_params=pltpu.CompilerParams(vmem_limit_bytes=limit * MIB),
    )(where, *args, *after)
    return list(out)


def dot(left, right, dims):
    return lax.dot_general(left, right, (dims, ((), ())), preferred_element_type=F32)


NN = ((1,), (0,))
NT = ((1,), (1,))
TN = ((0,), (0,))


def each(count, body):
    def step(i, carry):
        body(i)
        return carry

    lax.fori_loop(0, count, step, 0)


def row_of(vecs, start, count):
    return jnp.concatenate([vecs[start + i : start + i + 1, :] for i in range(count)], axis=1)


def vector_row(vecs, k):
    return row_of(vecs, 6 * k, 6)


def pick_col(where, left, right):
    return jnp.where(where[2] == 0, left, right)


def split_parts(value):
    high = value.astype(BF16)
    return high, (value - high.astype(F32)).astype(BF16)


def opening_kernel(where, tokens, grads, joint, output, down, *refs):
    outs, first = refs[:ROWS], refs[ROWS]
    tokens_in, grads_in, joint_in, output_in, down_in, done = refs[ROWS + 1 :]
    copies = [
        pltpu.make_async_copy(source, target, done.at[i])
        for i, (source, target) in enumerate(
            [
                (joint, joint_in),
                (output, output_in),
                (tokens, tokens_in),
                (grads, grads_in),
                (down.at[:, 3 * COLS :], down_in),
            ]
        )
    ]
    for copy in copies:
        copy.start()
    copies[0].wait()
    copies[1].wait()
    for h in range(HEADS // 2):
        pair = [joint_in[h].astype(BF16), joint_in[h + HEADS // 2].astype(BF16)]
        first[h * S : (h + 1) * S, :] = jnp.concatenate(pair, axis=1)
    first[HEADS // 2 * S :, :] = output_in[...].astype(BF16)
    copies[2].wait()
    copies[3].wait()
    copies[4].wait()
    for m, out in enumerate(outs):
        out[0:PAIRS, :] = tokens_in[where[0] ^ m]
        out[PAIRS:LEN, :] = grads_in[where[0] ^ m]
        out[LEN:, :] = down_in[...].astype(BF16)


def second_shard_kernel(where, up, second):
    for q in range(3):
        second[:, q * 128 : (q + 1) * 128] = up[pl.ds(q, W, stride=3), :].astype(BF16)


def third_shard_kernel(where, down, third):
    for q in range(3):
        third[q * S : (q + 1) * S, :] = down[:, q * COLS : (q + 1) * COLS].astype(BF16)


def pair_kernel(where, b0, b1, pair):
    pair[0] = b0[...]
    pair[1] = b1[...]


def cross_kernel(where, t0, t1, t2, t3, plane):
    for m, piece in enumerate([t0, t1, t2, t3]):
        plane[m] = piece[LEN:, :]


def planes_kernel(where, b0, b1, planes):
    planes[0:ROWS] = b0[...]
    planes[ROWS:] = b1[...]


def whole_kernel(where, *refs):
    *pieces, line = refs
    for k in range(QUADS):
        line[k] = pieces[k][...] if len(pieces) == QUADS else pieces[k // 2][k % 2]


def halves_kernel(where, from_x, from_y, near_y, far_x):
    near_y[...] = from_y[0:2]
    far_x[...] = from_x[2:4]


def token_kernel(where, tokens, grads, *outs):
    for m, out in enumerate(outs):
        out[0:PAIRS, :] = tokens[where[0] ^ m]
        out[PAIRS:LEN, :] = grads[where[0] ^ m]


ORDER = (0, 2, 1, 3)


def blocks(where, pieces):
    found = [(piece, i) for piece in pieces for i in range(piece.shape[0])]
    for at, (piece, i) in enumerate(found):
        yield where[0] ^ (at // QUADS), where[1] ^ ORDER[at % QUADS], piece[i]


def cross_blocks(where, pieces):
    for j, piece in enumerate(pieces):
        for i in range(2 * ROWS):
            yield where[0] ^ (i % ROWS), where[1] ^ ORDER[2 * j + i // ROWS], piece[i]


def unpack_tokens(x):
    parts = [jnp.concatenate([x[r][:, :W], x[r][:, W:]], axis=0) for r in range(ROWS)]
    return jnp.concatenate(parts, axis=1)


def pack_tokens(value, room, k):
    for r in range(ROWS):
        both = value[:, r * W : (r + 1) * W]
        packed = jnp.concatenate([both[:PAIRS], both[PAIRS:]], axis=1).astype(BF16)
        room[r, k * PAIRS : (k + 1) * PAIRS, :] = packed


def attend_kernel(where, t0, t1, t2, t3, vecs, *refs):
    pieces, refs = refs[:5], refs[5:]
    tokens, grads, wj, wo, mixed, probs, attended, part, room, mixing, scores, parts = refs
    for m, piece in enumerate([t0, t1, t2, t3]):
        room[where[0] ^ m] = piece[0:LEN, :]
    tokens[...] = unpack_tokens([room[r, 0:PAIRS, :] for r in range(ROWS)])
    grads[...] = unpack_tokens([room[r, PAIRS:, :] for r in range(ROWS)])
    half = HEADS // 2
    for row, quad, value in blocks(where, pieces):
        for h in range(half):
            rows = value[h * S : (h + 1) * S, :]
            for k, cut in enumerate([rows[:, :W], rows[:, W:]]):
                start = pl.multiple_of((h + k * half) * 3 * HD + quad * S, 16)
                wj[row, pl.ds(start, S), :] = cut
        start = pl.multiple_of(row * W + quad * S, 16)
        wo[pl.ds(start, S), :] = value[half * S :, :]
    total = dot(wj[0], tokens[:, :W], NT)
    for r in range(1, ROWS):
        total = total + dot(wj[r], tokens[:, r * W : (r + 1) * W], NT)
    mixing[...] = total
    query_bias, value_bias = [
        pick_col(where, row_of(vecs, start, 3), row_of(vecs, start + 3, 3)) for start in (0, 6)
    ]
    zero = jnp.zeros((1, HD), F32)
    row = []
    for h in range(HEADS):
        at = slice(h * HD, (h + 1) * HD)
        row += [query_bias[:, at], zero, value_bias[:, at]]
    row = jnp.concatenate(row, axis=1)
    high, low = split_parts(row)
    rest = (row - high.astype(F32) - low.astype(F32)).astype(BF16)
    parts[...] = jnp.zeros_like(parts)
    parts[0:1, :] = high.astype(F32)
    parts[1:2, :] = low.astype(F32)
    parts[2:3, :] = rest.astype(F32)
    bias = dot(parts[...].astype(BF16), jnp.ones((8, LEN), BF16), TN)
    mixed[...] = (mixing[...] + bias).astype(BF16)
    slot = lax.broadcasted_iota(jnp.int32, (LEN, 1), 0)
    slot = jnp.where(slot < PAIRS, 2 * slot, 2 * (slot - PAIRS) + 1)
    valid = slot < where[3]
    for h in range(HEADS):
        base = h * 3 * HD
        query, keyed, valued = [mixed[base + k * HD : base + (k + 1) * HD, :] for k in range(3)]
        scores[...] = dot(keyed, query, TN)
        for q in range(2):
            at = slice(q * 128, (q + 1) * 128)
            score = jnp.where(valid, scores[:, at] * 0.125, -1e30)
            expo = jnp.exp(score - jnp.max(score, axis=0, keepdims=True))
            prob = expo * (1.0 / jnp.sum(expo, axis=0, keepdims=True))
            probs[h, :, at] = prob.astype(BF16)
        attended[h * HD : (h + 1) * HD, :] = dot(valued, probs[h], NN).astype(BF16)
    part[...] = dot(attended[...], wo[...], ((0,), (1,))).astype(BF16)


def norm_rows(resid, gain, shift_by):
    mean = jnp.sum(resid, axis=1, keepdims=True) * (1.0 / D)
    var = jnp.sum(resid * resid, axis=1, keepdims=True) * (1.0 / D) - mean * mean
    inverse = lax.rsqrt(var + NORM_EPS)
    normed = (resid - mean) * inverse
    return normed * gain + shift_by, normed, inverse


def norm_back_rows(grad, normed, inverse, gain):
    scaled = grad * gain
    total = jnp.sum(scaled, axis=1, keepdims=True) * (1.0 / D)
    cross = jnp.sum(scaled * normed, axis=1, keepdims=True) * (1.0 / D)
    return (scaled - total - normed * cross) * inverse


STRIP = 32


def strip(i):
    return pl.ds(pl.multiple_of(i * STRIP, STRIP), STRIP)


def up_kernel(where, tokens, p0, p1, vecs, *refs):
    pieces, refs = refs[:5], refs[5:]
    hidden, low, normed, inverse, act, slope, wu, pre = refs
    for row, quad, value in blocks(where, pieces):
        rows = pl.ds(pl.multiple_of(row * W, W), W)
        wu[rows, pl.ds(pl.multiple_of(quad * COLS, COLS), COLS)] = value

    bias_out, gain, shift_by = [vector_row(vecs, k) for k in (2, 3, 4)]

    def first(i):
        at = strip(i)
        resid = tokens[at, :].astype(F32) + (p0[at, :].astype(F32) + p1[at, :].astype(F32))
        out, unit, scale = norm_rows(resid + bias_out, gain, shift_by)
        hidden[at, :] = out
        low[at, :] = out.astype(BF16)
        normed[at, :] = unit
        inverse[at, :] = scale

    each(LEN // STRIP, first)
    pre[...] = dot(low[...], wu[...], NN)
    bias = pick_col(where, row_of(vecs, 48, 12), row_of(vecs, 60, 12))
    for q in range(4):
        cols = slice(q * COLS, (q + 1) * COLS)
        shift_up = bias[:, cols]

        def second(i, cols=cols, shift_up=shift_up):
            at = (strip(i), cols)
            value = pre[at] + shift_up
            phi = 0.5 * (1.0 + lax.erf(value * (0.5**0.5)))
            density = jnp.exp(-0.5 * value * value) * 0.3989422804014327
            act[at] = (value * phi).astype(BF16)
            slope[at] = phi + value * density

        each(LEN // STRIP, second)


def down_kernel(where, act, *refs):
    pieces, cross, wd, part = refs[:5], refs[5:7], refs[7], refs[8]
    for row, quad, value in blocks(where, pieces):
        rows = pl.ds(pl.multiple_of(row * W + quad * S, 16), S)
        for q in range(3):
            wd[rows, q * COLS : (q + 1) * COLS] = value[q * S : (q + 1) * S, :]
    for row, quad, value in cross_blocks(where, cross):
        rows = pl.ds(pl.multiple_of(row * W + quad * S, 16), S)
        wd[rows, 3 * COLS :] = value
    part[...] = dot(act[...], wd[...], NT).astype(BF16)


def hand_out(where, room, outs):
    r = where[0]
    to_x, to_y, last_x, last_y, own = outs
    to_x[0:2] = room[r ^ 3, 0:2]
    to_x[2:4] = room[r ^ 1, 0:2]
    to_y[0:2] = room[r ^ 3, 2:4]
    to_y[2:4] = room[r ^ 2, 2:4]
    last_x[...] = room[r ^ 1, 2:4]
    last_y[...] = room[r ^ 2, 0:2]
    own[...] = room[r]


def handed_shapes(block):
    pair, line = shape(2, *block), shape(4, *block)
    return [line] * 2 + [pair] * 2 + [line]


HANDED = handed_shapes(CHUNK)
PAIR = shape(2, *CHUNK)
PLANES = shape(2 * ROWS, *CROSS)

VROWS = 32
VECTOR = (VROWS, COLS)
CARRIED = (2 * W + 2 * VROWS, COLS)

LATE_X = 4 * W + 2 * VROWS
LATE_Y = 4 * W
FIRST_X = (LATE_X + 2 * PART[0], COLS)
FIRST_Y = (LATE_Y + 2 * PART[0], COLS)


def put_vector(out, start, value):
    high, low = split_parts(value)
    out[start : start + VROWS, :] = high
    out[start + VROWS : start + 2 * VROWS, :] = low


def get_vector(value, start):
    high = value[start : start + VROWS, :].astype(F32)
    return high + value[start + VROWS : start + 2 * VROWS, :].astype(F32)


def second_norm_kernel(where, hidden, p0, p1, vecs, grads, act, *refs):
    (result, low, grad_two, sums), handed = refs[:4], refs[4:9]
    cross_own, cross_send, room, cross = refs[9:]
    sums[...] = jnp.zeros_like(sums)
    bias_down, gain, shift_by = [vector_row(vecs, k) for k in (5, 6, 7)]

    def body(i):
        at = strip(i)
        resid = hidden[at, :] + (p0[at, :].astype(F32) + p1[at, :].astype(F32)) + bias_down
        out, unit, scale = norm_rows(resid, gain, shift_by)
        result[at, :] = out
        grad = grads[at, :].astype(F32)
        back = norm_back_rows(grad, unit, scale, gain)
        grad_two[at, :] = back
        rounded = back.astype(BF16)
        low[at, :] = rounded
        sums[0:1, :] += jnp.sum(rounded.astype(F32), axis=0, keepdims=True)
        sums[1:2, :] += jnp.sum(grad * unit, axis=0, keepdims=True)
        sums[2:3, :] += jnp.sum(grad, axis=0, keepdims=True)

    each(LEN // STRIP, body)
    for q in range(4):
        cols = slice(q * COLS, (q + 1) * COLS)
        grad = dot(low[...], act[:, cols], TN).astype(BF16)
        for r in range(ROWS):
            for z in range(QUADS):
                start = r * W + z * S
                if q < 3:
                    room[r, z, q * S : (q + 1) * S, :] = grad[start : start + S, :]
                else:
                    cross[z, r] = grad[start : start + S, :]
    hand_out(where, room, handed)
    for k, mask in enumerate([0, 2]):
        rows = slice(k * ROWS, (k + 1) * ROWS)
        cross_own[rows] = cross[where[1] ^ mask]
        cross_send[rows] = cross[where[1] ^ mask ^ 1]


def hidden_back_kernel(where, low, slope, wd, wu, grad_pre, part, sums, back):
    back[...] = dot(low[...], wd[...], NN)
    sums[...] = jnp.zeros_like(sums)
    for q in range(4):
        cols = slice(q * COLS, (q + 1) * COLS)

        def body(i, cols=cols):
            at = (strip(i), cols)
            value = (back[at] * slope[at]).astype(BF16)
            grad_pre[at] = value
            sums[0:1, cols] += jnp.sum(value.astype(F32), axis=0, keepdims=True)

        each(LEN // STRIP, body)
    part[...] = dot(grad_pre[...], wu[...], NT).astype(BF16)


def up_grad_kernel(where, low, grad_pre, *refs):
    handed, room = refs[:5], refs[5]
    for z in range(QUADS):
        grad = dot(low[...], grad_pre[:, z * COLS : (z + 1) * COLS], TN).astype(BF16)
        for r in range(ROWS):
            room[r, z] = grad[r * W : (r + 1) * W, :]
    hand_out(where, room, handed)


def first_norm_kernel(
    where, grad_two, p0, p1, normed, inverse, vecs, wo, mixed, probs, *refs
):
    grad_one, grad_mixed, low, sums, back, inner, scores = refs
    sums[...] = jnp.zeros_like(sums)
    gain = vector_row(vecs, 3)

    def body(i):
        at = strip(i)
        grad = grad_two[at, :] + (p0[at, :].astype(F32) + p1[at, :].astype(F32))
        unit = normed[at, :]
        out = norm_back_rows(grad, unit, inverse[at, :], gain)
        grad_one[at, :] = out
        rounded = out.astype(BF16)
        low[at, :] = rounded
        sums[0:1, :] += jnp.sum(rounded.astype(F32), axis=0, keepdims=True)
        sums[1:2, :] += jnp.sum(grad * unit, axis=0, keepdims=True)
        sums[2:3, :] += jnp.sum(grad, axis=0, keepdims=True)

    each(LEN // STRIP, body)
    back[...] = dot(wo[...], low[...], ((0,), (1,))).astype(BF16)
    for h in range(HEADS):
        base = h * 3 * HD
        query, keyed, valued = [mixed[base + k * HD : base + (k + 1) * HD, :] for k in range(3)]
        grad_out = back[h * HD : (h + 1) * HD, :]
        inner[...] = dot(valued, grad_out, TN)
        for q in range(2):
            at = slice(q * 128, (q + 1) * 128)
            prob = probs[h, :, at].astype(F32)
            grad = inner[:, at]
            mean = jnp.sum(grad * prob, axis=0, keepdims=True)
            scores[:, at] = (prob * (grad - mean)).astype(BF16)
        grads = [
            dot(keyed, scores[...], NN) * 0.125,
            dot(query, scores[...], NT) * 0.125,
            dot(grad_out, probs[h], NT),
        ]
        for k, grad in enumerate(grads):
            grad_mixed[base + k * HD : base + (k + 1) * HD, :] = grad.astype(BF16)


def first_grad_kernel(where, grad_mixed, low, sums, attended, tokens, sums_two, sums_up, *refs):
    vector, room = refs
    half = HEADS // 2
    for r in range(ROWS):
        cut = tokens[:, r * W : (r + 1) * W]
        grad = dot(grad_mixed[...], cut, NN).astype(BF16)
        for z in range(QUADS):
            for h in range(half):
                starts = [(h + k * half) * 3 * HD + z * S for k in range(2)]
                pair = [grad[start : start + S, :] for start in starts]
                room[r, z, h * S : (h + 1) * S, :] = jnp.concatenate(pair, axis=1)
        grad = dot(low[:, r * W : (r + 1) * W], attended[...], ((0,), (1,))).astype(BF16)
        for z in range(QUADS):
            room[r, z, half * S :, :] = grad[z * S : (z + 1) * S, :]
    left = jnp.where(where[2] == 0, 1.0, 0.0)
    right = 1.0 - left
    total = dot(jnp.ones((8, LEN), BF16), grad_mixed[...], NT)[0:1, :]
    vector[...] = jnp.zeros_like(vector)
    for k, start in enumerate([0, 2 * HD]):
        at = [h * 3 * HD + start for h in range(HEADS)]
        row = jnp.concatenate([total[:, i : i + HD] for i in at], axis=1)
        vector[2 * k : 2 * k + 1, :] = row * left
        vector[2 * k + 1 : 2 * k + 2, :] = row * right
    for k, found in enumerate([sums, sums_two]):
        for i in range(3):
            for j in range(2):
                row = 4 + 6 * k + 2 * i + j
                vector[row : row + 1, :] = found[i : i + 1, j * COLS : (j + 1) * COLS] * left
    for j in range(4):
        row = sums_up[0:1, j * COLS : (j + 1) * COLS]
        vector[16 + j : 17 + j, :] = row * left
        vector[20 + j : 21 + j, :] = row * right


def first_hand_kernel(where, room, vector, late_x, late_y, to_x, to_y, last_x, last_y, own):
    r = where[0]
    for k in range(2):
        far, near = slice(k * W, (k + 1) * W), slice((2 + k) * W, (3 + k) * W)
        to_x[far, :] = room[r ^ 3, k]
        to_x[near, :] = room[r ^ 1, k]
        to_y[far, :] = room[r ^ 3, 2 + k]
        to_y[near, :] = room[r ^ 2, 2 + k]
        for start, out, late in [(LATE_X, to_x, late_x), (LATE_Y, to_y, late_y)]:
            at = start + k * PART[0]
            out[at : at + PART[0], :] = late[k]
    last_x[...] = room[r ^ 1, 2:4]
    last_y[...] = room[r ^ 2, 0:2]
    own[...] = room[r]
    put_vector(to_x, 4 * W, vector[...])


def token_back_kernel(where, grad_mixed, wj, part):
    for r in range(ROWS):
        part[:, r * W : (r + 1) * W] = dot(grad_mixed[...], wj[r], TN).astype(BF16)


def token_sum_kernel(where, result, grad_one, p0, p1, *refs):
    total, room = refs[-2:]
    cross = [*refs[:2], refs[6]] if len(refs) > 6 else []
    outs = refs[2:6] if cross else refs[:4]

    def body(i):
        at = strip(i)
        total[at, :] = grad_one[at, :] + (p0[at, :].astype(F32) + p1[at, :].astype(F32))

    each(LEN // STRIP, body)
    pack_tokens(result, room, 0)
    pack_tokens(total, room, 1)
    for m, out in enumerate(outs):
        row = where[0] ^ m
        out[0:LEN, :] = room[row]
        if cross:
            kept, got, own = cross
            sums = kept[row] + got[row].astype(F32)
            out[LEN:, :] = sums.astype(BF16)
            if m == 0:
                own[...] = sums


def token_out_kernel(where, t0, t1, t2, t3, result, total):
    for m, piece in enumerate([t0, t1, t2, t3]):
        for k, out in enumerate([result, total]):
            for q in range(3):
                value = piece[k * PAIRS : (k + 1) * PAIRS, q * 128 : (q + 1) * 128].astype(F32)
                out[where[0] ^ m, pl.ds(q, PAIRS, stride=3), :] = value


def pass_kernel(where, last_x, last_y, from_x, from_y, to_x, to_y):
    to_x[...] = (last_x[...].astype(F32) + from_y[0:2].astype(F32)).astype(BF16)
    to_y[...] = (last_y[...].astype(F32) + from_x[0:2].astype(F32)).astype(BF16)


def carry_pass_kernel(where, last_x, last_y, carried, from_x, from_y, to_x, to_y):
    for k in range(2):
        rows = slice(k * W, (k + 1) * W)
        to_x[k] = (last_x[k].astype(F32) + from_y[rows, :].astype(F32)).astype(BF16)
        to_y[rows, :] = (last_y[k].astype(F32) + from_x[rows, :].astype(F32)).astype(BF16)
    put_vector(to_y, 2 * W, get_vector(carried, 4 * W) + get_vector(from_x, 4 * W))


def add_plane(own, from_x, from_y, last_x, last_y, room):
    for k in range(2):
        room[k] = (own[k].astype(F32) + from_x(k)) + last_y(k)
        room[2 + k] = (own[2 + k].astype(F32) + from_y(k)) + last_x(k)


def kept_blocks(ref):
    skip = ref.shape[0] - 2
    return lambda k: ref[skip + k].astype(F32)


def kept_rows(ref, start, rows=W):
    return lambda k: ref[start + k * rows : start + (k + 1) * rows, :].astype(F32)


def line_kernel(where, own, from_x, from_y, last_x, last_y, kept, *refs):
    *sends, room = refs
    add_plane(own, *[kept_blocks(v) for v in (from_x, from_y, last_x, last_y)], room)
    if sends:
        kept[...] = room[where[1]]
        for mask, send in zip(ORDER[1:], sends):
            send[...] = room[where[1] ^ mask].astype(BF16)
    else:
        kept[...] = room[...]


def near_line_kernel(where, own, from_x, from_y, late_x, late_y, kept, *refs):
    *sends, room = refs
    late = [kept_rows(late_x, LATE_X, PART[0]), kept_rows(late_y, LATE_Y, PART[0])]
    add_plane(own, kept_blocks(from_x), kept_blocks(from_y), *late, room)
    if sends:
        for k, mask in enumerate([0, 2]):
            kept[k] = room[where[1] ^ mask]
            sends[0][k] = room[where[1] ^ mask ^ 1].astype(BF16)
    else:
        kept[...] = room[...]


def far_line_kernel(where, kept, got, total, send):
    total[...] = kept[0] + got[0].astype(F32)
    send[...] = (kept[1] + got[1].astype(F32)).astype(BF16)


def cross_far_kernel(where, own, got, kept, send):
    kept[...] = own[0:ROWS].astype(F32) + got[0:ROWS].astype(F32)
    send[...] = (own[ROWS:].astype(F32) + got[ROWS:].astype(F32)).astype(BF16)


def carry_near_kernel(where, own, first_x, first_y, last_x, from_y, passed, kept, *refs):
    *sends, room = refs
    near = [kept_rows(first_x, 2 * W), kept_rows(first_y, 2 * W)]
    add_plane(own, *near, kept_blocks(last_x), kept_rows(from_y, 0), room)
    vector = get_vector(passed, 2 * W) + get_vector(from_y, 2 * W)
    if kept.ndim == 2:
        for k, mask in enumerate([0, 2]):
            rows = slice(k * W, (k + 1) * W)
            kept[rows, :] = room[where[1] ^ mask]
            sends[0][rows, :] = room[where[1] ^ mask ^ 1].astype(BF16)
        kept[2 * W :, :] = vector
        put_vector(sends[0], 2 * W, vector)
    else:
        kept[...] = room[...]
        sends[0][...] = vector


def add_vector(own, got, start):
    high, low = split_parts(own)
    return (high.astype(F32) + low.astype(F32)) + get_vector(got, start)


def carry_far_kernel(where, kept, got, total, send):
    total[0:W, :] = kept[0:W, :] + got[0:W, :].astype(F32)
    send[0:W, :] = (kept[W : 2 * W, :] + got[W : 2 * W, :].astype(F32)).astype(BF16)
    vector = add_vector(kept[2 * W :, :], got, 2 * W)
    total[W:, :] = vector
    put_vector(send, W, vector)


def adamw(weight, first, second, grad, rate, decay):
    first_new = BETA_ONE * first + (1.0 - BETA_ONE) * grad
    second_new = BETA_TWO * second + (1.0 - BETA_TWO) * grad * grad
    fix_one = 1.0 - BETA_ONE**STEP
    fix_two = 1.0 - BETA_TWO**STEP
    update = first_new / fix_one / (jnp.sqrt(second_new / fix_two) + ADAM_EPS) + decay * weight
    return (first_new, second_new, weight - rate * update)


JOINT_RATE = D ** (-0.5)
OUTPUT_RATE = (4 * D // LEN) ** (-0.5)
DOWN_RATE = FF ** (-0.5)


def first_adam_kernel(where, kept, got, jw, jf, js, ow, of, os, *refs):
    outs, vector = refs[:6], refs[6]
    grad = kept[0:W, :] + got[0:W, :].astype(F32)
    half = HEADS // 2
    for h in range(HEADS):
        rows = grad[h % half * S : (h % half + 1) * S, :]
        cut = rows[:, :W] if h < half else rows[:, W:]
        new = adamw(jw[h], jf[h], js[h], cut, JOINT_RATE, DECAY)
        for out, value in zip(outs[:3], new):
            out[h] = value
    new = adamw(ow[...], of[...], os[...], grad[half * S :, :], OUTPUT_RATE, DECAY)
    for out, value in zip(outs[3:], new):
        out[...] = value
    vector[...] = add_vector(kept[W:, :], got, W)


def vector_adam_kernel(where, mine, other, weight, first, second, *refs):
    outs, grad = refs[:3], refs[3]
    total = mine[...] + other[...]
    for q in range(3):
        grad[pl.ds(q, 24, stride=3), :] = total[0:24, q * 128 : (q + 1) * 128]
    new = adamw(weight[...], first[...], second[...], grad[...], VECTOR_RATE, 0.0)
    for out, value in zip(outs, new):
        out[...] = value


def up_adam_kernel(where, kept, r2, r1, r3, w, f, s, *outs):
    grad = (kept[...] + r1[...].astype(F32)) + (r2[...].astype(F32) + r3[...].astype(F32))
    for q in range(3):
        at = (pl.ds(q, W, stride=3), slice(None))
        cut = grad[:, q * 128 : (q + 1) * 128]
        for out, value in zip(outs, adamw(w[at], f[at], s[at], cut, JOINT_RATE, DECAY)):
            out[at] = value


def down_adam_kernel(where, kept, got, own, r1, r2, r3, w, f, s, *outs):
    far = r2[LEN:, :].astype(F32) + r3[LEN:, :].astype(F32)
    cross = (own[...] + r1[LEN:, :].astype(F32)) + far
    most = kept[...] + got[...].astype(F32)
    for q in range(4):
        at = (slice(None), slice(q * COLS, (q + 1) * COLS))
        cut = most[q * S : (q + 1) * S, :] if q < 3 else cross
        for out, value in zip(outs, adamw(w[at], f[at], s[at], cut, DOWN_RATE, DECAY)):
            out[at] = value


def gather_line(where, shard, steps):
    if steps == 1:
        return [shard] + [swap(shard, "dp", mask) for mask in ORDER[1:]]
    pair = [shape(2, *shard.shape)]
    pair = run(pair_kernel, where, [shard, swap(shard, "dp", 2)], pair)[0]
    return [pair, swap(pair, "dp", 1)]


def gather_plane(where, line, after=()):
    block = line[0].shape[-2:]
    line = run(whole_kernel, where, line, [shape(4, *block)], after=after)[0]
    from_x = swap(line, "row", 1)
    from_y = swap(line, "row", 2)
    near_y, far_x = run(halves_kernel, where, [from_x, from_y], [shape(2, *block)] * 2)
    return [line, from_x, from_y, swap(near_y, "row", 1), swap(far_x, "row", 2)]


def gather_cross(where, plane):
    planes = run(planes_kernel, where, [plane, swap(plane, "dp", 2)], [PLANES])[0]
    return [planes, swap(planes, "dp", 1)]


def scatter_first(handed):
    return [swap(value, "row", 1 + i % 2) for i, value in enumerate(handed[:-3])]


def scatter_pass(where, handed, got, after=()):
    pair = [shape(*handed[2].shape)] * 2
    return run(pass_kernel, where, handed[2:4] + got, pair, after=after)


def scatter_second(passed):
    return [swap(passed[0], "row", 1), swap(passed[1], "row", 2)]


def exchange(pieces):
    return [pieces[0]] + [swap(pieces[m], "row", m) for m in range(1, ROWS)]


def wide_lines(joint, output, up, down):
    order = jnp.array(ORDER)
    n = lax.axis_size("dp") // QUADS

    def collect(shard, axis):
        whole = lax.all_gather(shard.astype(BF16), "dp", axis=axis, tiled=True)
        return jnp.stack(jnp.split(whole, QUADS, axis=axis))

    joint = collect(joint, 1)
    half = HEADS // 2
    pair = joint.reshape(QUADS, 2, half, S, W)
    pair = jnp.transpose(pair, (0, 2, 3, 1, 4)).reshape(QUADS, half * S, 2 * W)
    first = jnp.concatenate([pair, collect(output, 0)], axis=1)
    second = collect(up, 1)
    third = collect(down, 0).reshape(QUADS, S, 4, COLS)
    third = jnp.transpose(third, (0, 2, 1, 3)).reshape(QUADS, W, COLS)
    return [jnp.take(value, order, axis=0) for value in (first, second, third)]


def wide_sums(first, second, third):
    def give(value, axis):
        whole = jnp.concatenate(list(value), axis=axis)
        return lax.psum_scatter(whole, "dp", scatter_dimension=axis, tiled=True)

    half = HEADS // 2
    pair = first[:, : half * S].reshape(QUADS, half, S, 2, W)
    joint = jnp.transpose(pair, (0, 3, 1, 2, 4)).reshape(QUADS, HEADS, S, W)
    third = jnp.transpose(third.reshape(QUADS, 4, S, COLS), (0, 2, 1, 3))
    third = third.reshape(QUADS, S, FFC)
    return give(joint, 1), give(first[:, half * S :], 0), give(second, 1), give(third, 0)


def per_device(
    tokens_in,
    lengths,
    joint_weight,
    joint_first,
    joint_second,
    output_weight,
    output_first,
    output_second,
    up_weight,
    up_first,
    up_second,
    down_weight,
    down_first,
    down_second,
    vectors,
    vector_first,
    vector_second,
    out_grad,
):
    r = lax.axis_index("row")
    col = lax.axis_index("col")
    direct = lax.axis_size("dp") == QUADS
    z = lax.axis_index("dp") if direct else jnp.int32(0)
    where = jnp.stack([r, z, col, lengths[0]]).astype(jnp.int32)

    joint = [jnp.transpose(v, (1, 2, 0)) for v in (joint_weight, joint_first, joint_second)]
    output = [v[:, 0].T for v in (output_weight, output_first, output_second)]
    down = [v[:, 0].T for v in (down_weight, down_first, down_second)]
    up = [up_weight, up_first, up_second]
    flat = up_weight.size // 128

    sent = [tokens_in.reshape(ROWS, PAIRS, 2 * W), out_grad.reshape(ROWS, PAIRS, 2 * W)]
    blocks_out = [shape(LEN + S if direct else LEN, 2 * W)] * ROWS
    if direct:
        up = [v.reshape(flat, 128) for v in up]
        one = [shape(*CHUNK)]
        *pieces, first = run(
            opening_kernel,
            where,
            sent + [joint[0], output[0], down[0]],
            blocks_out + one,
            [
                pltpu.VMEM(sent[0].shape, BF16),
                pltpu.VMEM(sent[1].shape, BF16),
                pltpu.VMEM(joint[0].shape, F32),
                pltpu.VMEM(output[0].shape, F32),
                pltpu.VMEM(CROSS, F32),
                pltpu.SemaphoreType.DMA((5,)),
            ],
            limit=56,
            fetch=True,
        )
        tokens_pieces = exchange(pieces)
        first = gather_line(where, first, 1)
        first_pieces = gather_plane(where, first, tokens_pieces[1:])
        shard = run(second_shard_kernel, where, [up[0]], one, after=first[1:])[0]
        second = gather_line(where, shard, 2)
        plane = run(cross_kernel, where, tokens_pieces, [shape(ROWS, *CROSS)])[0]
        cross = gather_cross(where, plane)
        second_pieces = gather_plane(where, second)
        after = second_pieces[:1] + cross[:1]
        shard = run(third_shard_kernel, where, [down[0]], [shape(*PART)], after=after)[0]
        third = gather_line(where, shard, 2)
        third_pieces = gather_plane(where, third, first_pieces[3:])
        third_pieces += cross
    else:
        tokens_pieces = exchange(run(token_kernel, where, sent, blocks_out))
        lines = wide_lines(joint[0], output[0], up_weight[:, 0], down[0])
        cross = lines[2][:, 3 * S :]
        lines[2] = lines[2][:, : 3 * S]
        first_pieces, second_pieces, third_pieces = [
            gather_plane(where, list(line)) for line in lines
        ]
        cross = jnp.stack([cross] + [swap(cross, "row", m) for m in range(1, ROWS)], axis=1)
        third_pieces += list(cross.reshape(2, *PLANES.shape))

    vecs = vectors.reshape(72, 128)
    tokens, grads, wj, wo, mixed, probs, attended, part = run(
        attend_kernel,
        where,
        tokens_pieces + [vecs] + first_pieces,
        [
            shape(LEN, D),
            shape(LEN, D),
            shape(ROWS, MIX, W),
            shape(D, COLS),
            shape(MIX, LEN),
            shape(HEADS, LEN, LEN),
            shape(COLS, LEN),
            shape(LEN, D),
        ],
        [
            pltpu.VMEM((ROWS, LEN, 2 * W), BF16),
            pltpu.VMEM((MIX, LEN), F32),
            pltpu.VMEM((LEN, LEN), F32),
            pltpu.VMEM((8, MIX), F32),
        ],
    )
    hidden, hidden_low, normed, inverse, act, slope, wu = run(
        up_kernel,
        where,
        [tokens, part, swap(part, "col", 1), vecs] + second_pieces,
        [
            shape(LEN, D, dtype=F32),
            shape(LEN, D),
            shape(LEN, D, dtype=F32),
            shape(LEN, 1, dtype=F32),
            shape(LEN, FFC),
            shape(LEN, FFC, dtype=F32),
            shape(D, FFC),
        ],
        [pltpu.VMEM((LEN, FFC), F32)],
        after=third_pieces[6:],
    )
    wd, part = run(
        down_kernel, where, [act] + third_pieces, [shape(D, FFC), shape(LEN, D)]
    )
    out = run(
        second_norm_kernel,
        where,
        [hidden, part, swap(part, "col", 1), vecs, grads, act],
        [shape(LEN, D, dtype=F32), shape(LEN, D), shape(LEN, D, dtype=F32)]
        + [shape(8, D, dtype=F32)]
        + handed_shapes(PART)
        + [PLANES] * 2,
        [
            pltpu.VMEM((ROWS, QUADS) + PART, BF16),
            pltpu.VMEM((QUADS, ROWS) + CROSS, BF16),
        ],
    )
    (result, grad_low, grad_two, sums_two), third_handed, cross = out[:4], out[4:9], out[9:]
    third_got = scatter_first(third_handed)
    grad_pre, part, sums_up = run(
        hidden_back_kernel,
        where,
        [grad_low, slope, wd, wu],
        [shape(LEN, FFC), shape(LEN, D), shape(8, FFC, dtype=F32)],
        [pltpu.VMEM((LEN, FFC), F32)],
    )
    third_passed = scatter_pass(where, third_handed, third_got)
    second_handed = run(
        up_grad_kernel,
        where,
        [hidden_low, grad_pre],
        HANDED,
        [pltpu.VMEM((ROWS, QUADS) + CHUNK, BF16)],
    )
    grad_one, grad_mixed, low, sums_one = run(
        first_norm_kernel,
        where,
        [
            grad_two,
            part,
            swap(part, "col", 1),
            normed,
            inverse,
            vecs,
            wo,
            mixed,
            probs,
        ],
        [
            shape(LEN, D, dtype=F32),
            shape(MIX, LEN),
            shape(LEN, D),
            shape(8, D, dtype=F32),
        ],
        [
            pltpu.VMEM((COLS, LEN), BF16),
            pltpu.VMEM((LEN, LEN), F32),
            pltpu.VMEM((LEN, LEN), BF16),
        ],
    )
    vector, room = run(
        first_grad_kernel,
        where,
        [grad_mixed, low, sums_one, attended, tokens, sums_two, sums_up],
        [shape(*VECTOR, dtype=F32), shape(ROWS, QUADS, *CHUNK)],
    )
    cross_got = [swap(cross[1], "dp", 1)] if direct else []
    first_handed = run(
        first_hand_kernel,
        where,
        [room, vector] + third_passed,
        [shape(*FIRST_X), shape(*FIRST_Y)] + HANDED[2:],
        after=cross_got,
    )
    first_got = scatter_first(first_handed)

    def like(values):
        return [shape(*v.shape, dtype=F32) for v in values]

    def sums(dims, split):
        return [shape(*dims, dtype=F32), shape(*split)]

    if direct:
        plane = (ROWS,) + CROSS
        cross = run(cross_far_kernel, where, cross[:1] + cross_got, sums(plane, plane))
        cross_sum = [cross[0], swap(cross[1], "dp", 2)]
    else:
        cross_sum = []
    (part,) = run(
        token_back_kernel, where, [grad_mixed, wj], [shape(LEN, D)], after=first_handed[:1]
    )
    own = [shape(*CROSS, dtype=F32)] if direct else []
    pieces = run(
        token_sum_kernel,
        where,
        [result, grad_one, part, swap(part, "col", 1)] + cross_sum,
        blocks_out + own,
        [pltpu.VMEM((LEN, D), F32), pltpu.VMEM((ROWS, LEN, 2 * W), BF16)],
    )
    first_passed = run(
        carry_pass_kernel,
        where,
        first_handed[2:4] + first_handed[:1] + first_got,
        [PAIR, shape(*CARRIED)],
        after=pieces[:1],
    )
    first_last = scatter_second(first_passed)

    lines = [pltpu.VMEM((4,) + CHUNK, F32)]
    wide = [shape(4, *CHUNK, dtype=F32)]
    third_sum = run(
        near_line_kernel,
        where,
        third_handed[-1:] + third_got + first_got,
        sums((2,) + PART, (2,) + PART) if direct else [shape(4, *PART, dtype=F32)],
        [pltpu.VMEM((4,) + PART, F32)],
    )
    if direct:
        got = swap(third_sum[1], "dp", 1)
        third_sum = run(far_line_kernel, where, [third_sum[0], got], sums(PART, PART))
        third_sum[1] = swap(third_sum[1], "dp", 2)
        ready = third_sum[1:] + pieces[:1]
    else:
        ready = pieces[:1]
    second_got = scatter_first(second_handed)
    second_passed = scatter_pass(where, second_handed, second_got, ready)
    second_last = scatter_second(second_passed)
    first_sum = run(
        carry_near_kernel,
        where,
        first_handed[-1:] + first_got + first_last + first_passed[1:],
        sums((2 * W + VROWS, COLS), CARRIED) if direct else wide + [shape(*VECTOR, dtype=F32)],
        lines,
        after=second_passed,
    )
    second_sum = run(
        line_kernel,
        where,
        second_handed[-1:] + second_got + second_last,
        sums(CHUNK, CHUNK) + [shape(*CHUNK)] * 2 if direct else wide,
        lines,
    )
    if direct:
        got = swap(first_sum[1], "dp", 1)
        first_sum = run(
            carry_far_kernel,
            where,
            [first_sum[0], got],
            sums((W + VROWS, COLS), (W + 2 * VROWS, COLS)),
        )
        got = swap(first_sum[1], "dp", 2)
        state = joint + output
        new = run(
            first_adam_kernel,
            where,
            [first_sum[0], got] + state,
            like(state) + [shape(*VECTOR, dtype=F32)],
        )
        joint_new, output_new, vector = new[:3], new[3:6], new[6]

    flat_out = [shape(ROWS, 3 * PAIRS, 128, dtype=F32)] * 2
    got = exchange(pieces[:ROWS])
    out = run(token_out_kernel, where, got, flat_out)
    layer_out, tokens_grad = [v.reshape(tokens_in.shape) for v in out]

    def step_vectors(vector):
        state = [v.reshape(72, 128) for v in (vectors, vector_first, vector_second)]
        new = run(
            vector_adam_kernel,
            where,
            [vector, swap(vector, "col", 1)] + state,
            like(state),
            [pltpu.VMEM((72, 128), F32)],
            limit=48,
        )
        return [v.reshape(vectors.shape) for v in new]

    if direct:
        down_new = run(
            down_adam_kernel,
            where,
            third_sum + pieces[ROWS:] + got[1:] + down,
            like(down),
            limit=48,
        )
        vector_new = step_vectors(vector)
        got = [swap(v, "dp", mask) for v, mask in zip(second_sum[1:], ORDER[1:])]
        after = out[:1] + vector_new[:1] + down_new[:1]
        up_new = run(up_adam_kernel, where, second_sum[:1] + got + up, like(up), after=after)
        up_new = [v.reshape(up_weight.shape) for v in up_new]
    else:
        kept, sent = [v.reshape(2, ROWS, *CROSS) for v in cross]
        cross = jnp.stack([kept, sent], axis=1).reshape(QUADS, ROWS, *CROSS)
        cross = lax.psum_scatter(cross.astype(F32), "row", scatter_dimension=1)
        third = jnp.concatenate([third_sum[0], cross], axis=1)
        grads = wide_sums(first_sum[0], second_sum[0], third)
        joint_new = adamw(*joint, grads[0], JOINT_RATE, DECAY)
        output_new = adamw(*output, grads[1], OUTPUT_RATE, DECAY)
        up_new = adamw(*up, grads[2][:, None], JOINT_RATE, DECAY)
        down_new = adamw(*down, grads[3], DOWN_RATE, DECAY)
        vector_new = step_vectors(lax.psum(first_sum[1], "dp"))

    return (
        layer_out,
        tokens_grad,
        *[jnp.transpose(v, (2, 0, 1)) for v in joint_new],
        *[v.T[:, None] for v in output_new],
        *up_new,
        *[v.T[:, None] for v in down_new],
        *vector_new,
    )


def solution(mesh):
    first = P("row", "col", "dp")
    second = P("col", "row", "dp")
    tokens = P("dp", "row", None)
    weights = (first,) * 3 + (second,) * 3 + (first,) * 3 + (second,) * 3 + (P(),) * 3
    in_specs = (tokens, P(("dp", "row"))) + weights + (tokens,)
    out_specs = (tokens, tokens) + weights
    return jax.shard_map(
        per_device, mesh=mesh, in_specs=in_specs, out_specs=out_specs, check_vma=False
    )
```
